32 devices in a mesh: row: 8 (over y, x, core), col: 4 (over z).
Axes of the slice: x: 2, y: 2, z: 4, core: 2. Of those that a mesh axis runs over, the one named last changes fastest.
Arguments:
- top_inverse: float32 [2, 1024, 1024], P(None, 'row', 'col'), may hold values from -6 to 6
- panel: float32 [2, 512, 2048], P(None, 'row', 'col'), may hold values from -0.1875 to 0.1875
- leaf_rows: int32 [8, 2], P('col'), may hold values from 0 to 3, as said below
- leaf_counts: int32 [8], P('col'), may hold values from 1 to 2, as said below
- diag_inverse: float32 [2, 256, 2048], P(None, 'row', 'col'), may hold values from -6 to 6
Outputs:
- selected: float32 [2, 1024, 2048], P(None, 'row', 'col')
- diagonal: float32 [2, 256, 2048], P(None, 'row', 'col')
The draws below stay inside these ranges and needn't reach their ends.
Inputs may be any that keep to these rules, and one draw needn't show every extreme that they name: `leaf_rows`: the 2 entries of each leaf are distinct separator blocks. Slots 0 to leaf_counts - 1 of a leaf are live.
All inputs are finite; a program needn't handle non-finite values.
Results may differ from the reference program's by a relative error of at most 0.0003.
Values sent between devices are 32-bit elements; how exact they have to be, the bound alone decides.
No kernel may reach another device: no remote copies, remote signals or barrier semaphores. Data moves between devices by JAX's collectives and lax.ppermute only.
A program may use at most 128 MiB of HBM per device.

```python
import jax
import jax.numpy as jnp
from jax import lax

B = 256
NT = 4
P_SIZE = 2
NLEAF = 8


def draw_leaf_rows(key, part):
    leaf_keys = jax.random.split(key, NLEAF)
    shuffled = jax.vmap(lambda leaf_key: jax.random.permutation(leaf_key, NT))(leaf_keys)
    return shuffled[:, :P_SIZE].astype(jnp.int32)


def draw_leaf_counts(key, part):
    first_key, second_key, third_key = jax.random.split(jax.random.fold_in(key, 7), 3)
    live_counts = jax.random.randint(first_key, (NLEAF,), 1, P_SIZE + 1)
    full_leaf = jax.random.randint(second_key, (), 0, NLEAF)
    short_leaf = (full_leaf + 1 + jax.random.randint(third_key, (), 0, NLEAF - 1)) % NLEAF
    return live_counts.at[full_leaf].set(P_SIZE).at[short_leaf].set(1).astype(jnp.int32)


def level_of(own_key, extent, cuts, smallest, largest):
    loudness, own = 1.0, jax.random.fold_in(own_key, 6)
    for dim, shards_of in cuts:
        heights = jnp.exp(jax.random.uniform(jax.random.fold_in(own, dim), (shards_of,), jnp.float32, smallest / len(cuts), largest / len(cuts)))
        loudness = loudness * jnp.repeat(heights, extent[dim] // shards_of).reshape([-1 if axis == dim else 1 for axis in range(len(extent))])
    return loudness


def gaussian(own_key, shape, width, reach, cuts=(), held_as=jnp.bfloat16):
    entries = jax.random.normal(own_key, shape, jnp.float32) * width
    if len(cuts) > 0:
        entries = level_of(own_key, shape, cuts, -0.22, 0.18) * entries
    return jnp.clip(entries, min=-reach, max=reach).astype(held_as)


def setup_inputs(seed: int = 0) -> dict:
    seeds = jax.random.split(jax.random.key(seed), 6)
    return {
        "top_inverse": gaussian(seeds[0], (2, NT * B, NT * B), 1.0, 6.0, ((1, 8), (2, 4)), jnp.float32),
        "panel": gaussian(seeds[1], (2, P_SIZE * B, NLEAF * B), (2 * P_SIZE * B) ** -0.5, 0.1875, ((1, 8), (2, 4)), jnp.float32),
        "leaf_rows": draw_leaf_rows(jax.random.fold_in(seeds[5], 71), 0),
        "leaf_counts": draw_leaf_counts(jax.random.fold_in(seeds[5], 71), 0),
        "diag_inverse": gaussian(seeds[4], (2, B, NLEAF * B), 0.5, 6.0, ((1, 8), (2, 4)), jnp.float32),
    }


def complex_product(left_real, left_imag, right_real, right_imag):
    def product_highest(left, right):
        return jnp.dot(left, right, precision=lax.Precision.HIGHEST, preferred_element_type=jnp.float32)
    real_part = product_highest(left_real, right_real) - product_highest(left_imag, right_imag)
    imag_part = product_highest(left_real, right_imag) + product_highest(left_imag, right_real)
    return real_part, imag_part


def reference(top_inverse, panel, leaf_rows, leaf_counts, diag_inverse):
    inner = jnp.arange(B, dtype=jnp.int32)

    def one_leaf(member):
        rows_here = lax.dynamic_index_in_dim(leaf_rows, member, 0, keepdims=False)
        live_count = lax.dynamic_index_in_dim(leaf_counts, member, 0, keepdims=False)
        gather_index = (rows_here[:, None] * B + inner[None, :]).reshape(-1).astype(jnp.int32)
        active = ((jnp.arange(P_SIZE * B, dtype=jnp.int32) // B) < live_count).astype(jnp.float32)
        submatrix = jnp.take(jnp.take(top_inverse, gather_index, axis=1), gather_index, axis=2)
        lower = lax.dynamic_slice_in_dim(panel, member * B, B, 2) * active[None, :, None]
        real_part, imag_part = complex_product(submatrix[0], submatrix[1], lower[0], lower[1])
        sel_real = -real_part * active[:, None]
        sel_imag = -imag_part * active[:, None]
        diag_real, diag_imag = complex_product(sel_real.T, sel_imag.T, lower[0], lower[1])
        diag_block = lax.dynamic_slice_in_dim(diag_inverse, member * B, B, 2)
        return (jnp.stack([sel_real, sel_imag]), jnp.stack([diag_block[0] - diag_real, diag_block[1] - diag_imag]), gather_index)

    blocks, diagonal, indices = lax.map(one_leaf, jnp.arange(NLEAF, dtype=jnp.int32))
    dense = jnp.zeros((2, NT * B, NLEAF, B), jnp.float32)
    leaf_ids = jnp.arange(NLEAF, dtype=jnp.int32)[:, None]
    dense = dense.at[:, indices, leaf_ids, :].set(jnp.transpose(blocks, (1, 0, 2, 3)))
    selected = dense.reshape(2, NT * B, NLEAF * B)
    diagonal = jnp.transpose(diagonal, (1, 2, 0, 3)).reshape(2, B, NLEAF * B)
    return selected, diagonal
```

```python
import functools

import jax
import jax.numpy as jnp
from jax import lax
from jax.experimental import pallas as pl
from jax.experimental.pallas import tpu as pltpu
from jax.sharding import PartitionSpec as P

B = 256
F32 = jnp.float32
BF16 = jnp.bfloat16
VMEM_LIMIT = 48 * 1024 * 1024


def split(value):
    high = value.astype(BF16)
    low = (value - high.astype(F32)).astype(BF16)
    return high, low


def dot(left, right):
    return jnp.dot(left, right, preferred_element_type=F32)


def panel_kernel(n_row, share_rows, *refs):
    pieces, high_ref, low_ref = refs[:n_row], refs[n_row], refs[n_row + 1]
    me = lax.axis_index("row")
    for step in range(n_row):
        owner = me ^ step
        rows = pl.ds(pl.multiple_of(owner * share_rows, share_rows), share_rows)
        for part in range(2):
            high, low = split(pieces[step][part])
            high_ref[part, rows, :] = high
            low_ref[part, rows, :] = low


def select_kernel(n_row, n_col, *refs):
    rows_ref, counts_ref = refs[:2]
    blocks = refs[2 : 2 + n_col]
    high_ref, low_ref, out_ref, turned_ref, top = refs[2 + n_col :]
    leaves, slots = rows_ref.shape
    row_dev = out_ref.shape[1]
    share = B // n_row
    my_block = (lax.axis_index("row") * row_dev) // B
    my_col = lax.axis_index("col")
    for step in range(n_col):
        high, low = split(blocks[step][...].reshape(2 * row_dev, B))
        top[step, 0 : 2 * row_dev, :] = high
        top[step, 2 * row_dev : 4 * row_dev, :] = low
    for member in range(leaves):
        cols = slice(member * B, (member + 1) * B)
        count = counts_ref[member]
        live = lax.fori_loop(
            0, count, lambda q, seen: seen | (rows_ref[member, q] == my_block), False
        )

        @pl.when(live)
        def _():
            def slot(q, total):
                real, imag = total
                step = lax.rem(my_col - rows_ref[member, q] + n_col, n_col)
                rows = pl.ds(pl.multiple_of(q * B, B), B)
                left = top[step]
                both = left[0 : 2 * row_dev]
                with_real = dot(left, high_ref[0, rows, cols])
                with_imag = dot(left, high_ref[1, rows, cols])
                with_real = with_real[: 2 * row_dev] + with_real[2 * row_dev :]
                with_imag = with_imag[: 2 * row_dev] + with_imag[2 * row_dev :]
                with_real += dot(both, low_ref[0, rows, cols])
                with_imag += dot(both, low_ref[1, rows, cols])
                real = real - (with_real[:row_dev] - with_imag[row_dev:])
                imag = imag - (with_imag[:row_dev] + with_real[row_dev:])
                return real, imag

            zero = jnp.zeros((row_dev, B), F32)
            real, imag = lax.fori_loop(0, count, slot, (zero, zero))
            for part, value in enumerate((real, imag)):
                out_ref[part, :, cols] = value
                turned_ref[:, part, member] = value.T.reshape(n_row, share, row_dev)

        @pl.when(jnp.logical_not(live))
        def _():
            for part in range(2):
                out_ref[part, :, cols] = jnp.zeros((row_dev, B), F32)
                turned_ref[:, part, member] = jnp.zeros((n_row, share, row_dev), F32)


def diagonal_kernel(rows_ref, counts_ref, turned_ref, high_ref, low_ref, diag_ref, out_ref):
    leaves, slots = rows_ref.shape
    share, row_dev = turned_ref.shape[3:]
    holders = B // row_dev
    for member in range(leaves):
        cols = slice(member * B, (member + 1) * B)

        def slot(q, total):
            real, imag = total
            first = rows_ref[member, q] * holders
            rows = pl.ds(pl.multiple_of(q * B, B), B)
            left = jnp.concatenate(
                [turned_ref[first + h, :, member].reshape(2 * share, row_dev) for h in range(holders)],
                axis=1,
            )
            high, low = split(left)
            left = jnp.concatenate([high, low], axis=0)
            with_real = dot(left, high_ref[0, rows, cols])
            with_imag = dot(left, high_ref[1, rows, cols])
            with_real = with_real[: 2 * share] + with_real[2 * share :]
            with_imag = with_imag[: 2 * share] + with_imag[2 * share :]
            with_real += dot(high, low_ref[0, rows, cols])
            with_imag += dot(high, low_ref[1, rows, cols])
            real = real - (with_real[:share] - with_imag[share:])
            imag = imag - (with_imag[:share] + with_real[share:])
            return real, imag

        start = (diag_ref[0, :, cols], diag_ref[1, :, cols])
        real, imag = lax.fori_loop(0, counts_ref[member], slot, start)
        out_ref[0, :, cols] = real
        out_ref[1, :, cols] = imag


def on_device(n_row, n_col, top_inverse, panel, leaf_rows, leaf_counts, diag_inverse):
    smem = pl.BlockSpec(memory_space=pltpu.SMEM)
    vmem = pl.BlockSpec(memory_space=pltpu.VMEM)
    params = pltpu.CompilerParams(vmem_limit_bytes=VMEM_LIMIT)
    _, row_dev, width = top_inverse.shape
    _, panel_rows, columns = panel.shape
    leaves = columns // B
    share = B // n_row
    depth = n_row * panel_rows

    blocks = [top_inverse]
    for step in range(1, n_col):
        perm = [(i, (i + step) % n_col) for i in range(n_col)]
        blocks.append(lax.ppermute(top_inverse, "col", perm))

    pieces = [None] * n_row
    pieces[0] = panel
    for step in range(2, n_row, 2):
        pieces[step] = lax.ppermute(panel, "row", [(i, i ^ step) for i in range(n_row)])
    for step in range(0, n_row, 2):
        pieces[step + 1] = lax.ppermute(pieces[step], "row", [(i, i ^ 1) for i in range(n_row)])

    high, low = pl.pallas_call(
        functools.partial(panel_kernel, n_row, panel_rows),
        out_shape=[jax.ShapeDtypeStruct((2, depth, columns), BF16)] * 2,
        in_specs=[vmem] * n_row,
        out_specs=[vmem] * 2,
        compiler_params=params,
        cost_estimate=pl.CostEstimate(
            flops=0, bytes_accessed=16 * depth * columns, transcendentals=0
        ),
        name="split_panel",
    )(*pieces)

    selected, turned = pl.pallas_call(
        functools.partial(select_kernel, n_row, n_col),
        out_shape=[
            jax.ShapeDtypeStruct((2, row_dev, columns), F32),
            jax.ShapeDtypeStruct((n_row, 2, leaves, share, row_dev), F32),
        ],
        in_specs=[smem, smem] + [vmem] * (n_col + 2),
        out_specs=[vmem] * 2,
        scratch_shapes=[pltpu.VMEM((n_col, 4 * row_dev, B), BF16)],
        compiler_params=params,
        cost_estimate=pl.CostEstimate(
            flops=24 * row_dev * depth * columns,
            bytes_accessed=8 * (n_col * row_dev * B + (depth + 2 * row_dev) * columns),
            transcendentals=0,
        ),
        name="selected_rows",
    )(leaf_rows, leaf_counts, *blocks, high, low)

    turned = lax.all_to_all(turned, "row", 0, 0)

    diagonal = pl.pallas_call(
        diagonal_kernel,
        out_shape=jax.ShapeDtypeStruct(diag_inverse.shape, F32),
        in_specs=[smem, smem] + [vmem] * 4,
        out_specs=vmem,
        compiler_params=params,
        cost_estimate=pl.CostEstimate(
            flops=24 * share * depth * columns,
            bytes_accessed=8 * (depth + 2 * share) * columns,
            transcendentals=0,
        ),
        name="diagonal_rows",
    )(leaf_rows, leaf_counts, turned, high, low, diag_inverse)
    return selected, diagonal


def solution(mesh):
    return jax.shard_map(
        functools.partial(on_device, mesh.shape["row"], mesh.shape["col"]),
        mesh=mesh,
        in_specs=(
            P(None, "row", "col"),
            P(None, "row", "col"),
            P("col", None),
            P("col"),
            P(None, "row", "col"),
        ),
        out_specs=(P(None, "row", "col"), P(None, "row", "col")),
        check_vma=False,
    )
```

```python
import functools

import jax
import jax.numpy as jnp
from jax import lax
from jax.experimental import pallas as pl
from jax.experimental.pallas import tpu as pltpu
from jax.sharding import PartitionSpec as P

B = 256
F32 = jnp.float32
BF16 = jnp.bfloat16
VMEM_LIMIT = 48 * 1024 * 1024


def split(value):
    high = value.astype(BF16)
    low = (value - high.astype(F32)).astype(BF16)
    return high, low


def dot(left, right):
    return jnp.dot(left, right, preferred_element_type=F32)


def first_shared(n):
    return next(k for k in range(2, n + 2) if 2 * k >= n and (k == 2 or 2 * (k - 1) >= n))


def line_gather(own, axis, n):
    shared = first_shared(n)
    right = left = own
    far = []
    for k in range(2, n):
        if k == 2:
            rightward = [(i - 2, i) for i in range(2, n)]
            leftward = [(i + 2, i) for i in range(n - 2)]
        else:
            rightward = [(i - 1, i) for i in range(k, n)]
            leftward = [(i + 1, i) for i in range(n - k)]
        if k >= shared:
            if right is not left:
                right = jnp.where(2 * lax.axis_index(axis) >= n, right, left)
            right = left = lax.ppermute(right, axis, rightward + leftward)
            far += [right]
        else:
            right = lax.ppermute(right, axis, rightward)
            left = lax.ppermute(left, axis, leftward)
            far += [right, left]
    near = [lax.ppermute(own, axis, [(i, i ^ 1) for i in range(n) if i ^ 1 < n])]
    if n > 2:
        late, _ = lax.optimization_barrier((own, far[0]))
        odd = [(i, i + 1) for i in range(1, n - 1, 2)]
        far += [lax.ppermute(late, axis, odd + [(j, i) for i, j in odd])]
    return [own] + near + far


def line_place(me, owner, n):
    shared = first_shared(n)
    distance = jnp.abs(me - owner)
    near = jnp.where(owner == me ^ 1, 1, shared + n - 2)
    far = jnp.where(
        distance < shared, 2 * distance - 1 - (me > owner).astype(jnp.int32), shared + distance - 2
    )
    return jnp.where(distance == 0, 0, jnp.where(distance == 1, near, far))


def pack_kernel(*refs):
    pieces, out_ref = refs[:-1], refs[-1]
    share_rows = pieces[0].shape[1]
    for place, piece in enumerate(pieces):
        out_ref[:, place * share_rows : (place + 1) * share_rows, :] = piece[...]


def add_slot(total, left, high_ref, low_ref, rows, cols):
    real, imag = total
    size = real.shape[0]
    both = left[0 : 2 * size]
    with_real = dot(left, high_ref[0, rows, cols])
    with_imag = dot(left, high_ref[1, rows, cols])
    with_real = with_real[: 2 * size] + with_real[2 * size :]
    with_imag = with_imag[: 2 * size] + with_imag[2 * size :]
    with_real += dot(both, low_ref[0, rows, cols])
    with_imag += dot(both, low_ref[1, rows, cols])
    real = real - (with_real[:size] - with_imag[size:])
    imag = imag - (with_imag[:size] + with_real[size:])
    return real, imag


def row_is_live(rows_ref, counts_ref, member, block):
    return lax.fori_loop(
        0,
        counts_ref[member],
        lambda q, seen: seen | (rows_ref[member, q] == block),
        False,
    )


def early_kernel(n_row, n_col, n_blocks, share_rows, *refs):
    rows_ref, counts_ref = refs[:2]
    blocks = refs[2 : 2 + n_blocks]
    mine, mates, high_ref, low_ref, out_ref, top = refs[2 + n_blocks :]
    leaves = rows_ref.shape[0]
    row_dev = out_ref.shape[1]
    me = lax.axis_index("row")
    my_block = (me * row_dev) // B
    my_col = lax.axis_index("col")
    for packed, first in ((mine, me), (mates, me ^ 1)):
        for step in range(0, n_row, 2):
            owner = first ^ step
            rows = pl.ds(pl.multiple_of(owner * share_rows, share_rows), share_rows)
            place = slice(step // 2 * share_rows, (step // 2 + 1) * share_rows)
            for part in range(2):
                high, low = split(packed[part, place, :])
                high_ref[part, rows, :] = high
                low_ref[part, rows, :] = low
    for place in range(n_blocks):
        high, low = split(blocks[place][...].reshape(2 * row_dev, B))
        top[place, 0 : 2 * row_dev, :] = high
        top[place, 2 * row_dev : 4 * row_dev, :] = low
    for member in range(leaves):
        cols = slice(member * B, (member + 1) * B)
        live = row_is_live(rows_ref, counts_ref, member, my_block)
        for part in range(2):
            out_ref[part, :, cols] = jnp.zeros((row_dev, B), F32)

        def slot(q, carry):
            place = line_place(my_col, rows_ref[member, q], n_col)

            @pl.when(place < n_blocks)
            def _():
                rows = pl.ds(pl.multiple_of(q * B, B), B)
                total = out_ref[0, :, cols], out_ref[1, :, cols]
                total = add_slot(total, top[place], high_ref, low_ref, rows, cols)
                out_ref[0, :, cols], out_ref[1, :, cols] = total

            return carry

        lax.fori_loop(0, jnp.where(live, counts_ref[member], 0), slot, 0)


def select_kernel(n_row, n_col, n_early, n_late, *refs):
    rows_ref, counts_ref = refs[:2]
    blocks = refs[2 : 2 + n_late]
    early_ref, high_ref, low_ref, out_ref = refs[2 + n_late : 6 + n_late]
    sent = refs[6 + n_late : 6 + n_late + n_row]
    top, turned = refs[6 + n_late + n_row :]
    leaves = rows_ref.shape[0]
    row_dev = out_ref.shape[1]
    share = B // n_row
    me = lax.axis_index("row")
    my_block = (me * row_dev) // B
    my_col = lax.axis_index("col")
    for place in range(n_late):
        high, low = split(blocks[place][...].reshape(2 * row_dev, B))
        top[place, 0 : 2 * row_dev, :] = high
        top[place, 2 * row_dev : 4 * row_dev, :] = low
    for member in range(leaves):
        cols = slice(member * B, (member + 1) * B)
        live = row_is_live(rows_ref, counts_ref, member, my_block)
        for part in range(2):
            out_ref[part, :, cols] = early_ref[part, :, cols]

        def slot(q, carry):
            place = line_place(my_col, rows_ref[member, q], n_col)

            @pl.when(place >= n_early)
            def _():
                rows = pl.ds(pl.multiple_of(q * B, B), B)
                total = out_ref[0, :, cols], out_ref[1, :, cols]
                total = add_slot(total, top[place - n_early], high_ref, low_ref, rows, cols)
                out_ref[0, :, cols], out_ref[1, :, cols] = total

            return carry

        lax.fori_loop(0, jnp.where(live, counts_ref[member], 0), slot, 0)
        for part in range(2):
            turned[:, member, part] = out_ref[part, :, cols].T.reshape(n_row, share, row_dev)

    for step in range(n_row):
        sent[step][...] = turned[me ^ step]


def diagonal_kernel(n_row, *refs):
    rows_ref, counts_ref = refs[:2]
    pieces = refs[2 : 2 + n_row]
    high_ref, low_ref, diag_ref, out_ref, turned = refs[2 + n_row :]
    leaves, _, share, row_dev = pieces[0].shape
    holders = B // row_dev
    me = lax.axis_index("row")
    for step in range(n_row):
        high, low = split(pieces[step][...].reshape(leaves, 2 * share, row_dev))
        turned[me ^ step, :, 0 : 2 * share] = high
        turned[me ^ step, :, 2 * share : 4 * share] = low
    for member in range(leaves):
        cols = slice(member * B, (member + 1) * B)

        def slot(q, total):
            first = rows_ref[member, q] * holders
            rows = pl.ds(pl.multiple_of(q * B, B), B)
            left = jnp.concatenate([turned[first + h, member] for h in range(holders)], axis=1)
            return add_slot(total, left, high_ref, low_ref, rows, cols)

        start = (diag_ref[0, :, cols], diag_ref[1, :, cols])
        real, imag = lax.fori_loop(0, counts_ref[member], slot, start)
        out_ref[0, :, cols] = real
        out_ref[1, :, cols] = imag


def on_device(n_row, n_col, top_inverse, panel, leaf_rows, leaf_counts, diag_inverse):
    smem = pl.BlockSpec(memory_space=pltpu.SMEM)
    vmem = pl.BlockSpec(memory_space=pltpu.VMEM)
    params = pltpu.CompilerParams(vmem_limit_bytes=VMEM_LIMIT)
    _, row_dev, _ = top_inverse.shape
    _, panel_rows, columns = panel.shape
    leaves = columns // B
    share = B // n_row
    depth = n_row * panel_rows

    blocks = line_gather(top_inverse, "col", n_col)

    like = [panel]
    for step in range(2, n_row, 2):
        like.append(lax.ppermute(panel, "row", [(i, i ^ step) for i in range(n_row)]))
    early_blocks, late_blocks = blocks[:-2], blocks[-2:]
    like, early_blocks = lax.optimization_barrier((like, early_blocks))
    mine = pl.pallas_call(
        pack_kernel,
        out_shape=jax.ShapeDtypeStruct((2, depth // 2, columns), F32),
        in_specs=[vmem] * len(like),
        out_specs=vmem,
        compiler_params=params,
        cost_estimate=pl.CostEstimate(
            flops=0, bytes_accessed=8 * depth * columns, transcendentals=0
        ),
        name="pack_panel",
    )(*like)
    mates = lax.ppermute(mine, "row", [(i, i ^ 1) for i in range(n_row)])

    high, low, early = pl.pallas_call(
        functools.partial(early_kernel, n_row, n_col, len(early_blocks), panel_rows),
        out_shape=[jax.ShapeDtypeStruct((2, depth, columns), BF16)] * 2
        + [jax.ShapeDtypeStruct((2, row_dev, columns), F32)],
        in_specs=[smem, smem] + [vmem] * (len(early_blocks) + 2),
        out_specs=[vmem] * 3,
        scratch_shapes=[pltpu.VMEM((len(early_blocks), 4 * row_dev, B), BF16)],
        compiler_params=params,
        cost_estimate=pl.CostEstimate(
            flops=24 * row_dev * depth * columns,
            bytes_accessed=8 * (n_col * row_dev * B + (2 * depth + row_dev) * columns),
            transcendentals=0,
        ),
        name="early_rows",
    )(leaf_rows, leaf_counts, *early_blocks, mine, mates)

    piece = (leaves, 2, share, row_dev)
    selected, *sent = pl.pallas_call(
        functools.partial(select_kernel, n_row, n_col, len(early_blocks), len(late_blocks)),
        out_shape=[jax.ShapeDtypeStruct((2, row_dev, columns), F32)]
        + [jax.ShapeDtypeStruct(piece, F32)] * n_row,
        in_specs=[smem, smem] + [vmem] * (len(late_blocks) + 3),
        out_specs=[vmem] * (1 + n_row),
        scratch_shapes=[
            pltpu.VMEM((len(late_blocks), 4 * row_dev, B), BF16),
            pltpu.VMEM((n_row,) + piece, F32),
        ],
        compiler_params=params,
        cost_estimate=pl.CostEstimate(
            flops=24 * row_dev * B * columns,
            bytes_accessed=8 * (row_dev * B + (depth + 3 * row_dev) * columns),
            transcendentals=0,
        ),
        name="selected_rows",
    )(leaf_rows, leaf_counts, *late_blocks, early, high, low)

    for step in sorted(range(1, n_row), key=lambda step: -step if step > 1 else 0):
        sent[step] = lax.ppermute(sent[step], "row", [(i, i ^ step) for i in range(n_row)])

    diagonal = pl.pallas_call(
        functools.partial(diagonal_kernel, n_row),
        out_shape=jax.ShapeDtypeStruct(diag_inverse.shape, F32),
        in_specs=[smem, smem] + [vmem] * (n_row + 3),
        out_specs=vmem,
        scratch_shapes=[pltpu.VMEM((n_row, leaves, 4 * share, row_dev), BF16)],
        compiler_params=params,
        cost_estimate=pl.CostEstimate(
            flops=24 * share * depth * columns,
            bytes_accessed=8 * (depth + 2 * share) * columns,
            transcendentals=0,
        ),
        name="diagonal_rows",
    )(leaf_rows, leaf_counts, *sent, high, low, diag_inverse)
    return selected, diagonal


def solution(mesh):
    return jax.shard_map(
        functools.partial(on_device, mesh.shape["row"], mesh.shape["col"]),
        mesh=mesh,
        in_specs=(
            P(None, "row", "col"),
            P(None, "row", "col"),
            P("col", None),
            P("col"),
            P(None, "row", "col"),
        ),
        out_specs=(P(None, "row", "col"), P(None, "row", "col")),
        check_vma=False,
    )
```

```python
import functools

import jax
import jax.numpy as jnp
from jax import lax
from jax.experimental import pallas as pl
from jax.experimental.pallas import tpu as pltpu
from jax.sharding import PartitionSpec as P

B = 256
F32 = jnp.float32
BF16 = jnp.bfloat16
VMEM_LIMIT = 48 * 1024 * 1024


def split(value):
    high = value.astype(BF16)
    low = (value - high.astype(F32)).astype(BF16)
    return high, low


def dot(left, right):
    return jnp.dot(left, right, preferred_element_type=F32)


def first_shared(n):
    return next(k for k in range(2, n + 2) if 2 * k >= n and (k == 2 or 2 * (k - 1) >= n))


def line_gather(own, axis, n):
    shared = first_shared(n)
    right = left = own
    far = []
    for k in range(2, n):
        if k == 2:
            rightward = [(i - 2, i) for i in range(2, n)]
            leftward = [(i + 2, i) for i in range(n - 2)]
        else:
            rightward = [(i - 1, i) for i in range(k, n)]
            leftward = [(i + 1, i) for i in range(n - k)]
        if k >= shared:
            if right is not left:
                right = jnp.where(2 * lax.axis_index(axis) >= n, right, left)
            right = left = lax.ppermute(right, axis, rightward + leftward)
            far += [right]
        else:
            right = lax.ppermute(right, axis, rightward)
            left = lax.ppermute(left, axis, leftward)
            far += [right, left]
    near = [lax.ppermute(own, axis, [(i, i ^ 1) for i in range(n) if i ^ 1 < n])]
    if n > 2:
        late, _ = lax.optimization_barrier((own, [far[0], near[0]]))
        odd = [(i, i + 1) for i in range(1, n - 1, 2)]
        far += [lax.ppermute(late, axis, odd + [(j, i) for i, j in odd])]
    return [own] + near + far


def line_place(me, owner, n):
    shared = first_shared(n)
    distance = jnp.abs(me - owner)
    near = jnp.where(owner == me ^ 1, 1, shared + n - 2)
    far = jnp.where(
        distance < shared, 2 * distance - 1 - (me > owner).astype(jnp.int32), shared + distance - 2
    )
    return jnp.where(distance == 0, 0, jnp.where(distance == 1, near, far))


def pack_kernel(*refs):
    pieces, out_ref = refs[:-1], refs[-1]
    share_rows = pieces[0].shape[1]
    for place, piece in enumerate(pieces):
        out_ref[:, place * share_rows : (place + 1) * share_rows, :] = piece[...]


def add_slot(total, left, high_ref, low_ref, rows, cols):
    real, imag = total
    size = real.shape[0]
    both = left[0 : 2 * size]
    with_real = dot(left, high_ref[0, rows, cols])
    with_imag = dot(left, high_ref[1, rows, cols])
    with_real = with_real[: 2 * size] + with_real[2 * size :]
    with_imag = with_imag[: 2 * size] + with_imag[2 * size :]
    with_real += dot(both, low_ref[0, rows, cols])
    with_imag += dot(both, low_ref[1, rows, cols])
    real = real - (with_real[:size] - with_imag[size:])
    imag = imag - (with_imag[:size] + with_real[size:])
    return real, imag


def row_is_live(rows_ref, counts_ref, member, block):
    return lax.fori_loop(
        0,
        counts_ref[member],
        lambda q, seen: seen | (rows_ref[member, q] == block),
        False,
    )


def blocks_kernel(*refs):
    blocks, out_ref = refs[:-1], refs[-1]
    for place, block in enumerate(blocks):
        both = 2 * block.shape[1]
        high, low = split(block[...].reshape(both, B))
        out_ref[place, 0:both, :] = high
        out_ref[place, both : 2 * both, :] = low


def select_kernel(n_row, n_col, share_rows, *refs):
    rows_ref, counts_ref, top, mine, mates, high_ref, low_ref, out_ref = refs[:8]
    sent, turned = refs[8:-1], refs[-1]
    leaves = rows_ref.shape[0]
    row_dev = out_ref.shape[1]
    chips, share = turned.shape[0], turned.shape[3]
    me = lax.axis_index("row")
    my_block = (me * row_dev) // B
    my_col = lax.axis_index("col")
    for packed, first in ((mine, me), (mates, me ^ 1)):
        for step in range(0, n_row, 2):
            owner = first ^ step
            rows = pl.ds(pl.multiple_of(owner * share_rows, share_rows), share_rows)
            place = slice(step // 2 * share_rows, (step // 2 + 1) * share_rows)
            for part in range(2):
                high, low = split(packed[part, place, :])
                high_ref[part, rows, :] = high
                low_ref[part, rows, :] = low
    for member in range(leaves):
        cols = slice(member * B, (member + 1) * B)
        live = row_is_live(rows_ref, counts_ref, member, my_block)

        @pl.when(live)
        def _():
            def slot(q, total):
                place = line_place(my_col, rows_ref[member, q], n_col)
                rows = pl.ds(pl.multiple_of(q * B, B), B)
                return add_slot(total, top[place], high_ref, low_ref, rows, cols)

            zero = jnp.zeros((row_dev, B), F32)
            total = lax.fori_loop(0, counts_ref[member], slot, (zero, zero))
            for part, value in enumerate(total):
                out_ref[part, :, cols] = value
                turned[:, member, part] = value.T.reshape(chips, share, row_dev)

        @pl.when(jnp.logical_not(live))
        def _():
            for part in range(2):
                out_ref[part, :, cols] = jnp.zeros((row_dev, B), F32)
                turned[:, member, part] = jnp.zeros((chips, share, row_dev), F32)

    for step in range(chips):
        sent[step][...] = turned[(me // 2) ^ step]


def diagonal_kernel(rows_ref, *refs):
    pieces, (high_ref, low_ref, diag_ref, keep_ref, give_ref, turned, whole) = refs[:-7], refs[-7:]
    leaves, slots = rows_ref.shape
    _, _, chip_share, row_dev = pieces[0].shape
    share = keep_ref.shape[1]
    me = lax.axis_index("row")
    core = me % 2
    for step, piece in enumerate(pieces):
        source = (me // 2) ^ step
        high, low = split(piece[...].reshape(leaves, 2 * chip_share, row_dev))
        turned[source, :, 0 : 2 * chip_share] = high
        turned[source, :, 2 * chip_share : 4 * chip_share] = low
    for member in range(leaves):
        cols = slice(member * B, (member + 1) * B)
        left = jnp.concatenate([turned[rows_ref[member, q], member] for q in range(slots)], axis=1)
        both = left[: 2 * chip_share]

        def panel(ref, part):
            starts = [pl.multiple_of(q * B + core * row_dev, row_dev) for q in range(slots)]
            return jnp.concatenate(
                [ref[part, pl.ds(start, row_dev), cols] for start in starts], axis=0
            )

        with_real = dot(left, panel(high_ref, 0))
        with_imag = dot(left, panel(high_ref, 1))
        with_real = with_real[: 2 * chip_share] + with_real[2 * chip_share :]
        with_imag = with_imag[: 2 * chip_share] + with_imag[2 * chip_share :]
        with_real += dot(both, panel(low_ref, 0))
        with_imag += dot(both, panel(low_ref, 1))
        whole[0, :, cols] = with_real[:chip_share] - with_imag[chip_share:]
        whole[1, :, cols] = with_imag[:chip_share] + with_real[chip_share:]
    mine = pl.ds(pl.multiple_of(core * share, share), share)
    other = pl.ds(pl.multiple_of((1 - core) * share, share), share)
    keep_ref[...] = diag_ref[...] - whole[:, mine, :]
    give_ref[...] = whole[:, other, :]


def subtract_kernel(left_ref, right_ref, out_ref):
    out_ref[...] = left_ref[...] - right_ref[...]


def on_device(n_row, n_col, top_inverse, panel, leaf_rows, leaf_counts, diag_inverse):
    smem = pl.BlockSpec(memory_space=pltpu.SMEM)
    vmem = pl.BlockSpec(memory_space=pltpu.VMEM)
    params = pltpu.CompilerParams(vmem_limit_bytes=VMEM_LIMIT)
    _, row_dev, _ = top_inverse.shape
    _, panel_rows, columns = panel.shape
    leaves = columns // B
    chips = n_row // 2
    chip_share = B // chips
    depth = n_row * panel_rows

    blocks = line_gather(top_inverse, "col", n_col)

    like = [panel]
    for step in range(2, n_row, 2):
        like.append(lax.ppermute(panel, "row", [(i, i ^ step) for i in range(n_row)]))
    like, _ = lax.optimization_barrier((like, blocks[:-2]))
    mine = pl.pallas_call(
        pack_kernel,
        out_shape=jax.ShapeDtypeStruct((2, depth // 2, columns), F32),
        in_specs=[vmem] * len(like),
        out_specs=vmem,
        compiler_params=params,
        cost_estimate=pl.CostEstimate(
            flops=0, bytes_accessed=8 * depth * columns, transcendentals=0
        ),
        name="pack_panel",
    )(*like)
    mates = lax.ppermute(mine, "row", [(i, i ^ 1) for i in range(n_row)])

    top = pl.pallas_call(
        blocks_kernel,
        out_shape=jax.ShapeDtypeStruct((len(blocks), 4 * row_dev, B), BF16),
        in_specs=[vmem] * len(blocks),
        out_specs=vmem,
        compiler_params=params,
        cost_estimate=pl.CostEstimate(
            flops=10**11, bytes_accessed=10**9, transcendentals=0
        ),
        name="split_blocks",
    )(*blocks)

    piece = jax.ShapeDtypeStruct((leaves, 2, chip_share, row_dev), F32)
    high, low, selected, *sent = pl.pallas_call(
        functools.partial(select_kernel, n_row, n_col, panel_rows),
        out_shape=[jax.ShapeDtypeStruct((2, depth, columns), BF16)] * 2
        + [jax.ShapeDtypeStruct((2, row_dev, columns), F32)]
        + [piece] * chips,
        in_specs=[smem, smem] + [vmem] * 3,
        out_specs=[vmem] * (3 + chips),
        scratch_shapes=[pltpu.VMEM((chips,) + piece.shape, F32)],
        compiler_params=params,
        cost_estimate=pl.CostEstimate(
            flops=24 * row_dev * depth * columns,
            bytes_accessed=8 * (n_col * row_dev * B + (2 * depth + 2 * row_dev) * columns),
            transcendentals=0,
        ),
        name="selected_rows",
    )(leaf_rows, leaf_counts, top, mine, mates)

    for step in range(chips - 1, 0, -1):
        perm = [(i, i ^ (2 * step)) for i in range(n_row)]
        sent[step] = lax.ppermute(sent[step], "row", perm)

    keep, give = pl.pallas_call(
        diagonal_kernel,
        out_shape=[jax.ShapeDtypeStruct(diag_inverse.shape, F32)] * 2,
        in_specs=[smem] + [vmem] * (chips + 3),
        out_specs=[vmem] * 2,
        scratch_shapes=[
            pltpu.VMEM((chips, leaves, 4 * chip_share, row_dev), BF16),
            pltpu.VMEM((2, chip_share, columns), F32),
        ],
        compiler_params=params,
        cost_estimate=pl.CostEstimate(
            flops=12 * chip_share * depth * columns,
            bytes_accessed=8 * (depth + 2 * chip_share) * columns,
            transcendentals=0,
        ),
        name="diagonal_part",
    )(leaf_rows, *sent, high, low, diag_inverse)
    give = lax.ppermute(give, "row", [(i, i ^ 1) for i in range(n_row)])
    diagonal = pl.pallas_call(
        subtract_kernel,
        out_shape=jax.ShapeDtypeStruct(diag_inverse.shape, F32),
        in_specs=[vmem] * 2,
        out_specs=vmem,
        compiler_params=params,
        name="diagonal_rows",
    )(keep, give)
    return selected, diagonal


def solution(mesh):
    return jax.shard_map(
        functools.partial(on_device, mesh.shape["row"], mesh.shape["col"]),
        mesh=mesh,
        in_specs=(
            P(None, "row", "col"),
            P(None, "row", "col"),
            P("col", None),
            P("col"),
            P(None, "row", "col"),
        ),
        out_specs=(P(None, "row", "col"), P(None, "row", "col")),
        check_vma=False,
    )
```

```python
import functools

import jax
import jax.numpy as jnp
from jax import lax
from jax.experimental import pallas as pl
from jax.experimental.pallas import tpu as pltpu
from jax.sharding import PartitionSpec as P

B = 256
F32 = jnp.float32
BF16 = jnp.bfloat16
VMEM_LIMIT = 48 * 1024 * 1024


def split(value):
    high = value.astype(BF16)
    low = (value - high.astype(F32)).astype(BF16)
    return high, low


def dot(left, right):
    return jnp.dot(left, right, preferred_element_type=F32)


def line_gather(own, axis, n):
    pieces = [own]
    for step in line_steps(n):
        perm = [(i, i ^ step) for i in range(n)]
        pieces += [lax.ppermute(piece, axis, perm) for piece in pieces]
    return pieces


def line_steps(n):
    steps = []
    while n > 1:
        n //= 2
        steps.append(n)
    return steps


def line_order(n):
    order = [0]
    for step in line_steps(n):
        order += [k ^ step for k in order]
    return order


def pack_kernel(*refs):
    pieces, out_ref = refs[:-1], refs[-1]
    share_rows = pieces[0].shape[1]
    for place, piece in enumerate(pieces):
        out_ref[:, place * share_rows : (place + 1) * share_rows, :] = piece[...]


def add_slot(total, left, high_ref, low_ref, rows, cols):
    real, imag = total
    size = real.shape[0]
    both = left[0 : 2 * size]
    with_real = dot(left, high_ref[0, rows, cols])
    with_imag = dot(left, high_ref[1, rows, cols])
    with_real = with_real[: 2 * size] + with_real[2 * size :]
    with_imag = with_imag[: 2 * size] + with_imag[2 * size :]
    with_real += dot(both, low_ref[0, rows, cols])
    with_imag += dot(both, low_ref[1, rows, cols])
    real = real - (with_real[:size] - with_imag[size:])
    imag = imag - (with_imag[:size] + with_real[size:])
    return real, imag


def row_is_live(rows_ref, counts_ref, member, block):
    return lax.fori_loop(
        0,
        counts_ref[member],
        lambda q, seen: seen | (rows_ref[member, q] == block),
        False,
    )


def blocks_kernel(*refs):
    blocks, out_ref = refs[:-1], refs[-1]
    for place, block in zip(line_order(len(blocks)), blocks):
        both = 2 * block.shape[1]
        high, low = split(block[...].reshape(both, B))
        out_ref[place, 0:both, :] = high
        out_ref[place, both : 2 * both, :] = low


def select_kernel(n_row, share_rows, *refs):
    rows_ref, counts_ref, top, mine, mates, high_ref, low_ref, out_ref = refs[:8]
    sent, turned = refs[8:-1], refs[-1]
    leaves = rows_ref.shape[0]
    row_dev = out_ref.shape[1]
    chips, share = turned.shape[0], turned.shape[3]
    me = lax.axis_index("row")
    my_block = (me * row_dev) // B
    my_col = lax.axis_index("col")
    for packed, first in ((mine, me), (mates, me ^ 1)):
        for step in range(0, n_row, 2):
            owner = first ^ step
            rows = pl.ds(pl.multiple_of(owner * share_rows, share_rows), share_rows)
            place = slice(step // 2 * share_rows, (step // 2 + 1) * share_rows)
            for part in range(2):
                high, low = split(packed[part, place, :])
                high_ref[part, rows, :] = high
                low_ref[part, rows, :] = low
    for member in range(leaves):
        cols = slice(member * B, (member + 1) * B)
        live = row_is_live(rows_ref, counts_ref, member, my_block)

        @pl.when(live)
        def _():
            def slot(q, total):
                place = my_col ^ rows_ref[member, q]
                rows = pl.ds(pl.multiple_of(q * B, B), B)
                return add_slot(total, top[place], high_ref, low_ref, rows, cols)

            zero = jnp.zeros((row_dev, B), F32)
            total = lax.fori_loop(0, counts_ref[member], slot, (zero, zero))
            for part, value in enumerate(total):
                out_ref[part, :, cols] = value
                turned[:, member, part] = value.T.reshape(chips, share, row_dev)

        @pl.when(jnp.logical_not(live))
        def _():
            for part in range(2):
                out_ref[part, :, cols] = jnp.zeros((row_dev, B), F32)
                turned[:, member, part] = jnp.zeros((chips, share, row_dev), F32)

    for step in range(chips):
        sent[step][...] = turned[(me // 2) ^ step]


def diagonal_kernel(rows_ref, *refs):
    pieces, (high_ref, low_ref, diag_ref, keep_ref, give_ref, turned, whole) = refs[:-7], refs[-7:]
    leaves, slots = rows_ref.shape
    _, _, chip_share, row_dev = pieces[0].shape
    share = keep_ref.shape[1]
    me = lax.axis_index("row")
    core = me % 2
    for step, piece in enumerate(pieces):
        source = (me // 2) ^ step
        high, low = split(piece[...].reshape(leaves, 2 * chip_share, row_dev))
        turned[source, :, 0 : 2 * chip_share] = high
        turned[source, :, 2 * chip_share : 4 * chip_share] = low
    for member in range(leaves):
        cols = slice(member * B, (member + 1) * B)
        left = jnp.concatenate([turned[rows_ref[member, q], member] for q in range(slots)], axis=1)
        both = left[: 2 * chip_share]

        def panel(ref, part):
            starts = [pl.multiple_of(q * B + core * row_dev, row_dev) for q in range(slots)]
            return jnp.concatenate(
                [ref[part, pl.ds(start, row_dev), cols] for start in starts], axis=0
            )

        with_real = dot(left, panel(high_ref, 0))
        with_imag = dot(left, panel(high_ref, 1))
        with_real = with_real[: 2 * chip_share] + with_real[2 * chip_share :]
        with_imag = with_imag[: 2 * chip_share] + with_imag[2 * chip_share :]
        with_real += dot(both, panel(low_ref, 0))
        with_imag += dot(both, panel(low_ref, 1))
        whole[0, :, cols] = with_real[:chip_share] - with_imag[chip_share:]
        whole[1, :, cols] = with_imag[:chip_share] + with_real[chip_share:]
    mine = pl.ds(pl.multiple_of(core * share, share), share)
    other = pl.ds(pl.multiple_of((1 - core) * share, share), share)
    keep_ref[...] = diag_ref[...] - whole[:, mine, :]
    give_ref[...] = whole[:, other, :]


def subtract_kernel(left_ref, right_ref, out_ref):
    out_ref[...] = left_ref[...] - right_ref[...]


def on_device(n_row, n_col, top_inverse, panel, leaf_rows, leaf_counts, diag_inverse):
    smem = pl.BlockSpec(memory_space=pltpu.SMEM)
    vmem = pl.BlockSpec(memory_space=pltpu.VMEM)
    params = pltpu.CompilerParams(vmem_limit_bytes=VMEM_LIMIT)
    _, row_dev, _ = top_inverse.shape
    _, panel_rows, columns = panel.shape
    leaves = columns // B
    chips = n_row // 2
    chip_share = B // chips
    depth = n_row * panel_rows

    blocks = line_gather(top_inverse, "col", n_col)

    like = [panel]
    for step in range(2, n_row, 2):
        like.append(lax.ppermute(panel, "row", [(i, i ^ step) for i in range(n_row)]))
    like, _ = lax.optimization_barrier((like, blocks[: n_col // 2 + 1]))
    mine = pl.pallas_call(
        pack_kernel,
        out_shape=jax.ShapeDtypeStruct((2, depth // 2, columns), F32),
        in_specs=[vmem] * len(like),
        out_specs=vmem,
        compiler_params=params,
        cost_estimate=pl.CostEstimate(
            flops=0, bytes_accessed=8 * depth * columns, transcendentals=0
        ),
        name="pack_panel",
    )(*like)
    mates = lax.ppermute(mine, "row", [(i, i ^ 1) for i in range(n_row)])

    top = pl.pallas_call(
        blocks_kernel,
        out_shape=jax.ShapeDtypeStruct((len(blocks), 4 * row_dev, B), BF16),
        in_specs=[vmem] * len(blocks),
        out_specs=vmem,
        compiler_params=params,
        cost_estimate=pl.CostEstimate(
            flops=10**11, bytes_accessed=10**9, transcendentals=0
        ),
        name="split_blocks",
    )(*blocks)

    piece = jax.ShapeDtypeStruct((leaves, 2, chip_share, row_dev), F32)
    high, low, selected, *sent = pl.pallas_call(
        functools.partial(select_kernel, n_row, panel_rows),
        out_shape=[jax.ShapeDtypeStruct((2, depth, columns), BF16)] * 2
        + [jax.ShapeDtypeStruct((2, row_dev, columns), F32)]
        + [piece] * chips,
        in_specs=[smem, smem] + [vmem] * 3,
        out_specs=[vmem] * (3 + chips),
        scratch_shapes=[pltpu.VMEM((chips,) + piece.shape, F32)],
        compiler_params=params,
        cost_estimate=pl.CostEstimate(
            flops=24 * row_dev * depth * columns,
            bytes_accessed=8 * (n_col * row_dev * B + (2 * depth + 2 * row_dev) * columns),
            transcendentals=0,
        ),
        name="selected_rows",
    )(leaf_rows, leaf_counts, top, mine, mates)

    for step in range(chips - 1, 0, -1):
        perm = [(i, i ^ (2 * step)) for i in range(n_row)]
        sent[step] = lax.ppermute(sent[step], "row", perm)

    keep, give = pl.pallas_call(
        diagonal_kernel,
        out_shape=[jax.ShapeDtypeStruct(diag_inverse.shape, F32)] * 2,
        in_specs=[smem] + [vmem] * (chips + 3),
        out_specs=[vmem] * 2,
        scratch_shapes=[
            pltpu.VMEM((chips, leaves, 4 * chip_share, row_dev), BF16),
            pltpu.VMEM((2, chip_share, columns), F32),
        ],
        compiler_params=params,
        cost_estimate=pl.CostEstimate(
            flops=12 * chip_share * depth * columns,
            bytes_accessed=8 * (depth + 2 * chip_share) * columns,
            transcendentals=0,
        ),
        name="diagonal_part",
    )(leaf_rows, *sent, high, low, diag_inverse)
    give = lax.ppermute(give, "row", [(i, i ^ 1) for i in range(n_row)])
    diagonal = pl.pallas_call(
        subtract_kernel,
        out_shape=jax.ShapeDtypeStruct(diag_inverse.shape, F32),
        in_specs=[vmem] * 2,
        out_specs=vmem,
        compiler_params=params,
        name="diagonal_rows",
    )(keep, give)
    return selected, diagonal


def solution(mesh):
    return jax.shard_map(
        functools.partial(on_device, mesh.shape["row"], mesh.shape["col"]),
        mesh=mesh,
        in_specs=(
            P(None, "row", "col"),
            P(None, "row", "col"),
            P("col", None),
            P("col"),
            P(None, "row", "col"),
        ),
        out_specs=(P(None, "row", "col"), P(None, "row", "col")),
        check_vma=False,
    )
```

```python
import functools

import jax
import jax.numpy as jnp
from jax import lax
from jax.experimental import pallas as pl
from jax.experimental.pallas import tpu as pltpu
from jax.sharding import PartitionSpec as P

B = 256
F32 = jnp.float32
BF16 = jnp.bfloat16
VMEM_LIMIT = 48 * 1024 * 1024


def split(value):
    high = value.astype(BF16)
    low = (value - high.astype(F32)).astype(BF16)
    return high, low


def dot(left, right):
    return jnp.dot(left, right, preferred_element_type=F32)


def line_gather(own, axis, n):
    pieces = [own]
    for step in line_steps(n):
        perm = [(i, i ^ step) for i in range(n)]
        pieces += [lax.ppermute(piece, axis, perm) for piece in pieces]
    return pieces


def line_steps(n):
    steps = []
    while n > 1:
        n //= 2
        steps.append(n)
    return steps


def line_order(n):
    order = [0]
    for step in line_steps(n):
        order += [k ^ step for k in order]
    return order


def pack_kernel(*refs):
    pieces, out_ref = refs[:-1], refs[-1]
    share_rows = pieces[0].shape[1]
    for place, piece in enumerate(pieces):
        out_ref[:, place * share_rows : (place + 1) * share_rows, :] = piece[...]


def add_slot(total, left, high_ref, low_ref, rows, cols):
    real, imag = total
    size = real.shape[0]
    both = left[0 : 2 * size]
    with_real = dot(left, high_ref[0, rows, cols])
    with_imag = dot(left, high_ref[1, rows, cols])
    with_real = with_real[: 2 * size] + with_real[2 * size :]
    with_imag = with_imag[: 2 * size] + with_imag[2 * size :]
    with_real += dot(both, low_ref[0, rows, cols])
    with_imag += dot(both, low_ref[1, rows, cols])
    real = real - (with_real[:size] - with_imag[size:])
    imag = imag - (with_imag[:size] + with_real[size:])
    return real, imag


def row_is_live(rows_ref, counts_ref, member, block):
    return lax.fori_loop(
        0,
        counts_ref[member],
        lambda q, seen: seen | (rows_ref[member, q] == block),
        False,
    )


def blocks_kernel(*refs):
    blocks, out_ref = refs[:-1], refs[-1]
    for place, block in zip(line_order(len(blocks)), blocks):
        both = 2 * block.shape[1]
        high, low = split(block[...].reshape(both, B))
        out_ref[place, 0:both, :] = high
        out_ref[place, both : 2 * both, :] = low


def select_kernel(n_row, share_rows, *refs):
    rows_ref, counts_ref, top, mine, mates, high_ref, low_ref, out_ref = refs[:8]
    sent, turned = refs[8:-1], refs[-1]
    leaves = rows_ref.shape[0]
    row_dev = out_ref.shape[1]
    share = turned.shape[3]
    me = lax.axis_index("row")
    my_block = (me * row_dev) // B
    my_col = lax.axis_index("col")
    for packed, first in ((mine, me), (mates, me ^ 1)):
        for step in range(0, n_row, 2):
            owner = first ^ step
            rows = pl.ds(pl.multiple_of(owner * share_rows, share_rows), share_rows)
            place = slice(step // 2 * share_rows, (step // 2 + 1) * share_rows)
            for part in range(2):
                high, low = split(packed[part, place, :])
                high_ref[part, rows, :] = high
                low_ref[part, rows, :] = low
    for member in range(leaves):
        cols = slice(member * B, (member + 1) * B)
        live = row_is_live(rows_ref, counts_ref, member, my_block)

        @pl.when(live)
        def _():
            def slot(q, total):
                place = my_col ^ rows_ref[member, q]
                rows = pl.ds(pl.multiple_of(q * B, B), B)
                return add_slot(total, top[place], high_ref, low_ref, rows, cols)

            zero = jnp.zeros((row_dev, B), F32)
            total = lax.fori_loop(0, counts_ref[member], slot, (zero, zero))
            for part, value in enumerate(total):
                out_ref[part, :, cols] = value
                turned[:, member, part] = value.T.reshape(n_row, share, row_dev)

        @pl.when(jnp.logical_not(live))
        def _():
            for part in range(2):
                out_ref[part, :, cols] = jnp.zeros((row_dev, B), F32)
                turned[:, member, part] = jnp.zeros((n_row, share, row_dev), F32)

    for step in range(n_row):
        sent[step][...] = turned[me ^ step]


def put_piece(out_ref, place, piece):
    leaves, _, share, row_dev = piece.shape
    high, low = split(piece[...].reshape(leaves, 2 * share, row_dev))
    out_ref[place, :, 0 : 2 * share] = high
    out_ref[place, :, 2 * share : 4 * share] = low


def pieces_kernel(*refs):
    pieces, out_ref = refs[:-1], refs[-1]
    me = lax.axis_index("row")
    for step, piece in enumerate(reversed(pieces), 2):
        put_piece(out_ref, me ^ step, piece)


def diagonal_kernel(rows_ref, mine, mates, others, high_ref, low_ref, diag_ref, out_ref, here):
    leaves, slots = rows_ref.shape
    _, _, share, row_dev = mine.shape
    me = lax.axis_index("row")
    put_piece(here, me % 2, mine)
    put_piece(here, 1 - me % 2, mates)
    for member in range(leaves):
        cols = slice(member * B, (member + 1) * B)
        left = []
        for q in range(slots):
            block = rows_ref[member, q]
            for core in range(B // row_dev):
                owner = block * (B // row_dev) + core
                left.append(
                    jnp.where(owner // 2 == me // 2, here[core, member], others[owner, member])
                )
        left = jnp.concatenate(left, axis=1)
        both = left[: 2 * share]
        with_real = dot(left, high_ref[0, :, cols])
        with_imag = dot(left, high_ref[1, :, cols])
        with_real = with_real[: 2 * share] + with_real[2 * share :]
        with_imag = with_imag[: 2 * share] + with_imag[2 * share :]
        with_real += dot(both, low_ref[0, :, cols])
        with_imag += dot(both, low_ref[1, :, cols])
        out_ref[0, :, cols] = diag_ref[0, :, cols] - (with_real[:share] - with_imag[share:])
        out_ref[1, :, cols] = diag_ref[1, :, cols] - (with_imag[:share] + with_real[share:])


def on_device(n_row, n_col, top_inverse, panel, leaf_rows, leaf_counts, diag_inverse):
    smem = pl.BlockSpec(memory_space=pltpu.SMEM)
    vmem = pl.BlockSpec(memory_space=pltpu.VMEM)
    params = pltpu.CompilerParams(vmem_limit_bytes=VMEM_LIMIT)
    _, row_dev, _ = top_inverse.shape
    _, panel_rows, columns = panel.shape
    leaves = columns // B
    share = B // n_row
    depth = n_row * panel_rows

    blocks = line_gather(top_inverse, "col", n_col)

    like = [panel]
    for step in range(2, n_row, 2):
        like.append(lax.ppermute(panel, "row", [(i, i ^ step) for i in range(n_row)]))
    like, _ = lax.optimization_barrier((like, blocks[: n_col // 2 + 1]))
    mine = pl.pallas_call(
        pack_kernel,
        out_shape=jax.ShapeDtypeStruct((2, depth // 2, columns), F32),
        in_specs=[vmem] * len(like),
        out_specs=vmem,
        compiler_params=params,
        cost_estimate=pl.CostEstimate(
            flops=0, bytes_accessed=8 * depth * columns, transcendentals=0
        ),
        name="pack_panel",
    )(*like)
    mates = lax.ppermute(mine, "row", [(i, i ^ 1) for i in range(n_row)])

    top = pl.pallas_call(
        blocks_kernel,
        out_shape=jax.ShapeDtypeStruct((len(blocks), 4 * row_dev, B), BF16),
        in_specs=[vmem] * len(blocks),
        out_specs=vmem,
        compiler_params=params,
        cost_estimate=pl.CostEstimate(
            flops=10**11, bytes_accessed=10**9, transcendentals=0
        ),
        name="split_blocks",
    )(*blocks)

    piece = jax.ShapeDtypeStruct((leaves, 2, share, row_dev), F32)
    high, low, selected, *sent = pl.pallas_call(
        functools.partial(select_kernel, n_row, panel_rows),
        out_shape=[jax.ShapeDtypeStruct((2, depth, columns), BF16)] * 2
        + [jax.ShapeDtypeStruct((2, row_dev, columns), F32)]
        + [piece] * n_row,
        in_specs=[smem, smem] + [vmem] * 3,
        out_specs=[vmem] * (3 + n_row),
        scratch_shapes=[pltpu.VMEM((n_row,) + piece.shape, F32)],
        compiler_params=params,
        cost_estimate=pl.CostEstimate(
            flops=24 * row_dev * depth * columns,
            bytes_accessed=8 * (n_col * row_dev * B + (2 * depth + 2 * row_dev) * columns),
            transcendentals=0,
        ),
        name="selected_rows",
    )(leaf_rows, leaf_counts, top, mine, mates)

    for step in range(n_row - 1, 0, -1):
        sent[step] = lax.ppermute(sent[step], "row", [(i, i ^ step) for i in range(n_row)])
    others = pl.pallas_call(
        pieces_kernel,
        out_shape=jax.ShapeDtypeStruct((n_row, leaves, 4 * share, row_dev), BF16),
        in_specs=[vmem] * (n_row - 2),
        out_specs=vmem,
        compiler_params=params,
        cost_estimate=pl.CostEstimate(
            flops=10**11, bytes_accessed=10**9, transcendentals=0
        ),
        name="split_pieces",
    )(*sent[:1:-1])

    diagonal = pl.pallas_call(
        diagonal_kernel,
        out_shape=jax.ShapeDtypeStruct(diag_inverse.shape, F32),
        in_specs=[smem] + [vmem] * 6,
        out_specs=vmem,
        scratch_shapes=[pltpu.VMEM((2, leaves, 4 * share, row_dev), BF16)],
        compiler_params=params,
        cost_estimate=pl.CostEstimate(
            flops=24 * share * depth * columns,
            bytes_accessed=8 * (depth + 2 * share) * columns,
            transcendentals=0,
        ),
        name="diagonal_rows",
    )(leaf_rows, sent[0], sent[1], others, high, low, diag_inverse)
    return selected, diagonal


def solution(mesh):
    return jax.shard_map(
        functools.partial(on_device, mesh.shape["row"], mesh.shape["col"]),
        mesh=mesh,
        in_specs=(
            P(None, "row", "col"),
            P(None, "row", "col"),
            P("col", None),
            P("col"),
            P(None, "row", "col"),
        ),
        out_specs=(P(None, "row", "col"), P(None, "row", "col")),
        check_vma=False,
    )
```

```python
import functools

import jax
import jax.numpy as jnp
from jax import lax
from jax.experimental import pallas as pl
from jax.experimental.pallas import tpu as pltpu
from jax.sharding import PartitionSpec as P

B = 256
F32 = jnp.float32
BF16 = jnp.bfloat16
VMEM_LIMIT = 48 * 1024 * 1024


def split(value):
    high = value.astype(BF16)
    low = (value - high.astype(F32)).astype(BF16)
    return high, low


def dot(left, right):
    return jnp.dot(left, right, preferred_element_type=F32)


def line_gather(own, axis, n):
    pieces = [own]
    for step in line_steps(n):
        perm = [(i, i ^ step) for i in range(n)]
        pieces += [lax.ppermute(piece, axis, perm) for piece in pieces]
    return pieces


def line_steps(n):
    steps = []
    while n > 1:
        n //= 2
        steps.append(n)
    return steps


def line_order(n):
    order = [0]
    for step in line_steps(n):
        order += [k ^ step for k in order]
    return order


def pack_kernel(*refs):
    pieces, out_ref = refs[:-1], refs[-1]
    share_rows = pieces[0].shape[1]
    for place, piece in enumerate(pieces):
        out_ref[:, place * share_rows : (place + 1) * share_rows, :] = piece[...]


def add_slot(total, left, high_ref, low_ref, rows, cols):
    real, imag = total
    size = real.shape[0]
    both = left[0 : 2 * size]
    left = jnp.concatenate([both, left[2 * size : 4 * size], both], axis=1)

    def panel(part):
        high, low = high_ref[part, rows, cols], low_ref[part, rows, cols]
        return jnp.concatenate([high, high, low], axis=0)

    with_real, with_imag = dot(left, panel(0)), dot(left, panel(1))
    real = real - (with_real[:size] - with_imag[size:])
    imag = imag - (with_imag[:size] + with_real[size:])
    return real, imag


def row_is_live(rows_ref, counts_ref, member, block):
    return lax.fori_loop(
        0,
        counts_ref[member],
        lambda q, seen: seen | (rows_ref[member, q] == block),
        False,
    )


def blocks_kernel(*refs):
    blocks, out_ref = refs[:-1], refs[-1]
    for place, block in zip(line_order(len(blocks)), blocks):
        both = 2 * block.shape[1]
        high, low = split(block[...].reshape(both, B))
        out_ref[place, 0:both, :] = high
        out_ref[place, both : 2 * both, :] = low


def select_kernel(n_row, share_rows, *refs):
    rows_hbm, counts_hbm, top, own, mate, mine, mates, high_ref, low_ref, out_hbm = refs[:10]
    sent, (turned, out_ref, rows_ref, counts_ref, in_sems, out_sems) = refs[10:-6], refs[-6:]
    leaves = rows_ref.shape[0]
    row_dev = out_ref.shape[1]
    chips, share = turned.shape[0], turned.shape[3]
    me = lax.axis_index("row")
    my_block = (me * row_dev) // B
    my_col = lax.axis_index("col")
    arrivals = [
        pltpu.make_async_copy(rows_hbm, rows_ref, in_sems.at[0]),
        pltpu.make_async_copy(counts_hbm, counts_ref, in_sems.at[1]),
    ]
    for copy in arrivals:
        copy.start()

    def put(owner, ref, place):
        rows = pl.ds(pl.multiple_of(owner * share_rows, share_rows), share_rows)
        for part in range(2):
            high, low = split(ref[part, place, :])
            high_ref[part, rows, :] = high
            low_ref[part, rows, :] = low

    for first, one, packed in ((me, own, mine), (me ^ 1, mate, mates)):
        put(first, one, slice(0, share_rows))
        for step in range(2, n_row, 2):
            put(first ^ step, packed, slice((step // 2 - 1) * share_rows, step // 2 * share_rows))
    for copy in arrivals:
        copy.wait()
    departures = []
    for member in range(leaves):
        cols = slice(member * B, (member + 1) * B)
        live = row_is_live(rows_ref, counts_ref, member, my_block)

        @pl.when(live)
        def _():
            def slot(q, total):
                place = my_col ^ rows_ref[member, q]
                rows = pl.ds(pl.multiple_of(q * B, B), B)
                return add_slot(total, top[place], high_ref, low_ref, rows, cols)

            zero = jnp.zeros((row_dev, B), F32)
            total = lax.fori_loop(0, counts_ref[member], slot, (zero, zero))
            for part, value in enumerate(total):
                out_ref[part, :, cols] = value
                turned[:, member, part] = value.T.reshape(chips, share, row_dev)

        @pl.when(jnp.logical_not(live))
        def _():
            for part in range(2):
                out_ref[part, :, cols] = jnp.zeros((row_dev, B), F32)
                turned[:, member, part] = jnp.zeros((chips, share, row_dev), F32)

        departures.append(
            pltpu.make_async_copy(
                out_ref.at[:, :, cols], out_hbm.at[:, :, cols], out_sems.at[member]
            )
        )
        departures[-1].start()

    for step in range(chips):
        sent[step][...] = turned[(me // 2) ^ step]
    for copy in departures:
        copy.wait()


def diagonal_kernel(rows_ref, *refs):
    pieces, (high_ref, low_ref, diag_ref, keep_ref, give_ref, turned, whole) = refs[:-7], refs[-7:]
    leaves, slots = rows_ref.shape
    _, _, chip_share, row_dev = pieces[0].shape
    share = keep_ref.shape[1]
    me = lax.axis_index("row")
    core = me % 2
    for step, piece in enumerate(reversed(pieces)):
        source = (me // 2) ^ step
        high, low = split(piece[...].reshape(leaves, 2 * chip_share, row_dev))
        turned[source, :, 0 : 2 * chip_share] = high
        turned[source, :, 2 * chip_share : 4 * chip_share] = low
    for member in range(leaves):
        cols = slice(member * B, (member + 1) * B)
        left = jnp.concatenate([turned[rows_ref[member, q], member] for q in range(slots)], axis=1)
        both = left[: 2 * chip_share]

        def panel(ref, part):
            starts = [pl.multiple_of(q * B + core * row_dev, row_dev) for q in range(slots)]
            return jnp.concatenate(
                [ref[part, pl.ds(start, row_dev), cols] for start in starts], axis=0
            )

        with_real = dot(left, panel(high_ref, 0))
        with_imag = dot(left, panel(high_ref, 1))
        with_real = with_real[: 2 * chip_share] + with_real[2 * chip_share :]
        with_imag = with_imag[: 2 * chip_share] + with_imag[2 * chip_share :]
        with_real += dot(both, panel(low_ref, 0))
        with_imag += dot(both, panel(low_ref, 1))
        whole[0, :, cols] = with_real[:chip_share] - with_imag[chip_share:]
        whole[1, :, cols] = with_imag[:chip_share] + with_real[chip_share:]
    mine = pl.ds(pl.multiple_of(core * share, share), share)
    other = pl.ds(pl.multiple_of((1 - core) * share, share), share)
    keep_ref[...] = diag_ref[...] - whole[:, mine, :]
    give_ref[...] = whole[:, other, :]


def subtract_kernel(left_ref, right_ref, out_ref):
    out_ref[...] = left_ref[...] - right_ref[...]


def on_device(n_row, n_col, top_inverse, panel, leaf_rows, leaf_counts, diag_inverse):
    smem = pl.BlockSpec(memory_space=pltpu.SMEM)
    vmem = pl.BlockSpec(memory_space=pltpu.VMEM)
    hbm = pl.BlockSpec(memory_space=pl.ANY)
    params = pltpu.CompilerParams(vmem_limit_bytes=VMEM_LIMIT)
    _, row_dev, _ = top_inverse.shape
    _, panel_rows, columns = panel.shape
    leaves = columns // B
    chips = n_row // 2
    chip_share = B // chips
    depth = n_row * panel_rows

    blocks = line_gather(top_inverse, "col", n_col)

    swap = [(i, i ^ 1) for i in range(n_row)]
    like = [
        lax.ppermute(panel, "row", [(i, i ^ step) for i in range(n_row)])
        for step in range(2, n_row, 2)
    ]
    mine = pl.pallas_call(
        pack_kernel,
        out_shape=jax.ShapeDtypeStruct((2, (n_row // 2 - 1) * panel_rows, columns), F32),
        in_specs=[vmem] * len(like),
        out_specs=vmem,
        compiler_params=params,
        cost_estimate=pl.CostEstimate(
            flops=0, bytes_accessed=8 * depth * columns, transcendentals=0
        ),
        name="pack_panel",
    )(*like)
    mate = lax.ppermute(panel, "row", swap)
    mates = lax.ppermute(mine, "row", swap)

    top = pl.pallas_call(
        blocks_kernel,
        out_shape=jax.ShapeDtypeStruct((len(blocks), 4 * row_dev, B), BF16),
        in_specs=[vmem] * len(blocks),
        out_specs=vmem,
        compiler_params=params,
        cost_estimate=pl.CostEstimate(
            flops=10**11, bytes_accessed=10**9, transcendentals=0
        ),
        name="split_blocks",
    )(*blocks)

    piece = jax.ShapeDtypeStruct((leaves, 2, chip_share, row_dev), F32)
    high, low, selected, *sent = pl.pallas_call(
        functools.partial(select_kernel, n_row, panel_rows),
        out_shape=[jax.ShapeDtypeStruct((2, depth, columns), BF16)] * 2
        + [jax.ShapeDtypeStruct((2, row_dev, columns), F32)]
        + [piece] * chips,
        in_specs=[hbm, hbm] + [vmem] * 5,
        out_specs=[vmem, vmem, hbm] + [vmem] * chips,
        scratch_shapes=[
            pltpu.VMEM((chips,) + piece.shape, F32),
            pltpu.VMEM((2, row_dev, columns), F32),
            pltpu.SMEM(leaf_rows.shape, leaf_rows.dtype),
            pltpu.SMEM(leaf_counts.shape, leaf_counts.dtype),
            pltpu.SemaphoreType.DMA((2,)),
            pltpu.SemaphoreType.DMA((leaves,)),
        ],
        compiler_params=params,
        cost_estimate=pl.CostEstimate(
            flops=24 * row_dev * depth * columns,
            bytes_accessed=8 * (n_col * row_dev * B + (2 * depth + 2 * row_dev) * columns),
            transcendentals=0,
        ),
        name="selected_rows",
    )(leaf_rows, leaf_counts, top, panel, mate, mine, mates)

    for step in range(chips - 1, 0, -1):
        perm = [(i, i ^ (2 * step)) for i in range(n_row)]
        sent[step] = lax.ppermute(sent[step], "row", perm)

    keep, give = pl.pallas_call(
        diagonal_kernel,
        out_shape=[jax.ShapeDtypeStruct(diag_inverse.shape, F32)] * 2,
        in_specs=[smem] + [vmem] * (chips + 3),
        out_specs=[vmem] * 2,
        scratch_shapes=[
            pltpu.VMEM((chips, leaves, 4 * chip_share, row_dev), BF16),
            pltpu.VMEM((2, chip_share, columns), F32),
        ],
        compiler_params=params,
        cost_estimate=pl.CostEstimate(
            flops=12 * chip_share * depth * columns,
            bytes_accessed=8 * (depth + 2 * chip_share) * columns,
            transcendentals=0,
        ),
        name="diagonal_part",
    )(leaf_rows, *sent[::-1], high, low, diag_inverse)
    give = lax.ppermute(give, "row", [(i, i ^ 1) for i in range(n_row)])
    diagonal = pl.pallas_call(
        subtract_kernel,
        out_shape=jax.ShapeDtypeStruct(diag_inverse.shape, F32),
        in_specs=[vmem] * 2,
        out_specs=vmem,
        compiler_params=params,
        name="diagonal_rows",
    )(keep, give)
    return selected, diagonal


def solution(mesh):
    return jax.shard_map(
        functools.partial(on_device, mesh.shape["row"], mesh.shape["col"]),
        mesh=mesh,
        in_specs=(
            P(None, "row", "col"),
            P(None, "row", "col"),
            P("col", None),
            P("col"),
            P(None, "row", "col"),
        ),
        out_specs=(P(None, "row", "col"), P(None, "row", "col")),
        check_vma=False,
    )
```

```python
import functools

import jax
import jax.numpy as jnp
from jax import lax
from jax.experimental import pallas as pl
from jax.experimental.pallas import tpu as pltpu
from jax.sharding import PartitionSpec as P

B = 256
HALVES = 2
F32 = jnp.float32
BF16 = jnp.bfloat16
VMEM_LIMIT = 48 * 1024 * 1024


def split(value):
    high = value.astype(BF16)
    low = (value - high.astype(F32)).astype(BF16)
    return high, low


def dot(left, right):
    return jnp.dot(left, right, preferred_element_type=F32)


def strip_order(n):
    order, step = [0], n // 2
    while step > 1:
        order += [place ^ step for place in order]
        step //= 2
    return order


def halves_kernel(block_ref, *out_refs):
    size = block_ref.shape[1] // HALVES
    for half, out_ref in enumerate(out_refs):
        out_ref[...] = block_ref[:, half * size : (half + 1) * size, :]


def pack_kernel(*refs):
    pieces, out_ref = refs[:-1], refs[-1]
    share_rows = pieces[0].shape[1]
    for place, piece in enumerate(pieces):
        out_ref[:, place * share_rows : (place + 1) * share_rows, :] = piece[...]


def blocks_kernel(order, half, *refs):
    blocks, out_ref = refs[:-1], refs[-1]
    size = out_ref.shape[1] // 4
    whole = len(order) + 1
    for place, block in zip(order + [1] + [place ^ 1 for place in order[1:]], blocks):
        value = block[:, half * size : (half + 1) * size, :] if whole > 0 else block[...]
        whole -= 1
        high, low = split(value.reshape(2 * size, B))
        out_ref[place, 0 : 2 * size, :] = high
        out_ref[place, 2 * size : 4 * size, :] = low


def add_slot(total, left, high_ref, low_ref, rows, cols):
    size = total.shape[0] // 2
    both = left[0 : 2 * size]
    left = jnp.concatenate([both, left[2 * size : 4 * size], both], axis=1)

    def panel(part):
        high, low = high_ref[part, rows, cols], low_ref[part, rows, cols]
        return jnp.concatenate([high, high, low], axis=0)

    with_real, with_imag = dot(left, panel(0)), dot(left, panel(1))
    turned = jnp.concatenate([-with_imag[size:], with_imag[:size]], axis=0)
    return total - (with_real + turned)


def split_panels(n_row, share_rows, own, mate, mine, mates, high_ref, low_ref):
    me = lax.axis_index("row")

    def put(owner, ref, place):
        rows = pl.ds(pl.multiple_of(owner * share_rows, share_rows), share_rows)
        for part in range(2):
            high, low = split(ref[part, place, :])
            high_ref[part, rows, :] = high
            low_ref[part, rows, :] = low

    for first, one, packed in ((me, own, mine), (me ^ 1, mate, mates)):
        put(first, one, slice(0, share_rows))
        for step in range(2, n_row, 2):
            put(first ^ step, packed, slice((step // 2 - 1) * share_rows, step // 2 * share_rows))


def select_half(rows_ref, counts_ref, top, high_ref, low_ref, out_ref, sent, turned):
    leaves = rows_ref.shape[0]
    size = out_ref.shape[1]
    chips, _, share, _ = turned.shape
    me = lax.axis_index("row")
    my_block = (me * size * HALVES) // B
    my_col = lax.axis_index("col")
    for member in range(leaves):
        cols = slice(member * B, (member + 1) * B)
        live = lax.fori_loop(
            0,
            counts_ref[member],
            lambda q, seen: seen | (rows_ref[member, q] == my_block),
            False,
        )

        @pl.when(live)
        def _():
            def slot(q, total):
                place = my_col ^ rows_ref[member, q]
                rows = pl.ds(pl.multiple_of(q * B, B), B)
                return add_slot(total, top[place], high_ref, low_ref, rows, cols)

            total = lax.fori_loop(0, counts_ref[member], slot, jnp.zeros((2 * size, B), F32))
            out_ref[0, :, cols] = total[:size]
            out_ref[1, :, cols] = total[size:]
            turned[:, member] = total.T.reshape(chips, share, 2 * size)

        @pl.when(jnp.logical_not(live))
        def _():
            out_ref[:, :, cols] = jnp.zeros((2, size, B), F32)
            turned[:, member] = jnp.zeros((chips, share, 2 * size), F32)

    for step in range(chips):
        sent[step][...] = turned[(me // 2) ^ step]


def first_kernel(n_row, share_rows, *refs):
    rows_hbm, counts_hbm, top, own, mate, mine, mates, high_ref, low_ref, out_ref = refs[:10]
    sent, (turned, rows_ref, counts_ref, sems) = refs[10:-4], refs[-4:]
    arrivals = [
        pltpu.make_async_copy(rows_hbm, rows_ref, sems.at[0]),
        pltpu.make_async_copy(counts_hbm, counts_ref, sems.at[1]),
    ]
    for copy in arrivals:
        copy.start()
    split_panels(n_row, share_rows, own, mate, mine, mates, high_ref, low_ref)
    for copy in arrivals:
        copy.wait()
    select_half(rows_ref, counts_ref, top, high_ref, low_ref, out_ref, sent, turned)


def second_kernel(*refs):
    rows_ref, counts_ref, top, high_ref, low_ref, out_ref = refs[:6]
    sent, turned = refs[6:-1], refs[-1]
    select_half(rows_ref, counts_ref, top, high_ref, low_ref, out_ref, sent, turned)


def join_kernel(*refs):
    halves, out_ref = refs[:-1], refs[-1]
    size = halves[0].shape[1]
    for half, ref in enumerate(halves):
        out_ref[:, half * size : (half + 1) * size, :] = ref[...]


def diagonal_kernel(chips, rows_ref, *refs):
    firsts, seconds = refs[:chips], refs[chips : 2 * chips]
    high_ref, low_ref, diag_ref, keep_ref, give_ref, turned, whole = refs[2 * chips :]
    leaves, slots = rows_ref.shape
    _, chip_share, row_dev = firsts[0].shape
    share = keep_ref.shape[1]
    me = lax.axis_index("row")
    core = me % 2
    lane = lax.broadcasted_iota(jnp.int32, (chip_share, row_dev), 1)
    for step in range(chips):
        source = (me // 2) ^ (chips - 1 - step)
        for member in range(leaves):
            first, second = firsts[step][member], seconds[step][member]
            real = jnp.where(2 * lane < row_dev, first, pltpu.roll(second, row_dev // 2, 1))
            imag = jnp.where(2 * lane < row_dev, pltpu.roll(first, row_dev // 2, 1), second)
            high, low = split(jnp.concatenate([real, imag], axis=0))
            turned[source, member, 0 : 2 * chip_share] = high
            turned[source, member, 2 * chip_share : 4 * chip_share] = low
    for member in range(leaves):
        cols = slice(member * B, (member + 1) * B)
        left = jnp.concatenate([turned[rows_ref[member, q], member] for q in range(slots)], axis=1)
        both = left[: 2 * chip_share]

        def panel(ref, part):
            starts = [pl.multiple_of(q * B + core * row_dev, row_dev) for q in range(slots)]
            return jnp.concatenate(
                [ref[part, pl.ds(start, row_dev), cols] for start in starts], axis=0
            )

        with_real = dot(left, panel(high_ref, 0))
        with_imag = dot(left, panel(high_ref, 1))
        with_real = with_real[: 2 * chip_share] + with_real[2 * chip_share :]
        with_imag = with_imag[: 2 * chip_share] + with_imag[2 * chip_share :]
        with_real += dot(both, panel(low_ref, 0))
        with_imag += dot(both, panel(low_ref, 1))
        whole[0, :, cols] = with_real[:chip_share] - with_imag[chip_share:]
        whole[1, :, cols] = with_imag[:chip_share] + with_real[chip_share:]
    mine = pl.ds(pl.multiple_of(core * share, share), share)
    other = pl.ds(pl.multiple_of((1 - core) * share, share), share)
    keep_ref[...] = diag_ref[...] - whole[:, mine, :]
    give_ref[...] = whole[:, other, :]


def subtract_kernel(left_ref, right_ref, out_ref):
    out_ref[...] = left_ref[...] - right_ref[...]


def estimate(flops, size):
    return pl.CostEstimate(flops=flops, bytes_accessed=size, transcendentals=0)


def on_device(n_row, n_col, top_inverse, panel, leaf_rows, leaf_counts, diag_inverse):
    smem = pl.BlockSpec(memory_space=pltpu.SMEM)
    vmem = pl.BlockSpec(memory_space=pltpu.VMEM)
    hbm = pl.BlockSpec(memory_space=pl.ANY)
    params = pltpu.CompilerParams(vmem_limit_bytes=VMEM_LIMIT)
    late = estimate(10**11, 10**9)
    _, row_dev, _ = top_inverse.shape
    _, panel_rows, columns = panel.shape
    leaves = columns // B
    chips = n_row // 2
    share = B // chips
    depth = n_row * panel_rows
    size = row_dev // HALVES

    def swap(value, axis, step):
        count = {"row": n_row, "col": n_col}[axis]
        return lax.ppermute(value, axis, [(i, i ^ step) for i in range(count)])

    order = strip_order(n_col)
    blocks, step = [top_inverse], n_col // 2
    while step > 1:
        blocks += [swap(block, "col", step) for block in blocks]
        step //= 2
    handed = [[] for _ in range(HALVES)]
    for block in blocks[1:]:
        halves = pl.pallas_call(
            halves_kernel,
            out_shape=[jax.ShapeDtypeStruct((2, size, B), F32)] * HALVES,
            in_specs=[vmem],
            out_specs=[vmem] * HALVES,
            compiler_params=params,
            name="cut_rows",
        )(block)
        for half in range(HALVES):
            handed[half].append(swap(halves[half], "col", 1))
    blocks.append(swap(top_inverse, "col", 1))

    like = [swap(panel, "row", step) for step in range(2, n_row, 2)]
    mine = pl.pallas_call(
        pack_kernel,
        out_shape=jax.ShapeDtypeStruct((2, (chips - 1) * panel_rows, columns), F32),
        in_specs=[vmem] * len(like),
        out_specs=vmem,
        compiler_params=params,
        name="pack_panel",
    )(*like)
    mate = swap(panel, "row", 1)
    mates = swap(mine, "row", 1)

    tops = [
        pl.pallas_call(
            functools.partial(blocks_kernel, order, half),
            out_shape=jax.ShapeDtypeStruct((n_col, 4 * size, B), BF16),
            in_specs=[vmem] * n_col,
            out_specs=vmem,
            compiler_params=params,
            cost_estimate=late,
            name="split_blocks",
        )(*blocks, *handed[half])
        for half in range(HALVES)
    ]

    piece = jax.ShapeDtypeStruct((leaves, share, 2 * size), F32)
    part = [jax.ShapeDtypeStruct((2, size, columns), F32)] + [piece] * chips
    high, low, first, *sent = pl.pallas_call(
        functools.partial(first_kernel, n_row, panel_rows),
        out_shape=[jax.ShapeDtypeStruct((2, depth, columns), BF16)] * 2 + part,
        in_specs=[hbm, hbm] + [vmem] * 5,
        out_specs=[vmem] * (3 + chips),
        scratch_shapes=[
            pltpu.VMEM((chips,) + piece.shape, F32),
            pltpu.SMEM(leaf_rows.shape, leaf_rows.dtype),
            pltpu.SMEM(leaf_counts.shape, leaf_counts.dtype),
            pltpu.SemaphoreType.DMA((2,)),
        ],
        compiler_params=params,
        cost_estimate=estimate(12 * row_dev * depth * columns, 16 * depth * columns),
        name="first_rows",
    )(leaf_rows, leaf_counts, tops[0], panel, mate, mine, mates)
    def exchange(pieces):
        moved = [swap(pieces[step], "row", 2 * step) for step in range(chips - 1, 0, -1)]
        return moved + pieces[:1]

    sent, top = lax.optimization_barrier((exchange(sent), tops[1]))
    second, *sent_second = pl.pallas_call(
        second_kernel,
        out_shape=part,
        in_specs=[smem, smem] + [vmem] * 3,
        out_specs=[vmem] * (1 + chips),
        scratch_shapes=[pltpu.VMEM((chips,) + piece.shape, F32)],
        compiler_params=params,
        cost_estimate=estimate(12 * row_dev * depth * columns, 8 * depth * columns),
        name="second_rows",
    )(leaf_rows, leaf_counts, top, high, low)
    selected = pl.pallas_call(
        join_kernel,
        out_shape=jax.ShapeDtypeStruct((2, row_dev, columns), F32),
        in_specs=[vmem] * 2,
        out_specs=vmem,
        compiler_params=params,
        name="join_rows",
    )(first, second)

    selected, sent_second = lax.optimization_barrier((selected, exchange(sent_second)))

    keep, give = pl.pallas_call(
        functools.partial(diagonal_kernel, chips),
        out_shape=[jax.ShapeDtypeStruct(diag_inverse.shape, F32)] * 2,
        in_specs=[smem] + [vmem] * (2 * chips + 3),
        out_specs=[vmem] * 2,
        scratch_shapes=[
            pltpu.VMEM((chips, leaves, 4 * share, row_dev), BF16),
            pltpu.VMEM((2, share, columns), F32),
        ],
        compiler_params=params,
        cost_estimate=estimate(12 * share * depth * columns, 8 * depth * columns),
        name="diagonal_part",
    )(leaf_rows, *sent, *sent_second, high, low, diag_inverse)
    give = swap(give, "row", 1)
    diagonal = pl.pallas_call(
        subtract_kernel,
        out_shape=jax.ShapeDtypeStruct(diag_inverse.shape, F32),
        in_specs=[vmem] * 2,
        out_specs=vmem,
        compiler_params=params,
        name="diagonal_rows",
    )(keep, give)
    return selected, diagonal


def solution(mesh):
    return jax.shard_map(
        functools.partial(on_device, mesh.shape["row"], mesh.shape["col"]),
        mesh=mesh,
        in_specs=(
            P(None, "row", "col"),
            P(None, "row", "col"),
            P("col", None),
            P("col"),
            P(None, "row", "col"),
        ),
        out_specs=(P(None, "row", "col"), P(None, "row", "col")),
        check_vma=False,
    )
```

```python
import functools

import jax
import jax.numpy as jnp
from jax import lax
from jax.experimental import pallas as pl
from jax.experimental.pallas import tpu as pltpu
from jax.sharding import PartitionSpec as P

B = 256
F32 = jnp.float32
BF16 = jnp.bfloat16


def split(value):
    high = value.astype(BF16)
    low = (value - high.astype(F32)).astype(BF16)
    return high, low


def dot(left, right):
    return jnp.dot(left, right, preferred_element_type=F32)


def line_gather(own, axis, n):
    pieces = [own]
    for step in line_steps(n):
        perm = [(i, i ^ step) for i in range(n)]
        pieces += [lax.ppermute(piece, axis, perm) for piece in pieces]
    return pieces


def line_steps(n):
    steps = []
    while n > 1:
        n //= 2
        steps.append(n)
    return steps


def line_order(n):
    order = [0]
    for step in line_steps(n):
        order += [k ^ step for k in order]
    return order


def pack_kernel(*refs):
    (rows_ref, counts_ref), pieces = refs[:2], refs[2:-5]
    out_ref, high_ref, low_ref, rows_out, counts_out = refs[-5:]
    rows_out[...] = rows_ref[...]
    counts_out[...] = counts_ref[...]
    share_rows = pieces[0].shape[1]
    for place, piece in enumerate(pieces):
        here = slice(place * share_rows, (place + 1) * share_rows)
        out_ref[:, here, :] = piece[...]
        for part in range(2):
            high_ref[part, here, :], low_ref[part, here, :] = split(piece[part])


def add_slot(total, left, high_ref, low_ref, rows, cols):
    real, imag = total
    size = real.shape[0]
    both = left[0 : 2 * size]
    left = jnp.concatenate([both, left[2 * size : 4 * size], both], axis=1)

    def panel(part):
        high, low = high_ref[part, rows, cols], low_ref[part, rows, cols]
        return jnp.concatenate([high, high, low], axis=0)

    with_real, with_imag = dot(left, panel(0)), dot(left, panel(1))
    real = real - (with_real[:size] - with_imag[size:])
    imag = imag - (with_imag[:size] + with_real[size:])
    return real, imag


def row_is_live(rows_ref, counts_ref, member, block):
    return lax.fori_loop(
        0,
        counts_ref[0, member],
        lambda q, seen: seen | (rows_ref[member, q] == block),
        False,
    )


def blocks_kernel(*refs):
    blocks, out_ref = refs[:-1], refs[-1]
    for place, block in zip(line_order(len(blocks)), blocks):
        both = 2 * block.shape[1]
        high, low = split(block[...].reshape(both, B))
        out_ref[place, 0:both, :] = high
        out_ref[place, both : 2 * both, :] = low


def select_kernel(n_row, share_rows, *refs):
    rows_hbm, counts_hbm, top, own, mine_high, mine_low, mate, mates = refs[:8]
    high_ref, low_ref, out_ref = refs[8:11]
    sent, (turned, rows_ref, counts_ref, in_sems) = refs[11:-4], refs[-4:]
    leaves = rows_ref.shape[0]
    row_dev = out_ref.shape[1]
    chips, share = turned.shape[0], turned.shape[3]
    me = lax.axis_index("row")
    my_block = (me * row_dev) // B
    my_col = lax.axis_index("col")
    arrivals = [
        pltpu.make_async_copy(rows_hbm, rows_ref, in_sems.at[0]),
        pltpu.make_async_copy(counts_hbm, counts_ref, in_sems.at[1]),
    ]
    for copy in arrivals:
        copy.start()

    def put(owner, high, low):
        rows = pl.ds(pl.multiple_of(owner * share_rows, share_rows), share_rows)
        high_ref[:, rows, :], low_ref[:, rows, :] = high, low

    put(me, *split(own[...]))
    put(me ^ 1, *split(mate[...]))
    for step in range(1, chips):
        here = slice((step - 1) * share_rows, step * share_rows)
        put(me ^ (2 * step), mine_high[:, here, :], mine_low[:, here, :])
        put(me ^ (2 * step) ^ 1, *split(mates[:, here, :]))
    for copy in arrivals:
        copy.wait()
    for member in range(leaves):
        cols = slice(member * B, (member + 1) * B)
        live = row_is_live(rows_ref, counts_ref, member, my_block)

        @pl.when(live)
        def _():
            def slot(q, total):
                place = my_col ^ rows_ref[member, q]
                rows = pl.ds(pl.multiple_of(q * B, B), B)
                return add_slot(total, top[place], high_ref, low_ref, rows, cols)

            zero = jnp.zeros((row_dev, B), F32)
            total = lax.fori_loop(0, counts_ref[0, member], slot, (zero, zero))
            for part, value in enumerate(total):
                out_ref[part, :, cols] = value
                turned[:, member, part] = value.T.reshape(chips, share, row_dev)

        @pl.when(jnp.logical_not(live))
        def _():
            for part in range(2):
                out_ref[part, :, cols] = jnp.zeros((row_dev, B), F32)
                turned[:, member, part] = jnp.zeros((chips, share, row_dev), F32)

    for step in range(chips):
        sent[step][...] = turned[(me // 2) ^ step]


def write_kernel(value_ref, out_ref):
    out_ref[...] = value_ref[...]


def diagonal_kernel(rows_hbm, *refs):
    pieces, (high_ref, low_ref, diag_ref, keep_ref, give_ref) = refs[:-9], refs[-9:-4]
    turned, whole, rows_ref, sem = refs[-4:]
    arrival = pltpu.make_async_copy(rows_hbm, rows_ref, sem)
    arrival.start()
    leaves, slots = rows_ref.shape
    _, _, chip_share, row_dev = pieces[0].shape
    share = keep_ref.shape[1]
    me = lax.axis_index("row")
    core = me % 2
    for step, piece in enumerate(reversed(pieces)):
        source = (me // 2) ^ step
        high, low = split(piece[...].reshape(leaves, 2 * chip_share, row_dev))
        turned[source, :, 0 : 2 * chip_share] = high
        turned[source, :, 2 * chip_share : 4 * chip_share] = low
    arrival.wait()
    for member in range(leaves):
        cols = slice(member * B, (member + 1) * B)
        left = jnp.concatenate([turned[rows_ref[member, q], member] for q in range(slots)], axis=1)
        both = left[: 2 * chip_share]

        def panel(ref, part):
            starts = [pl.multiple_of(q * B + core * row_dev, row_dev) for q in range(slots)]
            return jnp.concatenate(
                [ref[part, pl.ds(start, row_dev), cols] for start in starts], axis=0
            )

        with_real = dot(left, panel(high_ref, 0))
        with_imag = dot(left, panel(high_ref, 1))
        with_real = with_real[: 2 * chip_share] + with_real[2 * chip_share :]
        with_imag = with_imag[: 2 * chip_share] + with_imag[2 * chip_share :]
        with_real += dot(both, panel(low_ref, 0))
        with_imag += dot(both, panel(low_ref, 1))
        whole[0, :, cols] = with_real[:chip_share] - with_imag[chip_share:]
        whole[1, :, cols] = with_imag[:chip_share] + with_real[chip_share:]
    mine = pl.ds(pl.multiple_of(core * share, share), share)
    other = pl.ds(pl.multiple_of((1 - core) * share, share), share)
    keep_ref[...] = diag_ref[...] - whole[:, mine, :]
    give_ref[...] = whole[:, other, :]


def subtract_kernel(left_ref, right_ref, out_ref):
    out_ref[...] = left_ref[...] - right_ref[...]


def on_device(n_row, n_col, top_inverse, panel, leaf_rows, leaf_counts, diag_inverse):
    vmem = pl.BlockSpec(memory_space=pltpu.VMEM)
    hbm = pl.BlockSpec(memory_space=pl.ANY)
    _, row_dev, _ = top_inverse.shape
    _, panel_rows, columns = panel.shape
    leaves = columns // B
    chips = n_row // 2
    chip_share = B // chips
    depth = n_row * panel_rows
    params = pltpu.CompilerParams(vmem_limit_bytes=max(16 << 20, 40 * depth * columns))

    blocks = line_gather(top_inverse, "col", n_col)

    swap = [(i, i ^ 1) for i in range(n_row)]
    like = [
        lax.ppermute(panel, "row", [(i, i ^ step) for i in range(n_row)])
        for step in range(2, n_row, 2)
    ]
    like = lax.optimization_barrier((like, blocks[: n_col // 2 + 1]))[0]
    packed = (2, depth // 2 - panel_rows, columns)
    leaf_counts = leaf_counts[None, :]
    mine, mine_high, mine_low, leaf_rows, leaf_counts = pl.pallas_call(
        pack_kernel,
        out_shape=[jax.ShapeDtypeStruct(packed, dtype) for dtype in (F32, BF16, BF16)]
        + [jax.ShapeDtypeStruct(value.shape, value.dtype) for value in (leaf_rows, leaf_counts)],
        in_specs=[vmem] * (2 + len(like)),
        out_specs=[vmem] * 5,
        compiler_params=params,
        name="pack_panel",
    )(leaf_rows, leaf_counts, *like)
    mate = lax.ppermute(panel, "row", swap)
    mates = lax.ppermute(mine, "row", swap)

    top = pl.pallas_call(
        blocks_kernel,
        out_shape=jax.ShapeDtypeStruct((len(blocks), 4 * row_dev, B), BF16),
        in_specs=[vmem] * len(blocks),
        out_specs=vmem,
        compiler_params=params,
        cost_estimate=pl.CostEstimate(
            flops=10**11, bytes_accessed=10**9, transcendentals=0
        ),
        name="split_blocks",
    )(*blocks)

    piece = jax.ShapeDtypeStruct((leaves, 2, chip_share, row_dev), F32)
    high, low, selected, *sent = pl.pallas_call(
        functools.partial(select_kernel, n_row, panel_rows),
        out_shape=[jax.ShapeDtypeStruct((2, depth, columns), BF16)] * 2
        + [jax.ShapeDtypeStruct((2, row_dev, columns), F32)]
        + [piece] * chips,
        in_specs=[hbm, hbm] + [vmem] * 6,
        out_specs=[vmem] * (3 + chips),
        scratch_shapes=[
            pltpu.VMEM((chips,) + piece.shape, F32),
            pltpu.SMEM(leaf_rows.shape, leaf_rows.dtype),
            pltpu.SMEM(leaf_counts.shape, leaf_counts.dtype),
            pltpu.SemaphoreType.DMA((2,)),
        ],
        compiler_params=params,
        cost_estimate=pl.CostEstimate(
            flops=24 * row_dev * depth * columns,
            bytes_accessed=8 * (n_col * row_dev * B + (2 * depth + 2 * row_dev) * columns),
            transcendentals=0,
        ),
        name="selected_rows",
    )(leaf_rows, leaf_counts, top, panel, mine_high, mine_low, mate, mates)

    for step in range(chips - 1, 0, -1):
        perm = [(i, i ^ (2 * step)) for i in range(n_row)]
        sent[step] = lax.ppermute(sent[step], "row", perm)
    selected = pl.pallas_call(
        write_kernel,
        out_shape=jax.ShapeDtypeStruct(selected.shape, F32),
        in_specs=[vmem],
        out_specs=vmem,
        compiler_params=params,
        name="write_rows",
    )(selected)
    selected, sent = lax.optimization_barrier((selected, sent[::-1]))

    keep, give = pl.pallas_call(
        diagonal_kernel,
        out_shape=[jax.ShapeDtypeStruct(diag_inverse.shape, F32)] * 2,
        in_specs=[hbm] + [vmem] * (chips + 3),
        out_specs=[vmem] * 2,
        scratch_shapes=[
            pltpu.VMEM((chips, leaves, 4 * chip_share, row_dev), BF16),
            pltpu.VMEM((2, chip_share, columns), F32),
            pltpu.SMEM(leaf_rows.shape, leaf_rows.dtype),
            pltpu.SemaphoreType.DMA,
        ],
        compiler_params=params,
        cost_estimate=pl.CostEstimate(
            flops=12 * chip_share * depth * columns,
            bytes_accessed=8 * (depth + 2 * chip_share) * columns,
            transcendentals=0,
        ),
        name="diagonal_part",
    )(leaf_rows, *sent, high, low, diag_inverse)
    give = lax.ppermute(give, "row", [(i, i ^ 1) for i in range(n_row)])
    diagonal = pl.pallas_call(
        subtract_kernel,
        out_shape=jax.ShapeDtypeStruct(diag_inverse.shape, F32),
        in_specs=[vmem] * 2,
        out_specs=vmem,
        compiler_params=params,
        name="diagonal_rows",
    )(keep, give)
    return selected, diagonal


def solution(mesh):
    return jax.shard_map(
        functools.partial(on_device, mesh.shape["row"], mesh.shape["col"]),
        mesh=mesh,
        in_specs=(
            P(None, "row", "col"),
            P(None, "row", "col"),
            P("col", None),
            P("col"),
            P(None, "row", "col"),
        ),
        out_specs=(P(None, "row", "col"), P(None, "row", "col")),
        check_vma=False,
    )
```

```python
import functools

import jax
import jax.numpy as jnp
from jax import lax
from jax.experimental import pallas as pl
from jax.experimental.pallas import tpu as pltpu
from jax.sharding import PartitionSpec as P

B = 256
F32 = jnp.float32
BF16 = jnp.bfloat16


def split(value):
    high = value.astype(BF16)
    low = (value - high.astype(F32)).astype(BF16)
    return high, low


def dot(left, right):
    return jnp.dot(left, right, preferred_element_type=F32)


def line_gather(own, axis, n, cut):
    blocks = {0: own}
    for step in line_steps(n):
        perm = [(i, i ^ step) for i in range(n)]
        if step > 1:
            blocks |= {k ^ step: lax.ppermute(block, axis, perm) for k, block in blocks.items()}
    halves = {k ^ 1: cut(block) for k, block in blocks.items() if k > 0}
    halves = {k: [lax.ppermute(half, axis, perm) for half in pair] for k, pair in halves.items()}
    blocks[1] = lax.ppermute(own, axis, perm)
    return blocks, halves


def line_steps(n):
    steps = []
    while n > 1:
        n //= 2
        steps.append(n)
    return steps


def cut_kernel(block_ref, *out_refs):
    size = block_ref.shape[1] // len(out_refs)
    for half, out_ref in enumerate(out_refs):
        out_ref[...] = block_ref[:, half * size : (half + 1) * size, :]


def pack_kernel(*refs):
    (rows_ref, counts_ref), pieces = refs[:2], refs[2:-5]
    out_ref, high_ref, low_ref, rows_out, counts_out = refs[-5:]
    rows_out[...] = rows_ref[...]
    counts_out[...] = counts_ref[...]
    share_rows = pieces[0].shape[1]
    for place, piece in enumerate(pieces):
        here = slice(place * share_rows, (place + 1) * share_rows)
        out_ref[:, here, :] = piece[...]
        for part in range(2):
            high_ref[part, here, :], low_ref[part, here, :] = split(piece[part])


def add_slot(total, left, high_ref, low_ref, rows, cols):
    real, imag = total
    size = real.shape[0]
    both = left[0 : 2 * size]
    left = jnp.concatenate([both, left[2 * size : 4 * size], both], axis=1)

    def panel(part):
        high, low = high_ref[part, rows, cols], low_ref[part, rows, cols]
        return jnp.concatenate([high, high, low], axis=0)

    with_real, with_imag = dot(left, panel(0)), dot(left, panel(1))
    real = real - (with_real[:size] - with_imag[size:])
    imag = imag - (with_imag[:size] + with_real[size:])
    return real, imag


def row_is_live(rows_ref, counts_ref, member, block):
    return lax.fori_loop(
        0,
        counts_ref[0, member],
        lambda q, seen: seen | (rows_ref[member, q] == block),
        False,
    )


def blocks_kernel(*refs):
    pieces, out_ref = refs[:-1], refs[-1]
    rows = out_ref.shape[1] // 4
    for k, piece in enumerate(pieces):
        size = piece.shape[1]
        place, first = k * size // rows, k * size % rows
        for part in range(2):
            for scale, value in enumerate(split(piece[part])):
                start = (2 * scale + part) * rows + first
                out_ref[place, start : start + size, :] = value


def add_slots(member, top, places, rows_ref, counts_ref, high_ref, low_ref, out_ref):
    row_dev = out_ref.shape[1]
    my_block = (lax.axis_index("row") * row_dev) // B
    my_col = lax.axis_index("col")
    cols = slice(member * B, (member + 1) * B)
    live = row_is_live(rows_ref, counts_ref, member, my_block)

    def slot(q, carry):
        held, place = places(my_col ^ rows_ref[member, q])

        @pl.when(held)
        def _():
            rows = pl.ds(pl.multiple_of(q * B, B), B)
            total = out_ref[0, :, cols], out_ref[1, :, cols]
            total = add_slot(total, top[place], high_ref, low_ref, rows, cols)
            out_ref[0, :, cols], out_ref[1, :, cols] = total

        return carry

    lax.fori_loop(0, jnp.where(live, counts_ref[0, member], 0), slot, 0)


def early_place(n_col, distance):
    return (distance % 2 == 0) | (distance == 1), jnp.where(distance == 1, n_col // 2, distance // 2)


def late_place(distance):
    return (distance % 2 == 1) & (distance > 1), (distance - 3) // 2


def fetch(sems, *pairs):
    copies = [pltpu.make_async_copy(*pair, sems.at[k]) for k, pair in enumerate(pairs)]
    for copy in copies:
        copy.start()
    return copies


def early_kernel(n_col, share_rows, chips, *refs):
    rows_hbm, counts_hbm, top, own, mine_high, mine_low, mate, mates = refs[:8]
    high_ref, low_ref, out_ref, rows_ref, counts_ref, sems = refs[8:]
    leaves = rows_ref.shape[0]
    me = lax.axis_index("row")
    arrivals = fetch(sems, (rows_hbm, rows_ref), (counts_hbm, counts_ref))

    def put(owner, high, low):
        rows = pl.ds(pl.multiple_of(owner * share_rows, share_rows), share_rows)
        high_ref[:, rows, :], low_ref[:, rows, :] = high, low

    put(me, *split(own[...]))
    put(me ^ 1, *split(mate[...]))
    for step in range(1, chips):
        here = slice((step - 1) * share_rows, step * share_rows)
        put(me ^ (2 * step), mine_high[:, here, :], mine_low[:, here, :])
        put(me ^ (2 * step) ^ 1, *split(mates[:, here, :]))
    out_ref[...] = jnp.zeros(out_ref.shape, F32)
    for copy in arrivals:
        copy.wait()
    places = functools.partial(early_place, n_col)
    for member in range(leaves):
        add_slots(member, top, places, rows_ref, counts_ref, high_ref, low_ref, out_ref)


def select_kernel(*refs):
    rows_hbm, counts_hbm, top, early_ref, high_ref, low_ref, out_ref = refs[:7]
    sent, (turned, rows_ref, counts_ref, sems) = refs[7:-4], refs[-4:]
    leaves = rows_ref.shape[0]
    row_dev = out_ref.shape[1]
    chips, share = turned.shape[0], turned.shape[3]
    me = lax.axis_index("row")
    arrivals = fetch(sems, (rows_hbm, rows_ref), (counts_hbm, counts_ref))
    out_ref[...] = early_ref[...]
    for copy in arrivals:
        copy.wait()
    for member in range(leaves):
        cols = slice(member * B, (member + 1) * B)
        add_slots(member, top, late_place, rows_ref, counts_ref, high_ref, low_ref, out_ref)
        for part in range(2):
            turned[:, member, part] = out_ref[part, :, cols].T.reshape(chips, share, row_dev)
    for step in range(chips):
        sent[step][...] = turned[(me // 2) ^ step]


def write_kernel(value_ref, out_ref):
    out_ref[...] = value_ref[...]


def diagonal_kernel(rows_hbm, *refs):
    pieces, (high_ref, low_ref, diag_ref, keep_ref, give_ref) = refs[:-9], refs[-9:-4]
    turned, whole, rows_ref, sem = refs[-4:]
    arrival = pltpu.make_async_copy(rows_hbm, rows_ref, sem)
    arrival.start()
    leaves, slots = rows_ref.shape
    _, _, chip_share, row_dev = pieces[0].shape
    share = keep_ref.shape[1]
    me = lax.axis_index("row")
    core = me % 2
    for step, piece in enumerate(reversed(pieces)):
        source = (me // 2) ^ step
        high, low = split(piece[...].reshape(leaves, 2 * chip_share, row_dev))
        turned[source, :, 0 : 2 * chip_share] = high
        turned[source, :, 2 * chip_share : 4 * chip_share] = low
    arrival.wait()
    for member in range(leaves):
        cols = slice(member * B, (member + 1) * B)
        left = jnp.concatenate([turned[rows_ref[member, q], member] for q in range(slots)], axis=1)
        both = left[: 2 * chip_share]

        def panel(ref, part):
            starts = [pl.multiple_of(q * B + core * row_dev, row_dev) for q in range(slots)]
            return jnp.concatenate(
                [ref[part, pl.ds(start, row_dev), cols] for start in starts], axis=0
            )

        with_real = dot(left, panel(high_ref, 0))
        with_imag = dot(left, panel(high_ref, 1))
        with_real = with_real[: 2 * chip_share] + with_real[2 * chip_share :]
        with_imag = with_imag[: 2 * chip_share] + with_imag[2 * chip_share :]
        with_real += dot(both, panel(low_ref, 0))
        with_imag += dot(both, panel(low_ref, 1))
        whole[0, :, cols] = with_real[:chip_share] - with_imag[chip_share:]
        whole[1, :, cols] = with_imag[:chip_share] + with_real[chip_share:]
    mine = pl.ds(pl.multiple_of(core * share, share), share)
    other = pl.ds(pl.multiple_of((1 - core) * share, share), share)
    keep_ref[...] = diag_ref[...] - whole[:, mine, :]
    give_ref[...] = whole[:, other, :]


def subtract_kernel(left_ref, right_ref, out_ref):
    out_ref[...] = left_ref[...] - right_ref[...]


def on_device(n_row, n_col, top_inverse, panel, leaf_rows, leaf_counts, diag_inverse):
    vmem = pl.BlockSpec(memory_space=pltpu.VMEM)
    hbm = pl.BlockSpec(memory_space=pl.ANY)
    _, row_dev, _ = top_inverse.shape
    _, panel_rows, columns = panel.shape
    leaves = columns // B
    chips = n_row // 2
    chip_share = B // chips
    depth = n_row * panel_rows
    params = pltpu.CompilerParams(vmem_limit_bytes=max(16 << 20, 40 * depth * columns))

    def cut(block):
        half = jax.ShapeDtypeStruct((2, row_dev // 2, B), F32)
        return pl.pallas_call(
            cut_kernel,
            out_shape=[half, half],
            in_specs=[vmem],
            out_specs=[vmem] * 2,
            compiler_params=params,
            name="cut_rows",
        )(block)

    blocks, halves = line_gather(top_inverse, "col", n_col, cut)

    swap = [(i, i ^ 1) for i in range(n_row)]
    like = [
        lax.ppermute(panel, "row", [(i, i ^ step) for i in range(n_row)])
        for step in range(2, n_row, 2)
    ]
    like = lax.optimization_barrier((like, blocks))[0]
    packed = (2, depth // 2 - panel_rows, columns)
    leaf_counts = leaf_counts[None, :]
    mine, mine_high, mine_low, leaf_rows, leaf_counts = pl.pallas_call(
        pack_kernel,
        out_shape=[jax.ShapeDtypeStruct(packed, dtype) for dtype in (F32, BF16, BF16)]
        + [jax.ShapeDtypeStruct(value.shape, value.dtype) for value in (leaf_rows, leaf_counts)],
        in_specs=[vmem] * (2 + len(like)),
        out_specs=[vmem] * 5,
        compiler_params=params,
        name="pack_panel",
    )(leaf_rows, leaf_counts, *like)
    mate = lax.ppermute(panel, "row", swap)
    mates = lax.ppermute(mine, "row", swap)

    early_blocks = [blocks[k] for k in range(0, n_col, 2)] + [blocks[1]]
    firsts = [halves[k][0] for k in range(3, n_col, 2)]
    early_blocks, firsts = lax.optimization_barrier((early_blocks, firsts))
    late_blocks = [half for k in range(3, n_col, 2) for half in halves[k]]

    def split_blocks(values):
        count = sum(value.shape[1] for value in values) // row_dev
        return pl.pallas_call(
            blocks_kernel,
            out_shape=jax.ShapeDtypeStruct((count, 4 * row_dev, B), BF16),
            in_specs=[vmem] * len(values),
            out_specs=vmem,
            compiler_params=params,
            cost_estimate=pl.CostEstimate(
                flops=10**11, bytes_accessed=10**9, transcendentals=0
            ),
            name="split_blocks",
        )(*values)

    indices = [
        pltpu.SMEM(leaf_rows.shape, leaf_rows.dtype),
        pltpu.SMEM(leaf_counts.shape, leaf_counts.dtype),
        pltpu.SemaphoreType.DMA((2,)),
    ]
    rows_shape = jax.ShapeDtypeStruct((2, row_dev, columns), F32)
    high, low, early = pl.pallas_call(
        functools.partial(early_kernel, n_col, panel_rows, chips),
        out_shape=[jax.ShapeDtypeStruct((2, depth, columns), BF16)] * 2 + [rows_shape],
        in_specs=[hbm, hbm] + [vmem] * 6,
        out_specs=[vmem] * 3,
        scratch_shapes=indices,
        compiler_params=params,
        name="early_rows",
    )(leaf_rows, leaf_counts, split_blocks(early_blocks), panel, mine_high, mine_low, mate, mates)
    early, late_blocks = lax.optimization_barrier((early, late_blocks))

    piece = jax.ShapeDtypeStruct((leaves, 2, chip_share, row_dev), F32)
    selected, *sent = pl.pallas_call(
        select_kernel,
        out_shape=[rows_shape] + [piece] * chips,
        in_specs=[hbm, hbm] + [vmem] * 4,
        out_specs=[vmem] * (1 + chips),
        scratch_shapes=[pltpu.VMEM((chips,) + piece.shape, F32)] + indices,
        compiler_params=params,
        name="selected_rows",
    )(leaf_rows, leaf_counts, split_blocks(late_blocks), early, high, low)

    for step in range(chips - 1, 0, -1):
        perm = [(i, i ^ (2 * step)) for i in range(n_row)]
        sent[step] = lax.ppermute(sent[step], "row", perm)
    selected = pl.pallas_call(
        write_kernel,
        out_shape=jax.ShapeDtypeStruct(selected.shape, F32),
        in_specs=[vmem],
        out_specs=vmem,
        compiler_params=params,
        name="write_rows",
    )(selected)
    selected, sent = lax.optimization_barrier((selected, sent[::-1]))

    keep, give = pl.pallas_call(
        diagonal_kernel,
        out_shape=[jax.ShapeDtypeStruct(diag_inverse.shape, F32)] * 2,
        in_specs=[hbm] + [vmem] * (chips + 3),
        out_specs=[vmem] * 2,
        scratch_shapes=[
            pltpu.VMEM((chips, leaves, 4 * chip_share, row_dev), BF16),
            pltpu.VMEM((2, chip_share, columns), F32),
            pltpu.SMEM(leaf_rows.shape, leaf_rows.dtype),
            pltpu.SemaphoreType.DMA,
        ],
        compiler_params=params,
        cost_estimate=pl.CostEstimate(
            flops=12 * chip_share * depth * columns,
            bytes_accessed=8 * (depth + 2 * chip_share) * columns,
            transcendentals=0,
        ),
        name="diagonal_part",
    )(leaf_rows, *sent, high, low, diag_inverse)
    give = lax.ppermute(give, "row", [(i, i ^ 1) for i in range(n_row)])
    diagonal = pl.pallas_call(
        subtract_kernel,
        out_shape=jax.ShapeDtypeStruct(diag_inverse.shape, F32),
        in_specs=[vmem] * 2,
        out_specs=vmem,
        compiler_params=params,
        name="diagonal_rows",
    )(keep, give)
    return selected, diagonal


def solution(mesh):
    return jax.shard_map(
        functools.partial(on_device, mesh.shape["row"], mesh.shape["col"]),
        mesh=mesh,
        in_specs=(
            P(None, "row", "col"),
            P(None, "row", "col"),
            P("col", None),
            P("col"),
            P(None, "row", "col"),
        ),
        out_specs=(P(None, "row", "col"), P(None, "row", "col")),
        check_vma=False,
    )
```

```python
import functools

import jax
import jax.numpy as jnp
from jax import lax
from jax.experimental import pallas as pl
from jax.experimental.pallas import tpu as pltpu
from jax.sharding import PartitionSpec as P

B = 256
F32 = jnp.float32
BF16 = jnp.bfloat16


def split(value):
    high = value.astype(BF16)
    low = (value - high.astype(F32)).astype(BF16)
    return high, low


def dot(left, right):
    return jnp.dot(left, right, preferred_element_type=F32)


def line_gather(own, axis, n, cut):
    blocks = {0: own}
    for step in line_steps(n):
        perm = [(i, i ^ step) for i in range(n)]
        if step > 1:
            blocks |= {k ^ step: lax.ppermute(block, axis, perm) for k, block in blocks.items()}
    halves = {k ^ 1: cut(block) for k, block in blocks.items() if k > 0}
    halves = {k: [lax.ppermute(half, axis, perm) for half in pair] for k, pair in halves.items()}
    blocks[1] = lax.ppermute(own, axis, perm)
    return blocks, halves


def line_steps(n):
    steps = []
    while n > 1:
        n //= 2
        steps.append(n)
    return steps


def cut_kernel(block_ref, *out_refs):
    size = block_ref.shape[1] // len(out_refs)
    for half, out_ref in enumerate(out_refs):
        out_ref[...] = block_ref[:, half * size : (half + 1) * size, :]


def pack_kernel(*refs):
    (rows_ref, counts_ref), pieces = refs[:2], refs[2:-5]
    out_ref, high_ref, low_ref, rows_out, counts_out = refs[-5:]
    rows_out[...] = rows_ref[...]
    counts_out[...] = counts_ref[...]
    share_rows = pieces[0].shape[1]
    for place, piece in enumerate(pieces):
        here = slice(place * share_rows, (place + 1) * share_rows)
        out_ref[:, here, :] = piece[...]
        for part in range(2):
            high_ref[part, here, :], low_ref[part, here, :] = split(piece[part])


def add_slot(total, left, high_ref, low_ref, rows, cols):
    real, imag = total
    size = real.shape[0]
    both = left[0 : 2 * size]
    left = jnp.concatenate([both, left[2 * size : 4 * size], both], axis=1)

    def panel(part):
        high, low = high_ref[part, rows, cols], low_ref[part, rows, cols]
        return jnp.concatenate([high, high, low], axis=0)

    with_real, with_imag = dot(left, panel(0)), dot(left, panel(1))
    real = real - (with_real[:size] - with_imag[size:])
    imag = imag - (with_imag[:size] + with_real[size:])
    return real, imag


def row_is_live(rows_ref, counts_ref, member, block):
    return lax.fori_loop(
        0,
        counts_ref[0, member],
        lambda q, seen: seen | (rows_ref[member, q] == block),
        False,
    )


def blocks_kernel(*refs):
    pieces, out_ref = refs[:-1], refs[-1]
    rows = out_ref.shape[1] // 4
    for k, piece in enumerate(pieces):
        size = piece.shape[1]
        place, first = k * size // rows, k * size % rows
        for part in range(2):
            for scale, value in enumerate(split(piece[part])):
                start = (2 * scale + part) * rows + first
                out_ref[place, start : start + size, :] = value


def add_slots(member, top, places, rows_ref, counts_ref, high_ref, low_ref, out_ref):
    row_dev = out_ref.shape[1]
    my_block = (lax.axis_index("row") * row_dev) // B
    my_col = lax.axis_index("col")
    cols = slice(member * B, (member + 1) * B)
    live = row_is_live(rows_ref, counts_ref, member, my_block)

    def slot(q, carry):
        held, place = places(my_col ^ rows_ref[member, q])

        @pl.when(held)
        def _():
            rows = pl.ds(pl.multiple_of(q * B, B), B)
            total = out_ref[0, :, cols], out_ref[1, :, cols]
            total = add_slot(total, top[place], high_ref, low_ref, rows, cols)
            out_ref[0, :, cols], out_ref[1, :, cols] = total

        return carry

    lax.fori_loop(0, jnp.where(live, counts_ref[0, member], 0), slot, 0)


def early_place(n_col, distance):
    return (distance % 2 == 0) | (distance == 1), jnp.where(distance == 1, n_col // 2, distance // 2)


def late_place(distance):
    return (distance % 2 == 1) & (distance > 1), (distance - 3) // 2


def fetch(sems, *pairs):
    copies = [pltpu.make_async_copy(*pair, sems.at[k]) for k, pair in enumerate(pairs)]
    for copy in copies:
        copy.start()
    return copies


def turn(member, out_ref, sent, turned):
    chips, _, share, row_dev = turned.shape
    cols = slice(member * B, (member + 1) * B)
    for part in range(2):
        turned[:, part] = out_ref[part, :, cols].T.reshape(chips, share, row_dev)
    for step in range(chips):
        sent[step][member] = turned[(lax.axis_index("row") // 2) ^ step]


def early_kernel(n_col, share_rows, chips, *refs):
    rows_hbm, counts_hbm, top, own, mine_high, mine_low, mate, mates = refs[:8]
    high_ref, low_ref, out_ref = refs[8:11]
    sent, (turned, rows_ref, counts_ref, sems) = refs[11:-4], refs[-4:]
    me = lax.axis_index("row")
    arrivals = fetch(sems, (rows_hbm, rows_ref), (counts_hbm, counts_ref))

    def put(owner, high, low):
        rows = pl.ds(pl.multiple_of(owner * share_rows, share_rows), share_rows)
        high_ref[:, rows, :], low_ref[:, rows, :] = high, low

    put(me, *split(own[...]))
    put(me ^ 1, *split(mate[...]))
    for step in range(1, chips):
        here = slice((step - 1) * share_rows, step * share_rows)
        put(me ^ (2 * step), mine_high[:, here, :], mine_low[:, here, :])
        put(me ^ (2 * step) ^ 1, *split(mates[:, here, :]))
    out_ref[...] = jnp.zeros(out_ref.shape, F32)
    for copy in arrivals:
        copy.wait()
    places = functools.partial(early_place, n_col)
    for member in range(rows_ref.shape[0]):
        add_slots(member, top, places, rows_ref, counts_ref, high_ref, low_ref, out_ref)
        turn(member, out_ref, sent, turned)


def select_kernel(chips, *refs):
    rows_hbm, counts_hbm, top, high_ref, low_ref, early_ref = refs[:6]
    early_sent, out_ref, sent = refs[6 : 6 + chips], refs[6 + chips], refs[7 + chips : -4]
    turned, rows_ref, counts_ref, sems = refs[-4:]
    row_dev = out_ref.shape[1]
    my_block = (lax.axis_index("row") * row_dev) // B
    my_col = lax.axis_index("col")
    arrivals = fetch(sems, (rows_hbm, rows_ref), (counts_hbm, counts_ref))
    out_ref[...] = early_ref[...]
    for step in range(chips):
        sent[step][...] = early_sent[step][...]
    for copy in arrivals:
        copy.wait()
    for member in range(rows_ref.shape[0]):
        any_late = lax.fori_loop(
            0,
            counts_ref[0, member],
            lambda q, seen: seen | late_place(my_col ^ rows_ref[member, q])[0],
            False,
        )

        @pl.when(any_late & row_is_live(rows_ref, counts_ref, member, my_block))
        def _():
            add_slots(member, top, late_place, rows_ref, counts_ref, high_ref, low_ref, out_ref)
            turn(member, out_ref, sent, turned)


def write_kernel(value_ref, out_ref):
    out_ref[...] = value_ref[...]


def diagonal_kernel(rows_hbm, *refs):
    pieces, (high_ref, low_ref, diag_ref, keep_ref, give_ref) = refs[:-9], refs[-9:-4]
    turned, whole, rows_ref, sem = refs[-4:]
    arrival = pltpu.make_async_copy(rows_hbm, rows_ref, sem)
    arrival.start()
    leaves, slots = rows_ref.shape
    _, _, chip_share, row_dev = pieces[0].shape
    share = keep_ref.shape[1]
    me = lax.axis_index("row")
    core = me % 2
    for step, piece in enumerate(reversed(pieces)):
        source = (me // 2) ^ step
        high, low = split(piece[...].reshape(leaves, 2 * chip_share, row_dev))
        turned[source, :, 0 : 2 * chip_share] = high
        turned[source, :, 2 * chip_share : 4 * chip_share] = low
    arrival.wait()
    for member in range(leaves):
        cols = slice(member * B, (member + 1) * B)
        left = jnp.concatenate([turned[rows_ref[member, q], member] for q in range(slots)], axis=1)
        both = left[: 2 * chip_share]

        def panel(ref, part):
            starts = [pl.multiple_of(q * B + core * row_dev, row_dev) for q in range(slots)]
            return jnp.concatenate(
                [ref[part, pl.ds(start, row_dev), cols] for start in starts], axis=0
            )

        with_real = dot(left, panel(high_ref, 0))
        with_imag = dot(left, panel(high_ref, 1))
        with_real = with_real[: 2 * chip_share] + with_real[2 * chip_share :]
        with_imag = with_imag[: 2 * chip_share] + with_imag[2 * chip_share :]
        with_real += dot(both, panel(low_ref, 0))
        with_imag += dot(both, panel(low_ref, 1))
        whole[0, :, cols] = with_real[:chip_share] - with_imag[chip_share:]
        whole[1, :, cols] = with_imag[:chip_share] + with_real[chip_share:]
    mine = pl.ds(pl.multiple_of(core * share, share), share)
    other = pl.ds(pl.multiple_of((1 - core) * share, share), share)
    keep_ref[...] = diag_ref[...] - whole[:, mine, :]
    give_ref[...] = whole[:, other, :]


def subtract_kernel(left_ref, right_ref, out_ref):
    out_ref[...] = left_ref[...] - right_ref[...]


def on_device(n_row, n_col, top_inverse, panel, leaf_rows, leaf_counts, diag_inverse):
    vmem = pl.BlockSpec(memory_space=pltpu.VMEM)
    hbm = pl.BlockSpec(memory_space=pl.ANY)
    _, row_dev, _ = top_inverse.shape
    _, panel_rows, columns = panel.shape
    leaves = columns // B
    chips = n_row // 2
    chip_share = B // chips
    depth = n_row * panel_rows
    params = pltpu.CompilerParams(vmem_limit_bytes=max(16 << 20, 40 * depth * columns))

    def cut(block):
        half = jax.ShapeDtypeStruct((2, row_dev // 2, B), F32)
        return pl.pallas_call(
            cut_kernel,
            out_shape=[half, half],
            in_specs=[vmem],
            out_specs=[vmem] * 2,
            compiler_params=params,
            name="cut_rows",
        )(block)

    blocks, halves = line_gather(top_inverse, "col", n_col, cut)

    swap = [(i, i ^ 1) for i in range(n_row)]
    like = [
        lax.ppermute(panel, "row", [(i, i ^ step) for i in range(n_row)])
        for step in range(2, n_row, 2)
    ]
    like = lax.optimization_barrier((like, blocks))[0]
    packed = (2, depth // 2 - panel_rows, columns)
    leaf_counts = leaf_counts[None, :]
    mine, mine_high, mine_low, leaf_rows, leaf_counts = pl.pallas_call(
        pack_kernel,
        out_shape=[jax.ShapeDtypeStruct(packed, dtype) for dtype in (F32, BF16, BF16)]
        + [jax.ShapeDtypeStruct(value.shape, value.dtype) for value in (leaf_rows, leaf_counts)],
        in_specs=[vmem] * (2 + len(like)),
        out_specs=[vmem] * 5,
        compiler_params=params,
        name="pack_panel",
    )(leaf_rows, leaf_counts, *like)
    mate = lax.ppermute(panel, "row", swap)
    mates = lax.ppermute(mine, "row", swap)

    early_blocks = [blocks[k] for k in range(0, n_col, 2)] + [blocks[1]]
    firsts = [halves[k][0] for k in range(3, n_col, 2)]
    early_blocks, firsts = lax.optimization_barrier((early_blocks, firsts))
    late_blocks = [half for k in range(3, n_col, 2) for half in halves[k]]

    def split_blocks(values):
        count = sum(value.shape[1] for value in values) // row_dev
        return pl.pallas_call(
            blocks_kernel,
            out_shape=jax.ShapeDtypeStruct((count, 4 * row_dev, B), BF16),
            in_specs=[vmem] * len(values),
            out_specs=vmem,
            compiler_params=params,
            cost_estimate=pl.CostEstimate(
                flops=10**11, bytes_accessed=10**9, transcendentals=0
            ),
            name="split_blocks",
        )(*values)

    indices = [
        pltpu.SMEM(leaf_rows.shape, leaf_rows.dtype),
        pltpu.SMEM(leaf_counts.shape, leaf_counts.dtype),
        pltpu.SemaphoreType.DMA((2,)),
    ]
    rows_shape = jax.ShapeDtypeStruct((2, row_dev, columns), F32)
    piece = jax.ShapeDtypeStruct((leaves, 2, chip_share, row_dev), F32)
    scratch = [pltpu.VMEM((chips,) + piece.shape[1:], F32)] + indices
    high, low, *early = pl.pallas_call(
        functools.partial(early_kernel, n_col, panel_rows, chips),
        out_shape=[jax.ShapeDtypeStruct((2, depth, columns), BF16)] * 2
        + [rows_shape]
        + [piece] * chips,
        in_specs=[hbm, hbm] + [vmem] * 6,
        out_specs=[vmem] * (3 + chips),
        scratch_shapes=scratch,
        compiler_params=params,
        name="early_rows",
    )(leaf_rows, leaf_counts, split_blocks(early_blocks), panel, mine_high, mine_low, mate, mates)
    early, late_blocks = lax.optimization_barrier((early, late_blocks))

    selected, *sent = pl.pallas_call(
        functools.partial(select_kernel, chips),
        out_shape=[rows_shape] + [piece] * chips,
        in_specs=[hbm, hbm] + [vmem] * (4 + chips),
        out_specs=[vmem] * (1 + chips),
        scratch_shapes=scratch,
        compiler_params=params,
        name="selected_rows",
    )(leaf_rows, leaf_counts, split_blocks(late_blocks), high, low, *early)

    for step in range(chips - 1, 0, -1):
        perm = [(i, i ^ (2 * step)) for i in range(n_row)]
        sent[step] = lax.ppermute(sent[step], "row", perm)
    selected = pl.pallas_call(
        write_kernel,
        out_shape=jax.ShapeDtypeStruct(selected.shape, F32),
        in_specs=[vmem],
        out_specs=vmem,
        compiler_params=params,
        name="write_rows",
    )(selected)
    selected, sent = lax.optimization_barrier((selected, sent[::-1]))

    keep, give = pl.pallas_call(
        diagonal_kernel,
        out_shape=[jax.ShapeDtypeStruct(diag_inverse.shape, F32)] * 2,
        in_specs=[hbm] + [vmem] * (chips + 3),
        out_specs=[vmem] * 2,
        scratch_shapes=[
            pltpu.VMEM((chips, leaves, 4 * chip_share, row_dev), BF16),
            pltpu.VMEM((2, chip_share, columns), F32),
            pltpu.SMEM(leaf_rows.shape, leaf_rows.dtype),
            pltpu.SemaphoreType.DMA,
        ],
        compiler_params=params,
        cost_estimate=pl.CostEstimate(
            flops=12 * chip_share * depth * columns,
            bytes_accessed=8 * (depth + 2 * chip_share) * columns,
            transcendentals=0,
        ),
        name="diagonal_part",
    )(leaf_rows, *sent, high, low, diag_inverse)
    give = lax.ppermute(give, "row", [(i, i ^ 1) for i in range(n_row)])
    diagonal = pl.pallas_call(
        subtract_kernel,
        out_shape=jax.ShapeDtypeStruct(diag_inverse.shape, F32),
        in_specs=[vmem] * 2,
        out_specs=vmem,
        compiler_params=params,
        name="diagonal_rows",
    )(keep, give)
    return selected, diagonal


def solution(mesh):
    return jax.shard_map(
        functools.partial(on_device, mesh.shape["row"], mesh.shape["col"]),
        mesh=mesh,
        in_specs=(
            P(None, "row", "col"),
            P(None, "row", "col"),
            P("col", None),
            P("col"),
            P(None, "row", "col"),
        ),
        out_specs=(P(None, "row", "col"), P(None, "row", "col")),
        check_vma=False,
    )
```

```python
import functools

import jax
import jax.numpy as jnp
from jax import lax
from jax.experimental import pallas as pl
from jax.experimental.pallas import tpu as pltpu
from jax.sharding import PartitionSpec as P

B = 256
F32 = jnp.float32
BF16 = jnp.bfloat16


def split(value):
    high = value.astype(BF16)
    low = (value - high.astype(F32)).astype(BF16)
    return high, low


def dot(left, right):
    return jnp.dot(left, right, preferred_element_type=F32)


def strip_gather(own, n_row, n_col):
    def swap(block, *distances):
        pairs = []
        for i in range(n_row):
            if distances[i % 2]:
                pairs += [(i * n_col + j, i * n_col + (j ^ distances[i % 2])) for j in range(n_col)]
        return lax.ppermute(block, ("row", "col"), pairs)

    blocks, step = {0: own}, n_col // 2
    while step > 2:
        blocks |= {k ^ step: swap(block, step, step) for k, block in blocks.items()}
        step //= 2
    groups = []
    for k in sorted(blocks):
        first, second = swap(blocks[k], 2, 1), swap(blocks[k], 1, 2)
        groups.append(([blocks[k], first, second], [swap(first, 1, 0), swap(second, 0, 1)]))
    return groups


def pack_kernel(*refs):
    (rows_ref, counts_ref), pieces = refs[:2], refs[2:-5]
    out_ref, high_ref, low_ref, rows_out, counts_out = refs[-5:]
    rows_out[...] = rows_ref[...]
    counts_out[...] = counts_ref[...]
    share_rows = pieces[0].shape[1]
    for place, piece in enumerate(pieces):
        here = slice(place * share_rows, (place + 1) * share_rows)
        out_ref[:, here, :] = piece[...]
        for part in range(2):
            high_ref[part, here, :], low_ref[part, here, :] = split(piece[part])


def add_slot(total, left, high_ref, low_ref, rows, cols):
    real, imag = total
    size = real.shape[0]
    both = left[0 : 2 * size]
    left = jnp.concatenate([both, left[2 * size : 4 * size], both], axis=1)

    def panel(part):
        high, low = high_ref[part, rows, cols], low_ref[part, rows, cols]
        return jnp.concatenate([high, high, low], axis=0)

    with_real, with_imag = dot(left, panel(0)), dot(left, panel(1))
    real = real - (with_real[:size] - with_imag[size:])
    imag = imag - (with_imag[:size] + with_real[size:])
    return real, imag


def row_is_live(rows_ref, counts_ref, member, block):
    return lax.fori_loop(
        0,
        counts_ref[0, member],
        lambda q, seen: seen | (rows_ref[member, q] == block),
        False,
    )


def put_block(out_ref, place, value):
    both = 2 * value.shape[1]
    out_ref[place, 0:both, :], out_ref[place, both : 2 * both, :] = split(value.reshape(both, B))


def early_blocks_kernel(*refs):
    blocks, out_ref = refs[:-1], refs[-1]
    core = lax.axis_index("row") % 2
    for k in range(0, len(blocks), 3):
        put_block(out_ref, k, blocks[k][...])
        put_block(out_ref, k + 2 - core, blocks[k + 1][...])
        put_block(out_ref, k + 1 + core, blocks[k + 2][...])


def late_blocks_kernel(*refs):
    blocks, out_ref = refs[:-1], refs[-1]
    core = lax.axis_index("row") % 2
    for k in range(0, len(blocks), 2):
        put_block(out_ref, k // 2, jnp.where(core == 0, blocks[k][...], blocks[k + 1][...]))


def add_slots(member, top, places, rows_ref, counts_ref, high_ref, low_ref, out_ref):
    row_dev = out_ref.shape[1]
    my_block = (lax.axis_index("row") * row_dev) // B
    my_col = lax.axis_index("col")
    cols = slice(member * B, (member + 1) * B)
    live = row_is_live(rows_ref, counts_ref, member, my_block)

    def slot(q, carry):
        held, place = places(my_col ^ rows_ref[member, q])

        @pl.when(held)
        def _():
            rows = pl.ds(pl.multiple_of(q * B, B), B)
            total = out_ref[0, :, cols], out_ref[1, :, cols]
            total = add_slot(total, top[place], high_ref, low_ref, rows, cols)
            out_ref[0, :, cols], out_ref[1, :, cols] = total

        return carry

    lax.fori_loop(0, jnp.where(live, counts_ref[0, member], 0), slot, 0)


def early_place(distance):
    return distance % 4 < 3, distance // 4 * 3 + distance % 4


def late_place(distance):
    return distance % 4 == 3, distance // 4


def fetch(sems, *pairs):
    copies = [pltpu.make_async_copy(*pair, sems.at[k]) for k, pair in enumerate(pairs)]
    for copy in copies:
        copy.start()
    return copies


def turn(member, out_ref, sent, turned):
    chips, _, share, row_dev = turned.shape
    cols = slice(member * B, (member + 1) * B)
    for part in range(2):
        turned[:, part] = out_ref[part, :, cols].T.reshape(chips, share, row_dev)
    for step in range(chips):
        sent[step][member] = turned[(lax.axis_index("row") // 2) ^ step]


def early_kernel(share_rows, chips, *refs):
    rows_hbm, counts_hbm, top, own, mine_high, mine_low, mate, mates = refs[:8]
    high_ref, low_ref, out_ref = refs[8:11]
    sent, (turned, rows_ref, counts_ref, sems) = refs[11:-4], refs[-4:]
    me = lax.axis_index("row")
    arrivals = fetch(sems, (rows_hbm, rows_ref), (counts_hbm, counts_ref))

    def put(owner, high, low):
        rows = pl.ds(pl.multiple_of(owner * share_rows, share_rows), share_rows)
        high_ref[:, rows, :], low_ref[:, rows, :] = high, low

    put(me, *split(own[...]))
    put(me ^ 1, *split(mate[...]))
    for step in range(1, chips):
        here = slice((step - 1) * share_rows, step * share_rows)
        put(me ^ (2 * step), mine_high[:, here, :], mine_low[:, here, :])
        put(me ^ (2 * step) ^ 1, *split(mates[:, here, :]))
    out_ref[...] = jnp.zeros(out_ref.shape, F32)
    for copy in arrivals:
        copy.wait()
    for member in range(rows_ref.shape[0]):
        add_slots(member, top, early_place, rows_ref, counts_ref, high_ref, low_ref, out_ref)
        turn(member, out_ref, sent, turned)


def select_kernel(chips, *refs):
    rows_hbm, counts_hbm, top, high_ref, low_ref, early_ref = refs[:6]
    early_sent, out_ref, sent = refs[6 : 6 + chips], refs[6 + chips], refs[7 + chips : -4]
    turned, rows_ref, counts_ref, sems = refs[-4:]
    row_dev = out_ref.shape[1]
    my_block = (lax.axis_index("row") * row_dev) // B
    my_col = lax.axis_index("col")
    arrivals = fetch(sems, (rows_hbm, rows_ref), (counts_hbm, counts_ref))
    out_ref[...] = early_ref[...]
    for step in range(chips):
        sent[step][...] = early_sent[step][...]
    for copy in arrivals:
        copy.wait()
    for member in range(rows_ref.shape[0]):
        any_late = lax.fori_loop(
            0,
            counts_ref[0, member],
            lambda q, seen: seen | late_place(my_col ^ rows_ref[member, q])[0],
            False,
        )

        @pl.when(any_late & row_is_live(rows_ref, counts_ref, member, my_block))
        def _():
            add_slots(member, top, late_place, rows_ref, counts_ref, high_ref, low_ref, out_ref)
            turn(member, out_ref, sent, turned)


def write_kernel(value_ref, out_ref):
    out_ref[...] = value_ref[...]


def diagonal_kernel(rows_hbm, *refs):
    pieces, (high_ref, low_ref, diag_ref, keep_ref, give_ref) = refs[:-9], refs[-9:-4]
    turned, whole, rows_ref, sem = refs[-4:]
    arrival = pltpu.make_async_copy(rows_hbm, rows_ref, sem)
    arrival.start()
    leaves, slots = rows_ref.shape
    _, _, chip_share, row_dev = pieces[0].shape
    share = keep_ref.shape[1]
    me = lax.axis_index("row")
    core = me % 2
    for step, piece in enumerate(reversed(pieces)):
        source = (me // 2) ^ step
        high, low = split(piece[...].reshape(leaves, 2 * chip_share, row_dev))
        turned[source, :, 0 : 2 * chip_share] = high
        turned[source, :, 2 * chip_share : 4 * chip_share] = low
    arrival.wait()
    for member in range(leaves):
        cols = slice(member * B, (member + 1) * B)
        left = jnp.concatenate([turned[rows_ref[member, q], member] for q in range(slots)], axis=1)
        both = left[: 2 * chip_share]

        def panel(ref, part):
            starts = [pl.multiple_of(q * B + core * row_dev, row_dev) for q in range(slots)]
            return jnp.concatenate(
                [ref[part, pl.ds(start, row_dev), cols] for start in starts], axis=0
            )

        with_real = dot(left, panel(high_ref, 0))
        with_imag = dot(left, panel(high_ref, 1))
        with_real = with_real[: 2 * chip_share] + with_real[2 * chip_share :]
        with_imag = with_imag[: 2 * chip_share] + with_imag[2 * chip_share :]
        with_real += dot(both, panel(low_ref, 0))
        with_imag += dot(both, panel(low_ref, 1))
        whole[0, :, cols] = with_real[:chip_share] - with_imag[chip_share:]
        whole[1, :, cols] = with_imag[:chip_share] + with_real[chip_share:]
    mine = pl.ds(pl.multiple_of(core * share, share), share)
    other = pl.ds(pl.multiple_of((1 - core) * share, share), share)
    keep_ref[...] = diag_ref[...] - whole[:, mine, :]
    give_ref[...] = whole[:, other, :]


def subtract_kernel(left_ref, right_ref, out_ref):
    out_ref[...] = left_ref[...] - right_ref[...]


def on_device(n_row, n_col, top_inverse, panel, leaf_rows, leaf_counts, diag_inverse):
    vmem = pl.BlockSpec(memory_space=pltpu.VMEM)
    hbm = pl.BlockSpec(memory_space=pl.ANY)
    _, row_dev, _ = top_inverse.shape
    _, panel_rows, columns = panel.shape
    leaves = columns // B
    chips = n_row // 2
    chip_share = B // chips
    depth = n_row * panel_rows
    params = pltpu.CompilerParams(vmem_limit_bytes=max(16 << 20, 40 * depth * columns))

    groups = strip_gather(top_inverse, n_row, n_col)

    swap = [(i, i ^ 1) for i in range(n_row)]
    like = [
        lax.ppermute(panel, "row", [(i, i ^ step) for i in range(n_row)])
        for step in range(2, n_row, 2)
    ]
    packed = (2, depth // 2 - panel_rows, columns)
    leaf_counts = leaf_counts[None, :]
    mine, mine_high, mine_low, leaf_rows, leaf_counts = pl.pallas_call(
        pack_kernel,
        out_shape=[jax.ShapeDtypeStruct(packed, dtype) for dtype in (F32, BF16, BF16)]
        + [jax.ShapeDtypeStruct(value.shape, value.dtype) for value in (leaf_rows, leaf_counts)],
        in_specs=[vmem] * (2 + len(like)),
        out_specs=[vmem] * 5,
        compiler_params=params,
        name="pack_panel",
    )(leaf_rows, leaf_counts, *like)
    mate = lax.ppermute(panel, "row", swap)
    mates = lax.ppermute(mine, "row", swap)

    early_blocks = [block for early, _ in groups for block in early]
    late_blocks = [block for _, late in groups for block in late]
    early_blocks, _ = lax.optimization_barrier((early_blocks, late_blocks[::2]))

    def split_blocks(kernel, values, count):
        return pl.pallas_call(
            kernel,
            out_shape=jax.ShapeDtypeStruct((count, 4 * row_dev, B), BF16),
            in_specs=[vmem] * len(values),
            out_specs=vmem,
            compiler_params=params,
            cost_estimate=pl.CostEstimate(
                flops=10**11, bytes_accessed=10**9, transcendentals=0
            ),
            name="split_blocks",
        )(*values)

    top = split_blocks(early_blocks_kernel, early_blocks, len(early_blocks))
    indices = [
        pltpu.SMEM(leaf_rows.shape, leaf_rows.dtype),
        pltpu.SMEM(leaf_counts.shape, leaf_counts.dtype),
        pltpu.SemaphoreType.DMA((2,)),
    ]
    rows_shape = jax.ShapeDtypeStruct((2, row_dev, columns), F32)
    piece = jax.ShapeDtypeStruct((leaves, 2, chip_share, row_dev), F32)
    scratch = [pltpu.VMEM((chips,) + piece.shape[1:], F32)] + indices
    high, low, *early = pl.pallas_call(
        functools.partial(early_kernel, panel_rows, chips),
        out_shape=[jax.ShapeDtypeStruct((2, depth, columns), BF16)] * 2
        + [rows_shape]
        + [piece] * chips,
        in_specs=[hbm, hbm] + [vmem] * 6,
        out_specs=[vmem] * (3 + chips),
        scratch_shapes=scratch,
        compiler_params=params,
        name="early_rows",
    )(leaf_rows, leaf_counts, top, panel, mine_high, mine_low, mate, mates)
    early, late_blocks = lax.optimization_barrier((early, late_blocks))
    top = split_blocks(late_blocks_kernel, late_blocks, len(groups))

    selected, *sent = pl.pallas_call(
        functools.partial(select_kernel, chips),
        out_shape=[rows_shape] + [piece] * chips,
        in_specs=[hbm, hbm] + [vmem] * (4 + chips),
        out_specs=[vmem] * (1 + chips),
        scratch_shapes=scratch,
        compiler_params=params,
        name="selected_rows",
    )(leaf_rows, leaf_counts, top, high, low, *early)

    for step in range(chips - 1, 0, -1):
        perm = [(i, i ^ (2 * step)) for i in range(n_row)]
        sent[step] = lax.ppermute(sent[step], "row", perm)
    selected = pl.pallas_call(
        write_kernel,
        out_shape=jax.ShapeDtypeStruct(selected.shape, F32),
        in_specs=[vmem],
        out_specs=vmem,
        compiler_params=params,
        name="write_rows",
    )(selected)
    selected, sent = lax.optimization_barrier((selected, sent[::-1]))

    keep, give = pl.pallas_call(
        diagonal_kernel,
        out_shape=[jax.ShapeDtypeStruct(diag_inverse.shape, F32)] * 2,
        in_specs=[hbm] + [vmem] * (chips + 3),
        out_specs=[vmem] * 2,
        scratch_shapes=[
            pltpu.VMEM((chips, leaves, 4 * chip_share, row_dev), BF16),
            pltpu.VMEM((2, chip_share, columns), F32),
            pltpu.SMEM(leaf_rows.shape, leaf_rows.dtype),
            pltpu.SemaphoreType.DMA,
        ],
        compiler_params=params,
        cost_estimate=pl.CostEstimate(
            flops=12 * chip_share * depth * columns,
            bytes_accessed=8 * (depth + 2 * chip_share) * columns,
            transcendentals=0,
        ),
        name="diagonal_part",
    )(leaf_rows, *sent, high, low, diag_inverse)
    give = lax.ppermute(give, "row", [(i, i ^ 1) for i in range(n_row)])
    diagonal = pl.pallas_call(
        subtract_kernel,
        out_shape=jax.ShapeDtypeStruct(diag_inverse.shape, F32),
        in_specs=[vmem] * 2,
        out_specs=vmem,
        compiler_params=params,
        name="diagonal_rows",
    )(keep, give)
    return selected, diagonal


def solution(mesh):
    return jax.shard_map(
        functools.partial(on_device, mesh.shape["row"], mesh.shape["col"]),
        mesh=mesh,
        in_specs=(
            P(None, "row", "col"),
            P(None, "row", "col"),
            P("col", None),
            P("col"),
            P(None, "row", "col"),
        ),
        out_specs=(P(None, "row", "col"), P(None, "row", "col")),
        check_vma=False,
    )
```

```python
import functools

import jax
import jax.numpy as jnp
from jax import lax
from jax.experimental import pallas as pl
from jax.experimental.pallas import tpu as pltpu
from jax.sharding import PartitionSpec as P

B = 256
F32 = jnp.float32
BF16 = jnp.bfloat16


def split(value):
    high = value.astype(BF16)
    low = (value - high.astype(F32)).astype(BF16)
    return high, low


def dot(left, right):
    return jnp.dot(left, right, preferred_element_type=F32)


def line_gather(own, axis, n, cut):
    blocks = {0: own}
    for step in line_steps(n):
        perm = [(i, i ^ step) for i in range(n)]
        if step > 1:
            blocks |= {k ^ step: lax.ppermute(block, axis, perm) for k, block in blocks.items()}
    halves = {k ^ 1: cut(block) for k, block in blocks.items() if k > 0}
    halves = {k: [lax.ppermute(half, axis, perm) for half in pair] for k, pair in halves.items()}
    blocks[1] = lax.ppermute(own, axis, perm)
    return blocks, halves


def line_steps(n):
    steps = []
    while n > 1:
        n //= 2
        steps.append(n)
    return steps


def cut_kernel(block_ref, *out_refs):
    size = block_ref.shape[1] // len(out_refs)
    for half, out_ref in enumerate(out_refs):
        out_ref[...] = block_ref[:, half * size : (half + 1) * size, :]


def pack_kernel(*refs):
    (rows_ref, counts_ref), pieces = refs[:2], refs[2:-5]
    out_ref, high_ref, low_ref, rows_out, counts_out = refs[-5:]
    rows_out[...] = rows_ref[...]
    counts_out[...] = counts_ref[...]
    share_rows = pieces[0].shape[1]
    for place, piece in enumerate(pieces):
        here = slice(place * share_rows, (place + 1) * share_rows)
        out_ref[:, here, :] = piece[...]
        for part in range(2):
            high_ref[part, here, :], low_ref[part, here, :] = split(piece[part])


def add_slot(total, left, high_ref, low_ref, rows, cols):
    real, imag = total
    size = real.shape[0]
    both = left[0 : 2 * size]
    left = jnp.concatenate([both, left[2 * size : 4 * size], both], axis=1)

    def panel(part):
        high, low = high_ref[part, rows, cols], low_ref[part, rows, cols]
        return jnp.concatenate([high, high, low], axis=0)

    with_real, with_imag = dot(left, panel(0)), dot(left, panel(1))
    real = real - (with_real[:size] - with_imag[size:])
    imag = imag - (with_imag[:size] + with_real[size:])
    return real, imag


def row_is_live(rows_ref, counts_ref, member, block):
    return lax.fori_loop(
        0,
        counts_ref[0, member],
        lambda q, seen: seen | (rows_ref[member, q] == block),
        False,
    )


def blocks_kernel(*refs):
    pieces, out_ref = refs[:-1], refs[-1]
    rows = out_ref.shape[1] // 4
    for k, piece in enumerate(pieces):
        size = piece.shape[1]
        place, first = k * size // rows, k * size % rows
        for part in range(2):
            for scale, value in enumerate(split(piece[part])):
                start = (2 * scale + part) * rows + first
                out_ref[place, start : start + size, :] = value


def add_slots(member, top, places, rows_ref, counts_ref, high_ref, low_ref, out_ref):
    row_dev = out_ref.shape[1]
    my_block = (lax.axis_index("row") * row_dev) // B
    my_col = lax.axis_index("col")
    cols = slice(member * B, (member + 1) * B)
    live = row_is_live(rows_ref, counts_ref, member, my_block)

    def slot(q, carry):
        held, place = places(my_col ^ rows_ref[member, q])

        @pl.when(held)
        def _():
            rows = pl.ds(pl.multiple_of(q * B, B), B)
            total = out_ref[0, :, cols], out_ref[1, :, cols]
            total = add_slot(total, top[place], high_ref, low_ref, rows, cols)
            out_ref[0, :, cols], out_ref[1, :, cols] = total

        return carry

    lax.fori_loop(0, jnp.where(live, counts_ref[0, member], 0), slot, 0)


def early_place(n_col, distance):
    return (distance % 2 == 0) | (distance == 1), jnp.where(distance == 1, n_col // 2, distance // 2)


def late_place(distance):
    return (distance % 2 == 1) & (distance > 1), (distance - 3) // 2


def fetch(sems, *pairs):
    copies = [pltpu.make_async_copy(*pair, sems.at[k]) for k, pair in enumerate(pairs)]
    for copy in copies:
        copy.start()
    return copies


def turn(member, out_ref, sent, turned):
    chips, _, share, row_dev = turned.shape
    cols = slice(member * B, (member + 1) * B)
    for part in range(2):
        turned[:, part] = out_ref[part, :, cols].T.reshape(chips, share, row_dev)
    for step in range(chips):
        sent[step][member] = turned[(lax.axis_index("row") // 2) ^ step]


def early_kernel(n_col, share_rows, near, far, *refs):
    rows_hbm, counts_hbm, top, own, mate, near_high, near_low, near_mates = refs[:8]
    far_panels, refs = refs[8 : 8 + 2 * len(far)], refs[8 + 2 * len(far) :]
    high_ref, low_ref, out_ref = refs[:3]
    sent, (turned, rows_ref, counts_ref, sems) = refs[3:-4], refs[-4:]
    me = lax.axis_index("row")
    arrivals = fetch(sems, (rows_hbm, rows_ref), (counts_hbm, counts_ref))

    def put(owner, high, low):
        rows = pl.ds(pl.multiple_of(owner * share_rows, share_rows), share_rows)
        high_ref[:, rows, :], low_ref[:, rows, :] = high, low

    put(me, *split(own[...]))
    put(me ^ 1, *split(mate[...]))
    for place, step in enumerate(near):
        here = slice(place * share_rows, (place + 1) * share_rows)
        put(me ^ step, near_high[:, here, :], near_low[:, here, :])
        put(me ^ step ^ 1, *split(near_mates[:, here, :]))
    for place, step in enumerate(far):
        put(me ^ step, *split(far_panels[2 * place][...]))
        put(me ^ step ^ 1, *split(far_panels[2 * place + 1][...]))
    out_ref[...] = jnp.zeros(out_ref.shape, F32)
    for copy in arrivals:
        copy.wait()
    places = functools.partial(early_place, n_col)
    for member in range(rows_ref.shape[0]):
        add_slots(member, top, places, rows_ref, counts_ref, high_ref, low_ref, out_ref)
        turn(member, out_ref, sent, turned)


def select_kernel(chips, *refs):
    rows_hbm, counts_hbm, top, high_ref, low_ref, early_ref = refs[:6]
    early_sent, out_ref, sent = refs[6 : 6 + chips], refs[6 + chips], refs[7 + chips : -4]
    turned, rows_ref, counts_ref, sems = refs[-4:]
    row_dev = out_ref.shape[1]
    my_block = (lax.axis_index("row") * row_dev) // B
    my_col = lax.axis_index("col")
    arrivals = fetch(sems, (rows_hbm, rows_ref), (counts_hbm, counts_ref))
    out_ref[...] = early_ref[...]
    for step in range(chips):
        sent[step][...] = early_sent[step][...]
    for copy in arrivals:
        copy.wait()
    for member in range(rows_ref.shape[0]):
        any_late = lax.fori_loop(
            0,
            counts_ref[0, member],
            lambda q, seen: seen | late_place(my_col ^ rows_ref[member, q])[0],
            False,
        )

        @pl.when(any_late & row_is_live(rows_ref, counts_ref, member, my_block))
        def _():
            add_slots(member, top, late_place, rows_ref, counts_ref, high_ref, low_ref, out_ref)
            turn(member, out_ref, sent, turned)


def write_kernel(value_ref, out_ref):
    out_ref[...] = value_ref[...]


def diagonal_kernel(rows_hbm, *refs):
    pieces, (high_ref, low_ref, diag_ref, keep_ref, give_ref) = refs[:-9], refs[-9:-4]
    turned, whole, rows_ref, sem = refs[-4:]
    arrival = pltpu.make_async_copy(rows_hbm, rows_ref, sem)
    arrival.start()
    leaves, slots = rows_ref.shape
    _, _, chip_share, row_dev = pieces[0].shape
    share = keep_ref.shape[1]
    me = lax.axis_index("row")
    core = me % 2
    for step, piece in enumerate(reversed(pieces)):
        source = (me // 2) ^ step
        high, low = split(piece[...].reshape(leaves, 2 * chip_share, row_dev))
        turned[source, :, 0 : 2 * chip_share] = high
        turned[source, :, 2 * chip_share : 4 * chip_share] = low
    arrival.wait()
    for member in range(leaves):
        cols = slice(member * B, (member + 1) * B)
        left = jnp.concatenate([turned[rows_ref[member, q], member] for q in range(slots)], axis=1)
        both = left[: 2 * chip_share]

        def panel(ref, part):
            starts = [pl.multiple_of(q * B + core * row_dev, row_dev) for q in range(slots)]
            return jnp.concatenate(
                [ref[part, pl.ds(start, row_dev), cols] for start in starts], axis=0
            )

        with_real = dot(left, panel(high_ref, 0))
        with_imag = dot(left, panel(high_ref, 1))
        with_real = with_real[: 2 * chip_share] + with_real[2 * chip_share :]
        with_imag = with_imag[: 2 * chip_share] + with_imag[2 * chip_share :]
        with_real += dot(both, panel(low_ref, 0))
        with_imag += dot(both, panel(low_ref, 1))
        whole[0, :, cols] = with_real[:chip_share] - with_imag[chip_share:]
        whole[1, :, cols] = with_imag[:chip_share] + with_real[chip_share:]
    mine = pl.ds(pl.multiple_of(core * share, share), share)
    other = pl.ds(pl.multiple_of((1 - core) * share, share), share)
    keep_ref[...] = diag_ref[...] - whole[:, mine, :]
    give_ref[...] = whole[:, other, :]


def subtract_kernel(left_ref, right_ref, out_ref):
    out_ref[...] = left_ref[...] - right_ref[...]


def on_device(n_row, n_col, top_inverse, panel, leaf_rows, leaf_counts, diag_inverse):
    vmem = pl.BlockSpec(memory_space=pltpu.VMEM)
    hbm = pl.BlockSpec(memory_space=pl.ANY)
    _, row_dev, _ = top_inverse.shape
    _, panel_rows, columns = panel.shape
    leaves = columns // B
    chips = n_row // 2
    chip_share = B // chips
    depth = n_row * panel_rows
    params = pltpu.CompilerParams(vmem_limit_bytes=max(16 << 20, 40 * depth * columns))

    def cut(block):
        half = jax.ShapeDtypeStruct((2, row_dev // 2, B), F32)
        return pl.pallas_call(
            cut_kernel,
            out_shape=[half, half],
            in_specs=[vmem],
            out_specs=[vmem] * 2,
            compiler_params=params,
            name="cut_rows",
        )(block)

    blocks, halves = line_gather(top_inverse, "col", n_col, cut)

    swap = [(i, i ^ 1) for i in range(n_row)]
    like = {
        step: lax.ppermute(panel, "row", [(i, i ^ step) for i in range(n_row)])
        for step in range(2, n_row, 2)
    }
    near = [step for step in like if step & -step == step]
    far = [step for step in like if step not in near]
    packed = (2, len(near) * panel_rows, columns)
    leaf_counts = leaf_counts[None, :]
    mine, near_high, near_low, leaf_rows, leaf_counts = pl.pallas_call(
        pack_kernel,
        out_shape=[jax.ShapeDtypeStruct(packed, dtype) for dtype in (F32, BF16, BF16)]
        + [jax.ShapeDtypeStruct(value.shape, value.dtype) for value in (leaf_rows, leaf_counts)],
        in_specs=[vmem] * (2 + len(near)),
        out_specs=[vmem] * 5,
        compiler_params=params,
        name="pack_panel",
    )(leaf_rows, leaf_counts, *[like[step] for step in near])
    mate = lax.ppermute(panel, "row", swap)
    near_mates = lax.ppermute(mine, "row", swap)
    far_panels = []
    for step in far:
        far_panels += [like[step], lax.ppermute(like[step], "row", swap)]

    early_blocks = [blocks[k] for k in range(0, n_col, 2)] + [blocks[1]]
    firsts = [halves[k][0] for k in range(3, n_col, 2)]
    early_blocks, firsts = lax.optimization_barrier((early_blocks, firsts))
    late_blocks = [half for k in range(3, n_col, 2) for half in halves[k]]

    def split_blocks(values):
        count = sum(value.shape[1] for value in values) // row_dev
        return pl.pallas_call(
            blocks_kernel,
            out_shape=jax.ShapeDtypeStruct((count, 4 * row_dev, B), BF16),
            in_specs=[vmem] * len(values),
            out_specs=vmem,
            compiler_params=params,
            cost_estimate=pl.CostEstimate(
                flops=10**11, bytes_accessed=10**9, transcendentals=0
            ),
            name="split_blocks",
        )(*values)

    indices = [
        pltpu.SMEM(leaf_rows.shape, leaf_rows.dtype),
        pltpu.SMEM(leaf_counts.shape, leaf_counts.dtype),
        pltpu.SemaphoreType.DMA((2,)),
    ]
    rows_shape = jax.ShapeDtypeStruct((2, row_dev, columns), F32)
    piece = jax.ShapeDtypeStruct((leaves, 2, chip_share, row_dev), F32)
    scratch = [pltpu.VMEM((chips,) + piece.shape[1:], F32)] + indices
    high, low, *early = pl.pallas_call(
        functools.partial(early_kernel, n_col, panel_rows, near, far),
        out_shape=[jax.ShapeDtypeStruct((2, depth, columns), BF16)] * 2
        + [rows_shape]
        + [piece] * chips,
        in_specs=[hbm, hbm] + [vmem] * (6 + len(far_panels)),
        out_specs=[vmem] * (3 + chips),
        scratch_shapes=scratch,
        compiler_params=params,
        name="early_rows",
    )(
        leaf_rows,
        leaf_counts,
        split_blocks(early_blocks),
        panel,
        mate,
        near_high,
        near_low,
        near_mates,
        *far_panels,
    )
    early, late_blocks = lax.optimization_barrier((early, late_blocks))

    selected, *sent = pl.pallas_call(
        functools.partial(select_kernel, chips),
        out_shape=[rows_shape] + [piece] * chips,
        in_specs=[hbm, hbm] + [vmem] * (4 + chips),
        out_specs=[vmem] * (1 + chips),
        scratch_shapes=scratch,
        compiler_params=params,
        name="selected_rows",
    )(leaf_rows, leaf_counts, split_blocks(late_blocks), high, low, *early)

    for step in range(chips - 1, 0, -1):
        perm = [(i, i ^ (2 * step)) for i in range(n_row)]
        sent[step] = lax.ppermute(sent[step], "row", perm)
    selected = pl.pallas_call(
        write_kernel,
        out_shape=jax.ShapeDtypeStruct(selected.shape, F32),
        in_specs=[vmem],
        out_specs=vmem,
        compiler_params=params,
        name="write_rows",
    )(selected)
    selected, sent = lax.optimization_barrier((selected, sent[::-1]))

    keep, give = pl.pallas_call(
        diagonal_kernel,
        out_shape=[jax.ShapeDtypeStruct(diag_inverse.shape, F32)] * 2,
        in_specs=[hbm] + [vmem] * (chips + 3),
        out_specs=[vmem] * 2,
        scratch_shapes=[
            pltpu.VMEM((chips, leaves, 4 * chip_share, row_dev), BF16),
            pltpu.VMEM((2, chip_share, columns), F32),
            pltpu.SMEM(leaf_rows.shape, leaf_rows.dtype),
            pltpu.SemaphoreType.DMA,
        ],
        compiler_params=params,
        cost_estimate=pl.CostEstimate(
            flops=12 * chip_share * depth * columns,
            bytes_accessed=8 * (depth + 2 * chip_share) * columns,
            transcendentals=0,
        ),
        name="diagonal_part",
    )(leaf_rows, *sent, high, low, diag_inverse)
    give = lax.ppermute(give, "row", [(i, i ^ 1) for i in range(n_row)])
    diagonal = pl.pallas_call(
        subtract_kernel,
        out_shape=jax.ShapeDtypeStruct(diag_inverse.shape, F32),
        in_specs=[vmem] * 2,
        out_specs=vmem,
        compiler_params=params,
        name="diagonal_rows",
    )(keep, give)
    return selected, diagonal


def solution(mesh):
    return jax.shard_map(
        functools.partial(on_device, mesh.shape["row"], mesh.shape["col"]),
        mesh=mesh,
        in_specs=(
            P(None, "row", "col"),
            P(None, "row", "col"),
            P("col", None),
            P("col"),
            P(None, "row", "col"),
        ),
        out_specs=(P(None, "row", "col"), P(None, "row", "col")),
        check_vma=False,
    )
```

```python
import functools

import jax
import jax.numpy as jnp
from jax import lax
from jax.experimental import pallas as pl
from jax.experimental.pallas import tpu as pltpu
from jax.sharding import PartitionSpec as P

B = 256
F32 = jnp.float32
BF16 = jnp.bfloat16


def split(value):
    high = value.astype(BF16)
    low = (value - high.astype(F32)).astype(BF16)
    return high, low


def dot(left, right):
    return jnp.dot(left, right, preferred_element_type=F32)


def line_gather(own, axis, n, cut):
    blocks = {0: own}
    for step in line_steps(n):
        perm = [(i, i ^ step) for i in range(n)]
        if step > 1:
            blocks |= {k ^ step: lax.ppermute(block, axis, perm) for k, block in blocks.items()}
    halves = {k ^ 1: cut(block) for k, block in blocks.items() if k > 0}
    halves = {k: [lax.ppermute(half, axis, perm) for half in pair] for k, pair in halves.items()}
    blocks[1] = lax.ppermute(own, axis, perm)
    return blocks, halves


def line_steps(n):
    steps = []
    while n > 1:
        n //= 2
        steps.append(n)
    return steps


def cut_kernel(block_ref, first_ref, second_ref):
    size = first_ref.shape[1]
    first_ref[...] = block_ref[:, :size, :]
    second_ref[...] = block_ref[:, size:, :]


def pack_kernel(*refs):
    (rows_ref, counts_ref), pieces = refs[:2], refs[2:-5]
    out_ref, high_ref, low_ref, rows_out, counts_out = refs[-5:]
    rows_out[...] = rows_ref[...]
    counts_out[...] = counts_ref[...]
    share_rows = pieces[0].shape[1]
    for place, piece in enumerate(pieces):
        here = slice(place * share_rows, (place + 1) * share_rows)
        out_ref[:, here, :] = piece[...]
        for part in range(2):
            high_ref[part, here, :], low_ref[part, here, :] = split(piece[part])


def add_slot(total, left, high_ref, low_ref, rows, cols):
    real, imag = total
    size = real.shape[0]
    both = left[0 : 2 * size]
    left = jnp.concatenate([both, left[2 * size : 4 * size], both], axis=1)

    def panel(part):
        high, low = high_ref[part, rows, cols], low_ref[part, rows, cols]
        return jnp.concatenate([high, high, low], axis=0)

    with_real, with_imag = dot(left, panel(0)), dot(left, panel(1))
    real = real - (with_real[:size] - with_imag[size:])
    imag = imag - (with_imag[:size] + with_real[size:])
    return real, imag


def row_is_live(rows_ref, counts_ref, member, block):
    return lax.fori_loop(
        0,
        counts_ref[0, member],
        lambda q, seen: seen | (rows_ref[member, q] == block),
        False,
    )


def blocks_kernel(*refs):
    pieces, out_ref = refs[:-1], refs[-1]
    rows = out_ref.shape[1] // 4
    first = 0
    for piece in pieces:
        size = piece.shape[1]
        for part in range(2):
            for scale, value in enumerate(split(piece[part])):
                start = (2 * scale + part) * rows + first % rows
                out_ref[first // rows, start : start + size, :] = value
        first += size


def add_slots(member, top, places, rows_ref, counts_ref, high_ref, low_ref, out_ref):
    row_dev = out_ref.shape[1]
    my_block = (lax.axis_index("row") * row_dev) // B
    my_col = lax.axis_index("col")
    cols = slice(member * B, (member + 1) * B)
    live = row_is_live(rows_ref, counts_ref, member, my_block)

    def slot(q, carry):
        held, place = places(my_col ^ rows_ref[member, q])

        @pl.when(held)
        def _():
            rows = pl.ds(pl.multiple_of(q * B, B), B)
            total = out_ref[0, :, cols], out_ref[1, :, cols]
            total = add_slot(total, top[place], high_ref, low_ref, rows, cols)
            out_ref[0, :, cols], out_ref[1, :, cols] = total

        return carry

    lax.fori_loop(0, jnp.where(live, counts_ref[0, member], 0), slot, 0)


def early_place(n_col, distance):
    return (distance % 2 == 0) | (distance == 1), jnp.where(distance == 1, n_col // 2, distance // 2)


def late_place(distance):
    return (distance % 2 == 1) & (distance > 1), (distance - 3) // 2


def fetch(sems, *pairs):
    copies = [pltpu.make_async_copy(*pair, sems.at[k]) for k, pair in enumerate(pairs)]
    for copy in copies:
        copy.start()
    return copies


def turn(member, out_ref, sent, turned):
    chips, _, share, row_dev = turned.shape
    cols = slice(member * B, (member + 1) * B)
    for part in range(2):
        turned[:, part] = out_ref[part, :, cols].T.reshape(chips, share, row_dev)
    for step in range(chips):
        sent[step][member] = turned[(lax.axis_index("row") // 2) ^ step]


def early_kernel(n_col, share_rows, near, far, *refs):
    rows_hbm, counts_hbm, top, own, mate, near_high, near_low, near_mates = refs[:8]
    far_panels, refs = refs[8 : 8 + 2 * len(far)], refs[8 + 2 * len(far) :]
    high_ref, low_ref, out_ref = refs[:3]
    sent, (turned, rows_ref, counts_ref, sems) = refs[3:-4], refs[-4:]
    me = lax.axis_index("row")
    arrivals = fetch(sems, (rows_hbm, rows_ref), (counts_hbm, counts_ref))

    def put(owner, high, low):
        rows = pl.ds(pl.multiple_of(owner * share_rows, share_rows), share_rows)
        high_ref[:, rows, :], low_ref[:, rows, :] = high, low

    put(me, *split(own[...]))
    put(me ^ 1, *split(mate[...]))
    for place, step in enumerate(near):
        here = slice(place * share_rows, (place + 1) * share_rows)
        put(me ^ step, near_high[:, here, :], near_low[:, here, :])
        put(me ^ step ^ 1, *split(near_mates[:, here, :]))
    for place, step in enumerate(far):
        put(me ^ step, *split(far_panels[2 * place][...]))
        put(me ^ step ^ 1, *split(far_panels[2 * place + 1][...]))
    out_ref[...] = jnp.zeros(out_ref.shape, F32)
    for copy in arrivals:
        copy.wait()
    places = functools.partial(early_place, n_col)
    for member in range(rows_ref.shape[0]):
        add_slots(member, top, places, rows_ref, counts_ref, high_ref, low_ref, out_ref)
        turn(member, out_ref, sent, turned)


def select_kernel(chips, *refs):
    rows_hbm, counts_hbm, top, high_ref, low_ref, early_ref = refs[:6]
    early_sent, out_ref, sent = refs[6 : 6 + chips], refs[6 + chips], refs[7 + chips : -4]
    turned, rows_ref, counts_ref, sems = refs[-4:]
    row_dev = out_ref.shape[1]
    my_block = (lax.axis_index("row") * row_dev) // B
    my_col = lax.axis_index("col")
    arrivals = fetch(sems, (rows_hbm, rows_ref), (counts_hbm, counts_ref))
    out_ref[...] = early_ref[...]
    for step in range(chips):
        sent[step][...] = early_sent[step][...]
    for copy in arrivals:
        copy.wait()
    for member in range(rows_ref.shape[0]):
        any_late = lax.fori_loop(
            0,
            counts_ref[0, member],
            lambda q, seen: seen | late_place(my_col ^ rows_ref[member, q])[0],
            False,
        )

        @pl.when(any_late & row_is_live(rows_ref, counts_ref, member, my_block))
        def _():
            add_slots(member, top, late_place, rows_ref, counts_ref, high_ref, low_ref, out_ref)
            turn(member, out_ref, sent, turned)


def write_kernel(value_ref, out_ref):
    out_ref[...] = value_ref[...]


def diagonal_kernel(rows_ref, *refs):
    pieces, (high_ref, low_ref, diag_ref, keep_ref, give_ref, whole) = refs[:-6], refs[-6:]
    leaves, slots = rows_ref.shape
    _, _, chip_share, row_dev = pieces[0].shape
    share = keep_ref.shape[1]
    me = lax.axis_index("row")
    core = me % 2

    def pick(member, q):
        block = jnp.broadcast_to(rows_ref[member : member + 1, q : q + 1], (2 * chip_share, row_dev))
        picked = jnp.zeros(block.shape, F32)
        for step, piece in enumerate(reversed(pieces)):
            here = block == (me // 2) ^ step
            picked = jnp.where(here, piece[member].reshape(block.shape), picked)
        return jnp.concatenate(split(picked), axis=0)

    for member in range(leaves):
        cols = slice(member * B, (member + 1) * B)
        left = jnp.concatenate([pick(member, q) for q in range(slots)], axis=1)
        both = left[: 2 * chip_share]

        def panel(ref, part):
            starts = [pl.multiple_of(q * B + core * row_dev, row_dev) for q in range(slots)]
            return jnp.concatenate(
                [ref[part, pl.ds(start, row_dev), cols] for start in starts], axis=0
            )

        with_real = dot(left, panel(high_ref, 0))
        with_imag = dot(left, panel(high_ref, 1))
        with_real = with_real[: 2 * chip_share] + with_real[2 * chip_share :]
        with_imag = with_imag[: 2 * chip_share] + with_imag[2 * chip_share :]
        with_real += dot(both, panel(low_ref, 0))
        with_imag += dot(both, panel(low_ref, 1))
        whole[0, :, cols] = with_real[:chip_share] - with_imag[chip_share:]
        whole[1, :, cols] = with_imag[:chip_share] + with_real[chip_share:]
    mine = pl.ds(pl.multiple_of(core * share, share), share)
    other = pl.ds(pl.multiple_of((1 - core) * share, share), share)
    keep_ref[...] = diag_ref[...] - whole[:, mine, :]
    give_ref[...] = whole[:, other, :]


def subtract_kernel(left_ref, right_ref, out_ref):
    out_ref[...] = left_ref[...] - right_ref[...]


def on_device(n_row, n_col, top_inverse, panel, leaf_rows, leaf_counts, diag_inverse):
    vmem = pl.BlockSpec(memory_space=pltpu.VMEM)
    hbm = pl.BlockSpec(memory_space=pl.ANY)
    _, row_dev, _ = top_inverse.shape
    _, panel_rows, columns = panel.shape
    leaves = columns // B
    chips = n_row // 2
    chip_share = B // chips
    depth = n_row * panel_rows
    params = pltpu.CompilerParams(vmem_limit_bytes=max(16 << 20, 40 * depth * columns))

    def cut(block):
        sizes = row_dev // 4, row_dev - row_dev // 4
        return pl.pallas_call(
            cut_kernel,
            out_shape=[jax.ShapeDtypeStruct((2, size, B), F32) for size in sizes],
            in_specs=[vmem],
            out_specs=[vmem] * 2,
            compiler_params=params,
            name="cut_rows",
        )(block)

    blocks, halves = line_gather(top_inverse, "col", n_col, cut)

    swap = [(i, i ^ 1) for i in range(n_row)]
    like = {
        step: lax.ppermute(panel, "row", [(i, i ^ step) for i in range(n_row)])
        for step in range(2, n_row, 2)
    }
    near = [step for step in like if step & -step == step]
    far = [step for step in like if step not in near]
    packed = (2, len(near) * panel_rows, columns)
    leaf_counts = leaf_counts[None, :]
    mine, near_high, near_low, leaf_rows, leaf_counts = pl.pallas_call(
        pack_kernel,
        out_shape=[jax.ShapeDtypeStruct(packed, dtype) for dtype in (F32, BF16, BF16)]
        + [jax.ShapeDtypeStruct(value.shape, value.dtype) for value in (leaf_rows, leaf_counts)],
        in_specs=[vmem] * (2 + len(near)),
        out_specs=[vmem] * 5,
        compiler_params=params,
        name="pack_panel",
    )(leaf_rows, leaf_counts, *[like[step] for step in near])
    mate = lax.ppermute(panel, "row", swap)
    near_mates = lax.ppermute(mine, "row", swap)
    far_panels = []
    for step in far:
        far_panels += [like[step], lax.ppermute(like[step], "row", swap)]

    early_blocks = [blocks[k] for k in range(0, n_col, 2)] + [blocks[1]]
    firsts = [halves[k][0] for k in range(3, n_col, 2)]
    early_blocks, firsts = lax.optimization_barrier((early_blocks, firsts))
    late_blocks = [half for k in range(3, n_col, 2) for half in halves[k]]

    def split_blocks(values):
        count = sum(value.shape[1] for value in values) // row_dev
        return pl.pallas_call(
            blocks_kernel,
            out_shape=jax.ShapeDtypeStruct((count, 4 * row_dev, B), BF16),
            in_specs=[vmem] * len(values),
            out_specs=vmem,
            compiler_params=params,
            cost_estimate=pl.CostEstimate(
                flops=10**11, bytes_accessed=10**9, transcendentals=0
            ),
            name="split_blocks",
        )(*values)

    indices = [
        pltpu.SMEM(leaf_rows.shape, leaf_rows.dtype),
        pltpu.SMEM(leaf_counts.shape, leaf_counts.dtype),
        pltpu.SemaphoreType.DMA((2,)),
    ]
    rows_shape = jax.ShapeDtypeStruct((2, row_dev, columns), F32)
    piece = jax.ShapeDtypeStruct((leaves, 2, chip_share, row_dev), F32)
    scratch = [pltpu.VMEM((chips,) + piece.shape[1:], F32)] + indices
    high, low, *early = pl.pallas_call(
        functools.partial(early_kernel, n_col, panel_rows, near, far),
        out_shape=[jax.ShapeDtypeStruct((2, depth, columns), BF16)] * 2
        + [rows_shape]
        + [piece] * chips,
        in_specs=[hbm, hbm] + [vmem] * (6 + len(far_panels)),
        out_specs=[vmem] * (3 + chips),
        scratch_shapes=scratch,
        compiler_params=params,
        name="early_rows",
    )(
        leaf_rows,
        leaf_counts,
        split_blocks(early_blocks),
        panel,
        mate,
        near_high,
        near_low,
        near_mates,
        *far_panels,
    )
    early, late_blocks = lax.optimization_barrier((early, late_blocks))

    selected, *sent = pl.pallas_call(
        functools.partial(select_kernel, chips),
        out_shape=[rows_shape] + [piece] * chips,
        in_specs=[hbm, hbm] + [vmem] * (4 + chips),
        out_specs=[vmem] * (1 + chips),
        scratch_shapes=scratch,
        compiler_params=params,
        name="selected_rows",
    )(leaf_rows, leaf_counts, split_blocks(late_blocks), high, low, *early)

    for step in range(chips - 1, 0, -1):
        perm = [(i, i ^ (2 * step)) for i in range(n_row)]
        sent[step] = lax.ppermute(sent[step], "row", perm)
    selected = pl.pallas_call(
        write_kernel,
        out_shape=jax.ShapeDtypeStruct(selected.shape, F32),
        in_specs=[vmem],
        out_specs=vmem,
        compiler_params=params,
        name="write_rows",
    )(selected)
    selected, sent = lax.optimization_barrier((selected, sent[::-1]))

    keep, give = pl.pallas_call(
        diagonal_kernel,
        out_shape=[jax.ShapeDtypeStruct(diag_inverse.shape, F32)] * 2,
        in_specs=[vmem] * (chips + 4),
        out_specs=[vmem] * 2,
        scratch_shapes=[pltpu.VMEM((2, chip_share, columns), F32)],
        compiler_params=params,
        cost_estimate=pl.CostEstimate(
            flops=12 * chip_share * depth * columns,
            bytes_accessed=8 * (depth + 2 * chip_share) * columns,
            transcendentals=0,
        ),
        name="diagonal_part",
    )(leaf_rows, *sent, high, low, diag_inverse)
    give = lax.ppermute(give, "row", [(i, i ^ 1) for i in range(n_row)])
    diagonal = pl.pallas_call(
        subtract_kernel,
        out_shape=jax.ShapeDtypeStruct(diag_inverse.shape, F32),
        in_specs=[vmem] * 2,
        out_specs=vmem,
        compiler_params=params,
        name="diagonal_rows",
    )(keep, give)
    return selected, diagonal


def solution(mesh):
    return jax.shard_map(
        functools.partial(on_device, mesh.shape["row"], mesh.shape["col"]),
        mesh=mesh,
        in_specs=(
            P(None, "row", "col"),
            P(None, "row", "col"),
            P("col", None),
            P("col"),
            P(None, "row", "col"),
        ),
        out_specs=(P(None, "row", "col"), P(None, "row", "col")),
        check_vma=False,
    )
```

```python
import functools

import jax
import jax.numpy as jnp
from jax import lax
from jax.experimental import pallas as pl
from jax.experimental.pallas import tpu as pltpu
from jax.sharding import PartitionSpec as P

B = 256
F32 = jnp.float32
BF16 = jnp.bfloat16


def split(value):
    high = value.astype(BF16)
    low = (value - high.astype(F32)).astype(BF16)
    return high, low


def dot(left, right):
    return jnp.dot(left, right, preferred_element_type=F32)


def line_gather(own, axis, n, cut):
    blocks = {0: own}
    for step in line_steps(n):
        perm = [(i, i ^ step) for i in range(n)]
        if step > 1:
            blocks |= {k ^ step: lax.ppermute(block, axis, perm) for k, block in blocks.items()}
    halves = {k ^ 1: cut(block) for k, block in blocks.items() if k > 0}
    halves = {k: [lax.ppermute(half, axis, perm) for half in pair] for k, pair in halves.items()}
    blocks[1] = lax.ppermute(own, axis, perm)
    return blocks, halves


def line_steps(n):
    steps = []
    while n > 1:
        n //= 2
        steps.append(n)
    return steps


def cut_kernel(block_ref, first_ref, second_ref):
    size = first_ref.shape[1]
    first_ref[...] = block_ref[:, :size, :]
    second_ref[...] = block_ref[:, size:, :]


def pack_kernel(*refs):
    (rows_ref, counts_ref), pieces = refs[:2], refs[2:-5]
    out_ref, high_ref, low_ref, rows_out, counts_out = refs[-5:]
    rows_out[...] = rows_ref[...]
    counts_out[...] = counts_ref[...]
    share_rows = pieces[0].shape[1]
    for place, piece in enumerate(pieces):
        here = slice(place * share_rows, (place + 1) * share_rows)
        out_ref[:, here, :] = piece[...]
        for part in range(2):
            high_ref[part, here, :], low_ref[part, here, :] = split(piece[part])


def add_slot(total, left, high_ref, low_ref, rows, cols):
    real, imag = total
    size = real.shape[0]
    both = left[0 : 2 * size]
    left = jnp.concatenate([both, left[2 * size : 4 * size], both], axis=1)

    def panel(part):
        high, low = high_ref[part, rows, cols], low_ref[part, rows, cols]
        return jnp.concatenate([high, high, low], axis=0)

    with_real, with_imag = dot(left, panel(0)), dot(left, panel(1))
    real = real - (with_real[:size] - with_imag[size:])
    imag = imag - (with_imag[:size] + with_real[size:])
    return real, imag


def row_is_live(rows_ref, counts_ref, member, block):
    return lax.fori_loop(
        0,
        counts_ref[0, member],
        lambda q, seen: seen | (rows_ref[member, q] == block),
        False,
    )


def blocks_kernel(*refs):
    pieces, out_ref = refs[:-1], refs[-1]
    rows = out_ref.shape[1] // 4
    first = 0
    for piece in pieces:
        size = piece.shape[1]
        for part in range(2):
            for scale, value in enumerate(split(piece[part])):
                start = (2 * scale + part) * rows + first % rows
                out_ref[first // rows, start : start + size, :] = value
        first += size


def add_product(member, q, top, place, high_ref, low_ref, out_ref):
    cols = slice(member * B, (member + 1) * B)
    rows = pl.ds(pl.multiple_of(q * B, B), B)
    total = out_ref[0, :, cols], out_ref[1, :, cols]
    total = add_slot(total, top[place], high_ref, low_ref, rows, cols)
    out_ref[0, :, cols], out_ref[1, :, cols] = total


def early_place(n_col, distance):
    return (distance % 2 == 0) | (distance == 1), jnp.where(distance == 1, n_col // 2, distance // 2)


def late_place(distance):
    return (distance - 3) // 2


def fetch(sems, *pairs):
    copies = [pltpu.make_async_copy(*pair, sems.at[k]) for k, pair in enumerate(pairs)]
    for copy in copies:
        copy.start()
    return copies


def turn(member, out_ref, sent, turned):
    chips, _, share, row_dev = turned.shape
    cols = slice(member * B, (member + 1) * B)
    for part in range(2):
        turned[:, part] = out_ref[part, :, cols].T.reshape(chips, share, row_dev)
    for step in range(chips):
        sent[step][member] = turned[(lax.axis_index("row") // 2) ^ step]


def early_kernel(n_col, share_rows, near, far, *refs):
    rows_hbm, counts_hbm, top, own, mate, near_high, near_low, near_mates = refs[:8]
    far_panels, refs = refs[8 : 8 + 2 * len(far)], refs[8 + 2 * len(far) :]
    high_ref, low_ref, late_ref, out_ref = refs[:4]
    sent, (turned, rows_ref, counts_ref, sems) = refs[4:-4], refs[-4:]
    leaves, slots = rows_ref.shape
    me = lax.axis_index("row")
    my_block = (me * out_ref.shape[1]) // B
    my_col = lax.axis_index("col")
    arrivals = fetch(sems, (rows_hbm, rows_ref), (counts_hbm, counts_ref))

    def put(owner, high, low):
        rows = pl.ds(pl.multiple_of(owner * share_rows, share_rows), share_rows)
        high_ref[:, rows, :], low_ref[:, rows, :] = high, low

    put(me, *split(own[...]))
    put(me ^ 1, *split(mate[...]))
    for place, step in enumerate(near):
        here = slice(place * share_rows, (place + 1) * share_rows)
        put(me ^ step, near_high[:, here, :], near_low[:, here, :])
        put(me ^ step ^ 1, *split(near_mates[:, here, :]))
    for place, step in enumerate(far):
        put(me ^ step, *split(far_panels[2 * place][...]))
        put(me ^ step ^ 1, *split(far_panels[2 * place + 1][...]))
    out_ref[...] = jnp.zeros(out_ref.shape, F32)
    for copy in arrivals:
        copy.wait()
    here = [lax.broadcasted_iota(jnp.int32, (leaves, slots), axis) for axis in range(2)]
    late_ref[...] = jnp.zeros((leaves, slots), jnp.int32)
    for member in range(leaves):

        def slot(q, carry):
            distance = my_col ^ rows_ref[member, q]
            held, place = early_place(n_col, distance)

            @pl.when(held)
            def _():
                add_product(member, q, top, place, high_ref, low_ref, out_ref)

            @pl.when(jnp.logical_not(held))
            def _():
                mark = (here[0] == member) & (here[1] == q)
                late_ref[...] = jnp.where(mark, 1 + late_place(distance), late_ref[...])

            return carry

        live = row_is_live(rows_ref, counts_ref, member, my_block)
        lax.fori_loop(0, jnp.where(live, counts_ref[0, member], 0), slot, 0)
        turn(member, out_ref, sent, turned)


def select_kernel(chips, late_ref, top, high_ref, low_ref, early_ref, *refs):
    early_sent, out_ref, sent, turned = refs[:chips], refs[chips], refs[chips + 1 : -1], refs[-1]
    leaves, slots = late_ref.shape
    out_ref[...] = early_ref[...]
    for step in range(chips):
        sent[step][...] = early_sent[step][...]
    for member in range(leaves):
        marks = late_ref[member : member + 1, :]

        @pl.when(jnp.max(marks) > 0)
        def _():
            def slot(q, carry):
                lane = lax.broadcasted_iota(jnp.int32, marks.shape, 1)
                mark = jnp.max(jnp.where(lane == q, marks, 0))

                @pl.when(mark > 0)
                def _():
                    add_product(member, q, top, mark - 1, high_ref, low_ref, out_ref)

                return carry

            lax.fori_loop(0, slots, slot, 0)
            turn(member, out_ref, sent, turned)


def write_kernel(value_ref, out_ref):
    out_ref[...] = value_ref[...]


def diagonal_kernel(rows_ref, *refs):
    pieces, (high_ref, low_ref, diag_ref, keep_ref, give_ref, whole) = refs[:-6], refs[-6:]
    leaves, slots = rows_ref.shape
    _, _, chip_share, row_dev = pieces[0].shape
    share = keep_ref.shape[1]
    me = lax.axis_index("row")
    core = me % 2

    def pick(member, q):
        block = jnp.broadcast_to(rows_ref[member : member + 1, q : q + 1], (2 * chip_share, row_dev))
        picked = jnp.zeros(block.shape, F32)
        for step, piece in enumerate(reversed(pieces)):
            here = block == (me // 2) ^ step
            picked = jnp.where(here, piece[member].reshape(block.shape), picked)
        return jnp.concatenate(split(picked), axis=0)

    for member in range(leaves):
        cols = slice(member * B, (member + 1) * B)
        left = jnp.concatenate([pick(member, q) for q in range(slots)], axis=1)
        both = left[: 2 * chip_share]

        def panel(ref, part):
            starts = [pl.multiple_of(q * B + core * row_dev, row_dev) for q in range(slots)]
            return jnp.concatenate(
                [ref[part, pl.ds(start, row_dev), cols] for start in starts], axis=0
            )

        with_real = dot(left, panel(high_ref, 0))
        with_imag = dot(left, panel(high_ref, 1))
        with_real = with_real[: 2 * chip_share] + with_real[2 * chip_share :]
        with_imag = with_imag[: 2 * chip_share] + with_imag[2 * chip_share :]
        with_real += dot(both, panel(low_ref, 0))
        with_imag += dot(both, panel(low_ref, 1))
        whole[0, :, cols] = with_real[:chip_share] - with_imag[chip_share:]
        whole[1, :, cols] = with_imag[:chip_share] + with_real[chip_share:]
    mine = pl.ds(pl.multiple_of(core * share, share), share)
    other = pl.ds(pl.multiple_of((1 - core) * share, share), share)
    keep_ref[...] = diag_ref[...] - whole[:, mine, :]
    give_ref[...] = whole[:, other, :]


def subtract_kernel(left_ref, right_ref, out_ref):
    out_ref[...] = left_ref[...] - right_ref[...]


def on_device(n_row, n_col, top_inverse, panel, leaf_rows, leaf_counts, diag_inverse):
    vmem = pl.BlockSpec(memory_space=pltpu.VMEM)
    hbm = pl.BlockSpec(memory_space=pl.ANY)
    _, row_dev, _ = top_inverse.shape
    _, panel_rows, columns = panel.shape
    leaves = columns // B
    chips = n_row // 2
    chip_share = B // chips
    depth = n_row * panel_rows
    params = pltpu.CompilerParams(vmem_limit_bytes=max(16 << 20, 40 * depth * columns))

    def cut(block):
        sizes = row_dev // 2, row_dev - row_dev // 2
        return pl.pallas_call(
            cut_kernel,
            out_shape=[jax.ShapeDtypeStruct((2, size, B), F32) for size in sizes],
            in_specs=[vmem],
            out_specs=[vmem] * 2,
            compiler_params=params,
            name="cut_rows",
        )(block)

    blocks, halves = line_gather(top_inverse, "col", n_col, cut)

    swap = [(i, i ^ 1) for i in range(n_row)]
    like = {
        step: lax.ppermute(panel, "row", [(i, i ^ step) for i in range(n_row)])
        for step in range(2, n_row, 2)
    }
    near = [step for step in like if step & -step == step]
    far = [step for step in like if step not in near]
    packed = (2, len(near) * panel_rows, columns)
    leaf_counts = leaf_counts[None, :]
    mine, near_high, near_low, leaf_rows, leaf_counts = pl.pallas_call(
        pack_kernel,
        out_shape=[jax.ShapeDtypeStruct(packed, dtype) for dtype in (F32, BF16, BF16)]
        + [jax.ShapeDtypeStruct(value.shape, value.dtype) for value in (leaf_rows, leaf_counts)],
        in_specs=[vmem] * (2 + len(near)),
        out_specs=[vmem] * 5,
        compiler_params=params,
        name="pack_panel",
    )(leaf_rows, leaf_counts, *[like[step] for step in near])
    mate = lax.ppermute(panel, "row", swap)
    near_mates = lax.ppermute(mine, "row", swap)
    far_panels = []
    for step in far:
        far_panels += [like[step], lax.ppermute(like[step], "row", swap)]

    early_blocks = [blocks[k] for k in range(0, n_col, 2)] + [blocks[1]]
    firsts = [halves[k][0] for k in range(3, n_col, 2)]
    early_blocks, firsts = lax.optimization_barrier((early_blocks, firsts))
    late_blocks = [half for k in range(3, n_col, 2) for half in halves[k]]

    def split_blocks(values):
        count = sum(value.shape[1] for value in values) // row_dev
        return pl.pallas_call(
            blocks_kernel,
            out_shape=jax.ShapeDtypeStruct((count, 4 * row_dev, B), BF16),
            in_specs=[vmem] * len(values),
            out_specs=vmem,
            compiler_params=params,
            cost_estimate=pl.CostEstimate(
                flops=10**11, bytes_accessed=10**9, transcendentals=0
            ),
            name="split_blocks",
        )(*values)

    indices = [
        pltpu.SMEM(leaf_rows.shape, leaf_rows.dtype),
        pltpu.SMEM(leaf_counts.shape, leaf_counts.dtype),
        pltpu.SemaphoreType.DMA((2,)),
    ]
    rows_shape = jax.ShapeDtypeStruct((2, row_dev, columns), F32)
    piece = jax.ShapeDtypeStruct((leaves, 2, chip_share, row_dev), F32)
    scratch = [pltpu.VMEM((chips,) + piece.shape[1:], F32)] + indices
    high, low, late, *early = pl.pallas_call(
        functools.partial(early_kernel, n_col, panel_rows, near, far),
        out_shape=[jax.ShapeDtypeStruct((2, depth, columns), BF16)] * 2
        + [jax.ShapeDtypeStruct(leaf_rows.shape, jnp.int32), rows_shape]
        + [piece] * chips,
        in_specs=[hbm, hbm] + [vmem] * (6 + len(far_panels)),
        out_specs=[vmem] * (4 + chips),
        scratch_shapes=scratch,
        compiler_params=params,
        name="early_rows",
    )(
        leaf_rows,
        leaf_counts,
        split_blocks(early_blocks),
        panel,
        mate,
        near_high,
        near_low,
        near_mates,
        *far_panels,
    )
    early, late_blocks = lax.optimization_barrier((early, late_blocks))

    selected, *sent = pl.pallas_call(
        functools.partial(select_kernel, chips),
        out_shape=[rows_shape] + [piece] * chips,
        in_specs=[vmem] * (5 + chips),
        out_specs=[vmem] * (1 + chips),
        scratch_shapes=scratch[:1],
        compiler_params=params,
        name="selected_rows",
    )(late, split_blocks(late_blocks), high, low, *early)

    for step in range(chips - 1, 0, -1):
        perm = [(i, i ^ (2 * step)) for i in range(n_row)]
        sent[step] = lax.ppermute(sent[step], "row", perm)
    selected = pl.pallas_call(
        write_kernel,
        out_shape=jax.ShapeDtypeStruct(selected.shape, F32),
        in_specs=[vmem],
        out_specs=vmem,
        compiler_params=params,
        name="write_rows",
    )(selected)
    selected, sent = lax.optimization_barrier((selected, sent[::-1]))

    keep, give = pl.pallas_call(
        diagonal_kernel,
        out_shape=[jax.ShapeDtypeStruct(diag_inverse.shape, F32)] * 2,
        in_specs=[vmem] * (chips + 4),
        out_specs=[vmem] * 2,
        scratch_shapes=[pltpu.VMEM((2, chip_share, columns), F32)],
        compiler_params=params,
        cost_estimate=pl.CostEstimate(
            flops=12 * chip_share * depth * columns,
            bytes_accessed=8 * (depth + 2 * chip_share) * columns,
            transcendentals=0,
        ),
        name="diagonal_part",
    )(leaf_rows, *sent, high, low, diag_inverse)
    give = lax.ppermute(give, "row", [(i, i ^ 1) for i in range(n_row)])
    diagonal = pl.pallas_call(
        subtract_kernel,
        out_shape=jax.ShapeDtypeStruct(diag_inverse.shape, F32),
        in_specs=[vmem] * 2,
        out_specs=vmem,
        compiler_params=params,
        name="diagonal_rows",
    )(keep, give)
    return selected, diagonal


def solution(mesh):
    return jax.shard_map(
        functools.partial(on_device, mesh.shape["row"], mesh.shape["col"]),
        mesh=mesh,
        in_specs=(
            P(None, "row", "col"),
            P(None, "row", "col"),
            P("col", None),
            P("col"),
            P(None, "row", "col"),
        ),
        out_specs=(P(None, "row", "col"), P(None, "row", "col")),
        check_vma=False,
    )
```

```python
import functools

import jax
import jax.numpy as jnp
from jax import lax
from jax.experimental import pallas as pl
from jax.experimental.pallas import tpu as pltpu
from jax.sharding import PartitionSpec as P

B = 256
F32 = jnp.float32
BF16 = jnp.bfloat16


def split(value):
    high = value.astype(BF16)
    low = (value - high.astype(F32)).astype(BF16)
    return high, low


def dot(left, right):
    return jnp.dot(left, right, preferred_element_type=F32)


def line_gather(own, axis, n, cut):
    blocks = {0: own}
    for step in line_steps(n):
        perm = [(i, i ^ step) for i in range(n)]
        if step > 1:
            blocks |= {k ^ step: lax.ppermute(block, axis, perm) for k, block in blocks.items()}
    halves = {k ^ 1: cut(block) for k, block in blocks.items() if k > 0}
    halves = {k: [lax.ppermute(half, axis, perm) for half in pair] for k, pair in halves.items()}
    blocks[1] = lax.ppermute(own, axis, perm)
    return blocks, halves


def line_steps(n):
    steps = []
    while n > 1:
        n //= 2
        steps.append(n)
    return steps


def cut_kernel(block_ref, first_ref, second_ref):
    size = first_ref.shape[1]
    first_ref[...] = block_ref[:, :size, :]
    second_ref[...] = block_ref[:, size:, :]


def pack_kernel(n_col, row_dev, rows_ref, counts_ref, *refs):
    pieces, (out_ref, high_ref, low_ref, early_ref, late_ref, rows_out) = refs[:-6], refs[-6:]
    rows = rows_ref[...]
    rows_out[...] = rows
    active = lax.broadcasted_iota(jnp.int32, rows.shape, 1) < counts_ref[...]
    mine = active & (rows == (lax.axis_index("row") * row_dev) // B)
    live = jnp.max(jnp.where(mine, 1, 0), axis=1, keepdims=True) > 0
    distance = rows ^ lax.axis_index("col")
    early = ((distance & 1) == 0) | (distance == 1)
    place = jnp.where(distance == 1, n_col // 2, distance >> 1)
    early_ref[...] = jnp.where(active & live & early, 1 + place, 0)
    late_ref[...] = jnp.where(active & live & jnp.logical_not(early), (distance - 1) >> 1, 0)
    share_rows = pieces[0].shape[1]
    for place, piece in enumerate(pieces):
        here = slice(place * share_rows, (place + 1) * share_rows)
        out_ref[:, here, :] = piece[...]
        for part in range(2):
            high_ref[part, here, :], low_ref[part, here, :] = split(piece[part])


def add_slot(total, left, high_ref, low_ref, rows, cols):
    real, imag = total
    size = real.shape[0]
    both = left[0 : 2 * size]
    left = jnp.concatenate([both, left[2 * size : 4 * size], both], axis=1)

    def panel(part):
        high, low = high_ref[part, rows, cols], low_ref[part, rows, cols]
        return jnp.concatenate([high, high, low], axis=0)

    with_real, with_imag = dot(left, panel(0)), dot(left, panel(1))
    real = real - (with_real[:size] - with_imag[size:])
    imag = imag - (with_imag[:size] + with_real[size:])
    return real, imag


def blocks_kernel(*refs):
    pieces, out_ref = refs[:-1], refs[-1]
    rows = out_ref.shape[1] // 4
    first = 0
    for piece in pieces:
        size = piece.shape[1]
        for part in range(2):
            for scale, value in enumerate(split(piece[part])):
                start = (2 * scale + part) * rows + first % rows
                out_ref[first // rows, start : start + size, :] = value
        first += size


def add_marked(member, marks_ref, top, high_ref, low_ref, out_ref):
    marks = marks_ref[member : member + 1, :]
    cols = slice(member * B, (member + 1) * B)

    def slot(q, carry):
        mark = jnp.max(jnp.where(lax.broadcasted_iota(jnp.int32, marks.shape, 1) == q, marks, 0))

        @pl.when(mark > 0)
        def _():
            rows = pl.ds(pl.multiple_of(q * B, B), B)
            total = out_ref[0, :, cols], out_ref[1, :, cols]
            total = add_slot(total, top[mark - 1], high_ref, low_ref, rows, cols)
            out_ref[0, :, cols], out_ref[1, :, cols] = total

        return carry

    lax.fori_loop(0, marks.shape[1], slot, 0)


def turn(member, out_ref, sent, turned):
    chips, _, share, row_dev = turned.shape
    cols = slice(member * B, (member + 1) * B)
    for part in range(2):
        turned[:, part] = out_ref[part, :, cols].T.reshape(chips, share, row_dev)
    for step in range(chips):
        sent[step][member] = turned[(lax.axis_index("row") // 2) ^ step]


def early_kernel(share_rows, near, far, marks_ref, top, *refs):
    own, mate, near_high, near_low, near_mates = refs[:5]
    far_panels, refs = refs[5 : 5 + 2 * len(far)], refs[5 + 2 * len(far) :]
    high_ref, low_ref, out_ref = refs[:3]
    sent, turned = refs[3:-1], refs[-1]
    me = lax.axis_index("row")

    def put(owner, high, low):
        rows = pl.ds(pl.multiple_of(owner * share_rows, share_rows), share_rows)
        high_ref[:, rows, :], low_ref[:, rows, :] = high, low

    put(me, *split(own[...]))
    put(me ^ 1, *split(mate[...]))
    for place, step in enumerate(near):
        here = slice(place * share_rows, (place + 1) * share_rows)
        put(me ^ step, near_high[:, here, :], near_low[:, here, :])
        put(me ^ step ^ 1, *split(near_mates[:, here, :]))
    for place, step in enumerate(far):
        put(me ^ step, *split(far_panels[2 * place][...]))
        put(me ^ step ^ 1, *split(far_panels[2 * place + 1][...]))
    out_ref[...] = jnp.zeros(out_ref.shape, F32)
    for member in range(marks_ref.shape[0]):
        add_marked(member, marks_ref, top, high_ref, low_ref, out_ref)
        turn(member, out_ref, sent, turned)


def select_kernel(chips, marks_ref, top, high_ref, low_ref, early_ref, *refs):
    early_sent, out_ref, sent, turned = refs[:chips], refs[chips], refs[chips + 1 : -1], refs[-1]
    out_ref[...] = early_ref[...]
    for step in range(chips):
        sent[step][...] = early_sent[step][...]
    for member in range(marks_ref.shape[0]):

        @pl.when(jnp.max(marks_ref[member : member + 1, :]) > 0)
        def _():
            add_marked(member, marks_ref, top, high_ref, low_ref, out_ref)
            turn(member, out_ref, sent, turned)


def write_kernel(value_ref, out_ref):
    out_ref[...] = value_ref[...]


def diagonal_kernel(rows_ref, *refs):
    pieces, (high_ref, low_ref, diag_ref, keep_ref, give_ref, whole) = refs[:-6], refs[-6:]
    leaves, slots = rows_ref.shape
    _, _, chip_share, row_dev = pieces[0].shape
    share = keep_ref.shape[1]
    me = lax.axis_index("row")
    core = me % 2

    def pick(member, q):
        block = jnp.broadcast_to(rows_ref[member : member + 1, q : q + 1], (2 * chip_share, row_dev))
        picked = jnp.zeros(block.shape, F32)
        for step, piece in enumerate(reversed(pieces)):
            here = block == (me // 2) ^ step
            picked = jnp.where(here, piece[member].reshape(block.shape), picked)
        return jnp.concatenate(split(picked), axis=0)

    for member in range(leaves):
        cols = slice(member * B, (member + 1) * B)
        left = jnp.concatenate([pick(member, q) for q in range(slots)], axis=1)
        both = left[: 2 * chip_share]

        def panel(ref, part):
            starts = [pl.multiple_of(q * B + core * row_dev, row_dev) for q in range(slots)]
            return jnp.concatenate(
                [ref[part, pl.ds(start, row_dev), cols] for start in starts], axis=0
            )

        with_real = dot(left, panel(high_ref, 0))
        with_imag = dot(left, panel(high_ref, 1))
        with_real = with_real[: 2 * chip_share] + with_real[2 * chip_share :]
        with_imag = with_imag[: 2 * chip_share] + with_imag[2 * chip_share :]
        with_real += dot(both, panel(low_ref, 0))
        with_imag += dot(both, panel(low_ref, 1))
        whole[0, :, cols] = with_real[:chip_share] - with_imag[chip_share:]
        whole[1, :, cols] = with_imag[:chip_share] + with_real[chip_share:]
    mine = pl.ds(pl.multiple_of(core * share, share), share)
    other = pl.ds(pl.multiple_of((1 - core) * share, share), share)
    keep_ref[...] = diag_ref[...] - whole[:, mine, :]
    give_ref[...] = whole[:, other, :]


def subtract_kernel(left_ref, right_ref, out_ref):
    out_ref[...] = left_ref[...] - right_ref[...]


def on_device(n_row, n_col, top_inverse, panel, leaf_rows, leaf_counts, diag_inverse):
    vmem = pl.BlockSpec(memory_space=pltpu.VMEM)
    _, row_dev, _ = top_inverse.shape
    _, panel_rows, columns = panel.shape
    leaves = columns // B
    chips = n_row // 2
    chip_share = B // chips
    depth = n_row * panel_rows
    params = pltpu.CompilerParams(vmem_limit_bytes=max(16 << 20, 40 * depth * columns))

    def cut(block):
        sizes = row_dev // 2, row_dev - row_dev // 2
        return pl.pallas_call(
            cut_kernel,
            out_shape=[jax.ShapeDtypeStruct((2, size, B), F32) for size in sizes],
            in_specs=[vmem],
            out_specs=[vmem] * 2,
            compiler_params=params,
            name="cut_rows",
        )(block)

    blocks, halves = line_gather(top_inverse, "col", n_col, cut)

    swap = [(i, i ^ 1) for i in range(n_row)]
    like = {
        step: lax.ppermute(panel, "row", [(i, i ^ step) for i in range(n_row)])
        for step in range(2, n_row, 2)
    }
    near = [step for step in like if step & -step == step]
    far = [step for step in like if step not in near]
    packed = (2, len(near) * panel_rows, columns)
    marks = jax.ShapeDtypeStruct(leaf_rows.shape, leaf_rows.dtype)
    mine, near_high, near_low, early_marks, late_marks, leaf_rows = pl.pallas_call(
        functools.partial(pack_kernel, n_col, row_dev),
        out_shape=[jax.ShapeDtypeStruct(packed, dtype) for dtype in (F32, BF16, BF16)] + [marks] * 3,
        in_specs=[vmem] * (2 + len(near)),
        out_specs=[vmem] * 6,
        compiler_params=params,
        name="pack_panel",
    )(leaf_rows, leaf_counts[:, None], *[like[step] for step in near])
    mate = lax.ppermute(panel, "row", swap)
    near_mates = lax.ppermute(mine, "row", swap)
    far_panels = []
    for step in far:
        far_panels += [like[step], lax.ppermute(like[step], "row", swap)]

    early_blocks = [blocks[k] for k in range(0, n_col, 2)] + [blocks[1]]
    firsts = [halves[k][0] for k in range(3, n_col, 2)]
    early_blocks, firsts = lax.optimization_barrier((early_blocks, firsts))
    late_blocks = [half for k in range(3, n_col, 2) for half in halves[k]]

    def split_blocks(values):
        count = sum(value.shape[1] for value in values) // row_dev
        return pl.pallas_call(
            blocks_kernel,
            out_shape=jax.ShapeDtypeStruct((count, 4 * row_dev, B), BF16),
            in_specs=[vmem] * len(values),
            out_specs=vmem,
            compiler_params=params,
            cost_estimate=pl.CostEstimate(
                flops=10**11, bytes_accessed=10**9, transcendentals=0
            ),
            name="split_blocks",
        )(*values)

    rows_shape = jax.ShapeDtypeStruct((2, row_dev, columns), F32)
    piece = jax.ShapeDtypeStruct((leaves, 2, chip_share, row_dev), F32)
    scratch = [pltpu.VMEM((chips,) + piece.shape[1:], F32)]
    high, low, *early = pl.pallas_call(
        functools.partial(early_kernel, panel_rows, near, far),
        out_shape=[jax.ShapeDtypeStruct((2, depth, columns), BF16)] * 2
        + [rows_shape]
        + [piece] * chips,
        in_specs=[vmem] * (7 + len(far_panels)),
        out_specs=[vmem] * (3 + chips),
        scratch_shapes=scratch,
        compiler_params=params,
        name="early_rows",
    )(
        early_marks,
        split_blocks(early_blocks),
        panel,
        mate,
        near_high,
        near_low,
        near_mates,
        *far_panels,
    )
    early, late_blocks = lax.optimization_barrier((early, late_blocks))

    selected, *sent = pl.pallas_call(
        functools.partial(select_kernel, chips),
        out_shape=[rows_shape] + [piece] * chips,
        in_specs=[vmem] * (5 + chips),
        out_specs=[vmem] * (1 + chips),
        scratch_shapes=scratch,
        compiler_params=params,
        name="selected_rows",
    )(late_marks, split_blocks(late_blocks), high, low, *early)

    for step in range(chips - 1, 0, -1):
        perm = [(i, i ^ (2 * step)) for i in range(n_row)]
        sent[step] = lax.ppermute(sent[step], "row", perm)
    selected = pl.pallas_call(
        write_kernel,
        out_shape=jax.ShapeDtypeStruct(selected.shape, F32),
        in_specs=[vmem],
        out_specs=vmem,
        compiler_params=params,
        name="write_rows",
    )(selected)
    selected, sent = lax.optimization_barrier((selected, sent[::-1]))

    keep, give = pl.pallas_call(
        diagonal_kernel,
        out_shape=[jax.ShapeDtypeStruct(diag_inverse.shape, F32)] * 2,
        in_specs=[vmem] * (chips + 4),
        out_specs=[vmem] * 2,
        scratch_shapes=[pltpu.VMEM((2, chip_share, columns), F32)],
        compiler_params=params,
        cost_estimate=pl.CostEstimate(
            flops=12 * chip_share * depth * columns,
            bytes_accessed=8 * (depth + 2 * chip_share) * columns,
            transcendentals=0,
        ),
        name="diagonal_part",
    )(leaf_rows, *sent, high, low, diag_inverse)
    give = lax.ppermute(give, "row", [(i, i ^ 1) for i in range(n_row)])
    diagonal = pl.pallas_call(
        subtract_kernel,
        out_shape=jax.ShapeDtypeStruct(diag_inverse.shape, F32),
        in_specs=[vmem] * 2,
        out_specs=vmem,
        compiler_params=params,
        name="diagonal_rows",
    )(keep, give)
    return selected, diagonal


def solution(mesh):
    return jax.shard_map(
        functools.partial(on_device, mesh.shape["row"], mesh.shape["col"]),
        mesh=mesh,
        in_specs=(
            P(None, "row", "col"),
            P(None, "row", "col"),
            P("col", None),
            P("col"),
            P(None, "row", "col"),
        ),
        out_specs=(P(None, "row", "col"), P(None, "row", "col")),
        check_vma=False,
    )
```

```python
import functools

import jax
import jax.numpy as jnp
from jax import lax
from jax.experimental import pallas as pl
from jax.experimental.pallas import tpu as pltpu
from jax.sharding import PartitionSpec as P

B = 256
F32 = jnp.float32
BF16 = jnp.bfloat16


def split(value):
    high = value.astype(BF16)
    low = (value - high.astype(F32)).astype(BF16)
    return high, low


def dot(left, right):
    return jnp.dot(left, right, preferred_element_type=F32)


def line_gather(own, axis, n, cut):
    blocks = {0: own}
    for step in line_steps(n):
        perm = [(i, i ^ step) for i in range(n)]
        if step > 1:
            blocks |= {k ^ step: lax.ppermute(block, axis, perm) for k, block in blocks.items()}
    halves = {k ^ 1: cut(block) for k, block in blocks.items() if k > 0}
    halves = {k: [lax.ppermute(half, axis, perm) for half in pair] for k, pair in halves.items()}
    blocks[1] = lax.ppermute(own, axis, perm)
    return blocks, halves


def line_steps(n):
    steps = []
    while n > 1:
        n //= 2
        steps.append(n)
    return steps


def cut_kernel(block_ref, first_ref, second_ref):
    size = first_ref.shape[1]
    first_ref[...] = block_ref[:, :size, :]
    second_ref[...] = block_ref[:, size:, :]


def pack_kernel(*refs):
    (rows_ref, counts_ref), pieces = refs[:2], refs[2:-5]
    out_ref, high_ref, low_ref, rows_out, counts_out = refs[-5:]
    rows_out[...] = rows_ref[...]
    counts_out[...] = counts_ref[...]
    share_rows = pieces[0].shape[1]
    for place, piece in enumerate(pieces):
        here = slice(place * share_rows, (place + 1) * share_rows)
        out_ref[:, here, :] = piece[...]
        for part in range(2):
            high_ref[part, here, :], low_ref[part, here, :] = split(piece[part])


def add_slot(total, left, high_ref, low_ref, rows, cols):
    real, imag = total
    size = real.shape[0]
    both = left[0 : 2 * size]
    left = jnp.concatenate([both, left[2 * size : 4 * size], both], axis=1)

    def panel(part):
        high, low = high_ref[part, rows, cols], low_ref[part, rows, cols]
        return jnp.concatenate([high, high, low], axis=0)

    with_real, with_imag = dot(left, panel(0)), dot(left, panel(1))
    real = real - (with_real[:size] - with_imag[size:])
    imag = imag - (with_imag[:size] + with_real[size:])
    return real, imag


def row_is_live(rows_ref, counts_ref, member, block):
    return lax.fori_loop(
        0,
        counts_ref[0, member],
        lambda q, seen: seen | (rows_ref[member, q] == block),
        False,
    )


def blocks_kernel(*refs):
    pieces, out_ref = refs[:-1], refs[-1]
    rows = out_ref.shape[1] // 4
    first = 0
    for piece in pieces:
        size = piece.shape[1]
        for part in range(2):
            for scale, value in enumerate(split(piece[part])):
                start = (2 * scale + part) * rows + first % rows
                out_ref[first // rows, start : start + size, :] = value
        first += size


def add_product(member, q, top, place, high_ref, low_ref, out_ref):
    cols = slice(member * B, (member + 1) * B)
    rows = pl.ds(pl.multiple_of(q * B, B), B)
    total = out_ref[0, :, cols], out_ref[1, :, cols]
    total = add_slot(total, top[place], high_ref, low_ref, rows, cols)
    out_ref[0, :, cols], out_ref[1, :, cols] = total


def early_place(n_col, distance):
    return (distance % 2 == 0) | (distance == 1), jnp.where(distance == 1, n_col // 2, distance // 2)


def late_place(distance):
    return (distance - 3) // 2


def fetch(sems, *pairs):
    copies = [pltpu.make_async_copy(*pair, sems.at[k]) for k, pair in enumerate(pairs)]
    for copy in copies:
        copy.start()
    return copies


def turn(member, out_ref, sent, turned):
    chips, _, share, row_dev = turned.shape
    cols = slice(member * B, (member + 1) * B)
    for part in range(2):
        turned[:, part] = out_ref[part, :, cols].T.reshape(chips, share, row_dev)
    for step in range(chips):
        sent[step][member] = turned[(lax.axis_index("row") // 2) ^ step]


def early_kernel(n_col, share_rows, near, far, *refs):
    rows_hbm, counts_hbm, top, own, mate, near_high, near_low, near_mates = refs[:8]
    far_panels, refs = refs[8 : 8 + 2 * len(far)], refs[8 + 2 * len(far) :]
    high_ref, low_ref, late_ref, out_ref = refs[:4]
    sent, (turned, rows_ref, counts_ref, sems) = refs[4:-4], refs[-4:]
    leaves, slots = rows_ref.shape
    me = lax.axis_index("row")
    my_block = (me * out_ref.shape[1]) // B
    my_col = lax.axis_index("col")
    arrivals = fetch(sems, (rows_hbm, rows_ref), (counts_hbm, counts_ref))

    def put(owner, high, low):
        rows = pl.ds(pl.multiple_of(owner * share_rows, share_rows), share_rows)
        high_ref[:, rows, :], low_ref[:, rows, :] = high, low

    put(me, *split(own[...]))
    put(me ^ 1, *split(mate[...]))
    for place, step in enumerate(near):
        here = slice(place * share_rows, (place + 1) * share_rows)
        put(me ^ step, near_high[:, here, :], near_low[:, here, :])
        put(me ^ step ^ 1, *split(near_mates[:, here, :]))
    for place, step in enumerate(far):
        put(me ^ step, *split(far_panels[2 * place][...]))
        put(me ^ step ^ 1, *split(far_panels[2 * place + 1][...]))
    out_ref[...] = jnp.zeros(out_ref.shape, F32)
    for copy in arrivals:
        copy.wait()
    here = [lax.broadcasted_iota(jnp.int32, (leaves, slots), axis) for axis in range(2)]
    late_ref[...] = jnp.zeros((leaves, slots), jnp.int32)
    for member in range(leaves):

        def slot(q, carry):
            distance = my_col ^ rows_ref[member, q]
            held, place = early_place(n_col, distance)

            @pl.when(held)
            def _():
                add_product(member, q, top, place, high_ref, low_ref, out_ref)

            @pl.when(jnp.logical_not(held))
            def _():
                mark = (here[0] == member) & (here[1] == q)
                late_ref[...] = jnp.where(mark, 1 + late_place(distance), late_ref[...])

            return carry

        live = row_is_live(rows_ref, counts_ref, member, my_block)
        lax.fori_loop(0, jnp.where(live, counts_ref[0, member], 0), slot, 0)
        turn(member, out_ref, sent, turned)


def select_kernel(chips, late_ref, top, high_ref, low_ref, early_ref, *refs):
    early_sent, out_ref, sent, turned = refs[:chips], refs[chips], refs[chips + 1 : -1], refs[-1]
    leaves, slots = late_ref.shape
    out_ref[...] = early_ref[...]
    for step in range(chips):
        sent[step][...] = early_sent[step][...]
    for member in range(leaves):
        marks = late_ref[member : member + 1, :]

        @pl.when(jnp.max(marks) > 0)
        def _():
            def slot(q, carry):
                lane = lax.broadcasted_iota(jnp.int32, marks.shape, 1)
                mark = jnp.max(jnp.where(lane == q, marks, 0))

                @pl.when(mark > 0)
                def _():
                    add_product(member, q, top, mark - 1, high_ref, low_ref, out_ref)

                return carry

            lax.fori_loop(0, slots, slot, 0)
            turn(member, out_ref, sent, turned)


def write_kernel(value_ref, out_ref):
    out_ref[...] = value_ref[...]


def diagonal_kernel(rows_ref, *refs):
    pieces, (high_ref, low_ref, diag_ref, keep_ref, give_ref, whole) = refs[:-6], refs[-6:]
    leaves, slots = rows_ref.shape
    _, _, chip_share, row_dev = pieces[0].shape
    share = keep_ref.shape[1]
    me = lax.axis_index("row")
    core = me % 2

    def pick(member, q):
        block = jnp.broadcast_to(rows_ref[member : member + 1, q : q + 1], (2 * chip_share, row_dev))
        picked = jnp.zeros(block.shape, F32)
        for step, piece in enumerate(reversed(pieces)):
            here = block == (me // 2) ^ step
            picked = jnp.where(here, piece[member].reshape(block.shape), picked)
        return jnp.concatenate(split(picked), axis=0)

    for member in range(leaves):
        cols = slice(member * B, (member + 1) * B)
        left = jnp.concatenate([pick(member, q) for q in range(slots)], axis=1)
        both = left[: 2 * chip_share]

        def panel(ref, part):
            starts = [pl.multiple_of(q * B + core * row_dev, row_dev) for q in range(slots)]
            return jnp.concatenate(
                [ref[part, pl.ds(start, row_dev), cols] for start in starts], axis=0
            )

        with_real = dot(left, panel(high_ref, 0))
        with_imag = dot(left, panel(high_ref, 1))
        with_real = with_real[: 2 * chip_share] + with_real[2 * chip_share :]
        with_imag = with_imag[: 2 * chip_share] + with_imag[2 * chip_share :]
        with_real += dot(both, panel(low_ref, 0))
        with_imag += dot(both, panel(low_ref, 1))
        whole[0, :, cols] = with_real[:chip_share] - with_imag[chip_share:]
        whole[1, :, cols] = with_imag[:chip_share] + with_real[chip_share:]
    mine = pl.ds(pl.multiple_of(core * share, share), share)
    other = pl.ds(pl.multiple_of((1 - core) * share, share), share)
    keep_ref[...] = diag_ref[...] - whole[:, mine, :]
    give_ref[...] = whole[:, other, :]


def subtract_kernel(left_ref, right_ref, out_ref):
    out_ref[...] = left_ref[...] - right_ref[...]


def on_device(n_row, n_col, top_inverse, panel, leaf_rows, leaf_counts, diag_inverse):
    vmem = pl.BlockSpec(memory_space=pltpu.VMEM)
    hbm = pl.BlockSpec(memory_space=pl.ANY)
    _, row_dev, _ = top_inverse.shape
    _, panel_rows, columns = panel.shape
    leaves = columns // B
    chips = n_row // 2
    chip_share = B // chips
    depth = n_row * panel_rows
    params = pltpu.CompilerParams(vmem_limit_bytes=max(16 << 20, 40 * depth * columns))

    def cut(block):
        sizes = 3 * row_dev // 8, row_dev - 3 * row_dev // 8
        return pl.pallas_call(
            cut_kernel,
            out_shape=[jax.ShapeDtypeStruct((2, size, B), F32) for size in sizes],
            in_specs=[vmem],
            out_specs=[vmem] * 2,
            compiler_params=params,
            name="cut_rows",
        )(block)

    blocks, halves = line_gather(top_inverse, "col", n_col, cut)

    swap = [(i, i ^ 1) for i in range(n_row)]
    like = {
        step: lax.ppermute(panel, "row", [(i, i ^ step) for i in range(n_row)])
        for step in range(2, n_row, 2)
    }
    near = [step for step in like if step & -step == step]
    far = [step for step in like if step not in near]
    packed = (2, len(near) * panel_rows, columns)
    leaf_counts = leaf_counts[None, :]
    mine, near_high, near_low, leaf_rows, leaf_counts = pl.pallas_call(
        pack_kernel,
        out_shape=[jax.ShapeDtypeStruct(packed, dtype) for dtype in (F32, BF16, BF16)]
        + [jax.ShapeDtypeStruct(value.shape, value.dtype) for value in (leaf_rows, leaf_counts)],
        in_specs=[vmem] * (2 + len(near)),
        out_specs=[vmem] * 5,
        compiler_params=params,
        name="pack_panel",
    )(leaf_rows, leaf_counts, *[like[step] for step in near])
    late_panel, _ = lax.optimization_barrier((panel, [like[step] for step in near]))
    mate = lax.ppermute(late_panel, "row", swap)
    near_mates = lax.ppermute(mine, "row", swap)
    far_panels = []
    for step in far:
        far_panels += [like[step], lax.ppermute(like[step], "row", swap)]

    early_blocks = [blocks[k] for k in range(0, n_col, 2)] + [blocks[1]]
    firsts = [halves[k][0] for k in range(3, n_col, 2)]
    early_blocks, firsts = lax.optimization_barrier((early_blocks, firsts))
    late_blocks = [half for k in range(3, n_col, 2) for half in halves[k]]

    def split_blocks(values):
        count = sum(value.shape[1] for value in values) // row_dev
        return pl.pallas_call(
            blocks_kernel,
            out_shape=jax.ShapeDtypeStruct((count, 4 * row_dev, B), BF16),
            in_specs=[vmem] * len(values),
            out_specs=vmem,
            compiler_params=params,
            cost_estimate=pl.CostEstimate(
                flops=10**11, bytes_accessed=10**9, transcendentals=0
            ),
            name="split_blocks",
        )(*values)

    indices = [
        pltpu.SMEM(leaf_rows.shape, leaf_rows.dtype),
        pltpu.SMEM(leaf_counts.shape, leaf_counts.dtype),
        pltpu.SemaphoreType.DMA((2,)),
    ]
    rows_shape = jax.ShapeDtypeStruct((2, row_dev, columns), F32)
    piece = jax.ShapeDtypeStruct((leaves, 2, chip_share, row_dev), F32)
    scratch = [pltpu.VMEM((chips,) + piece.shape[1:], F32)] + indices
    high, low, late, *early = pl.pallas_call(
        functools.partial(early_kernel, n_col, panel_rows, near, far),
        out_shape=[jax.ShapeDtypeStruct((2, depth, columns), BF16)] * 2
        + [jax.ShapeDtypeStruct(leaf_rows.shape, jnp.int32), rows_shape]
        + [piece] * chips,
        in_specs=[hbm, hbm] + [vmem] * (6 + len(far_panels)),
        out_specs=[vmem] * (4 + chips),
        scratch_shapes=scratch,
        compiler_params=params,
        name="early_rows",
    )(
        leaf_rows,
        leaf_counts,
        split_blocks(early_blocks),
        panel,
        mate,
        near_high,
        near_low,
        near_mates,
        *far_panels,
    )
    early, late_blocks = lax.optimization_barrier((early, late_blocks))

    selected, *sent = pl.pallas_call(
        functools.partial(select_kernel, chips),
        out_shape=[rows_shape] + [piece] * chips,
        in_specs=[vmem] * (5 + chips),
        out_specs=[vmem] * (1 + chips),
        scratch_shapes=scratch[:1],
        compiler_params=params,
        name="selected_rows",
    )(late, split_blocks(late_blocks), high, low, *early)

    for step in range(chips - 1, 0, -1):
        perm = [(i, i ^ (2 * step)) for i in range(n_row)]
        sent[step] = lax.ppermute(sent[step], "row", perm)
    selected = pl.pallas_call(
        write_kernel,
        out_shape=jax.ShapeDtypeStruct(selected.shape, F32),
        in_specs=[vmem],
        out_specs=vmem,
        compiler_params=params,
        name="write_rows",
    )(selected)
    selected, sent = lax.optimization_barrier((selected, sent[::-1]))

    keep, give = pl.pallas_call(
        diagonal_kernel,
        out_shape=[jax.ShapeDtypeStruct(diag_inverse.shape, F32)] * 2,
        in_specs=[vmem] * (chips + 4),
        out_specs=[vmem] * 2,
        scratch_shapes=[pltpu.VMEM((2, chip_share, columns), F32)],
        compiler_params=params,
        cost_estimate=pl.CostEstimate(
            flops=12 * chip_share * depth * columns,
            bytes_accessed=8 * (depth + 2 * chip_share) * columns,
            transcendentals=0,
        ),
        name="diagonal_part",
    )(leaf_rows, *sent, high, low, diag_inverse)
    give = lax.ppermute(give, "row", [(i, i ^ 1) for i in range(n_row)])
    diagonal = pl.pallas_call(
        subtract_kernel,
        out_shape=jax.ShapeDtypeStruct(diag_inverse.shape, F32),
        in_specs=[vmem] * 2,
        out_specs=vmem,
        compiler_params=params,
        name="diagonal_rows",
    )(keep, give)
    return selected, diagonal


def solution(mesh):
    return jax.shard_map(
        functools.partial(on_device, mesh.shape["row"], mesh.shape["col"]),
        mesh=mesh,
        in_specs=(
            P(None, "row", "col"),
            P(None, "row", "col"),
            P("col", None),
            P("col"),
            P(None, "row", "col"),
        ),
        out_specs=(P(None, "row", "col"), P(None, "row", "col")),
        check_vma=False,
    )
```

```python
import functools

import jax
import jax.numpy as jnp
from jax import lax
from jax.experimental import pallas as pl
from jax.experimental.pallas import tpu as pltpu
from jax.sharding import PartitionSpec as P

B = 256
F32 = jnp.float32
BF16 = jnp.bfloat16


def split(value):
    high = value.astype(BF16)
    low = (value - high.astype(F32)).astype(BF16)
    return high, low


def dot(left, right):
    return jnp.dot(left, right, preferred_element_type=F32)


def line_gather(own, axis, n, cut):
    blocks = {0: own}
    for step in line_steps(n):
        perm = [(i, i ^ step) for i in range(n)]
        if step > 1:
            blocks |= {k ^ step: lax.ppermute(block, axis, perm) for k, block in blocks.items()}
    halves = {k ^ 1: cut(block) for k, block in blocks.items() if k > 0}
    halves = {k: [lax.ppermute(half, axis, perm) for half in pair] for k, pair in halves.items()}
    blocks[1] = lax.ppermute(own, axis, perm)
    return blocks, halves


def line_steps(n):
    steps = []
    while n > 1:
        n //= 2
        steps.append(n)
    return steps


def cut_kernel(block_ref, first_ref, second_ref):
    size = first_ref.shape[1]
    first_ref[...] = block_ref[:, :size, :]
    second_ref[...] = block_ref[:, size:, :]


def pack_kernel(*refs):
    (rows_ref, counts_ref), pieces = refs[:2], refs[2:-5]
    out_ref, high_ref, low_ref, rows_out, counts_out = refs[-5:]
    rows_out[...] = rows_ref[...]
    counts_out[...] = counts_ref[...]
    share_rows = pieces[0].shape[1]
    for place, piece in enumerate(pieces):
        here = slice(place * share_rows, (place + 1) * share_rows)
        out_ref[:, here, :] = piece[...]
        for part in range(2):
            high_ref[part, here, :], low_ref[part, here, :] = split(piece[part])


def add_slot(total, left, high_ref, low_ref, rows, cols):
    real, imag = total
    size = real.shape[0]
    both = left[0 : 2 * size]
    left = jnp.concatenate([both, left[2 * size : 4 * size], both], axis=1)

    def panel(part):
        high, low = high_ref[part, rows, cols], low_ref[part, rows, cols]
        return jnp.concatenate([high, high, low], axis=0)

    with_real, with_imag = dot(left, panel(0)), dot(left, panel(1))
    real = real - (with_real[:size] - with_imag[size:])
    imag = imag - (with_imag[:size] + with_real[size:])
    return real, imag


def row_is_live(rows_ref, counts_ref, member, block):
    return lax.fori_loop(
        0,
        counts_ref[0, member],
        lambda q, seen: seen | (rows_ref[member, q] == block),
        False,
    )


def blocks_kernel(*refs):
    pieces, out_ref = refs[:-1], refs[-1]
    rows = out_ref.shape[1] // 4
    first = 0
    for piece in pieces:
        size = piece.shape[1]
        for part in range(2):
            for scale, value in enumerate(split(piece[part])):
                start = (2 * scale + part) * rows + first % rows
                out_ref[first // rows, start : start + size, :] = value
        first += size


def add_product(member, q, top, place, high_ref, low_ref, out_ref):
    cols = slice(member * B, (member + 1) * B)
    rows = pl.ds(pl.multiple_of(q * B, B), B)
    total = out_ref[0, :, cols], out_ref[1, :, cols]
    total = add_slot(total, top[place], high_ref, low_ref, rows, cols)
    out_ref[0, :, cols], out_ref[1, :, cols] = total


def early_place(n_col, distance):
    return (distance % 2 == 0) | (distance == 1), jnp.where(distance == 1, n_col // 2, distance // 2)


def late_place(distance):
    return (distance - 3) // 2


def fetch(sems, *pairs):
    copies = [pltpu.make_async_copy(*pair, sems.at[k]) for k, pair in enumerate(pairs)]
    for copy in copies:
        copy.start()
    return copies


def turn(member, out_ref, sent, turned):
    chips, _, share, row_dev = turned.shape
    cols = slice(member * B, (member + 1) * B)
    for part in range(2):
        turned[:, part] = out_ref[part, :, cols].T.reshape(chips, share, row_dev)
    for step in range(chips):
        sent[step][member] = turned[(lax.axis_index("row") // 2) ^ step]


def early_kernel(n_col, share_rows, near, far, *refs):
    rows_hbm, counts_hbm, top, own, mate, near_high, near_low, near_mates = refs[:8]
    far_panels, refs = refs[8 : 8 + 2 * len(far)], refs[8 + 2 * len(far) :]
    high_ref, low_ref, late_ref, out_ref = refs[:4]
    sent, (turned, rows_ref, counts_ref, sems) = refs[4:-4], refs[-4:]
    leaves, slots = rows_ref.shape
    me = lax.axis_index("row")
    my_block = (me * out_ref.shape[1]) // B
    my_col = lax.axis_index("col")
    arrivals = fetch(sems, (rows_hbm, rows_ref), (counts_hbm, counts_ref))

    def put(owner, high, low):
        rows = pl.ds(pl.multiple_of(owner * share_rows, share_rows), share_rows)
        high_ref[:, rows, :], low_ref[:, rows, :] = high, low

    put(me, *split(own[...]))
    put(me ^ 1, *split(mate[...]))
    for place, step in enumerate(near):
        here = slice(place * share_rows, (place + 1) * share_rows)
        put(me ^ step, near_high[:, here, :], near_low[:, here, :])
        put(me ^ step ^ 1, *split(near_mates[:, here, :]))
    for place, step in enumerate(far):
        put(me ^ step, *split(far_panels[2 * place][...]))
        put(me ^ step ^ 1, *split(far_panels[2 * place + 1][...]))
    out_ref[...] = jnp.zeros(out_ref.shape, F32)
    for copy in arrivals:
        copy.wait()
    here = [lax.broadcasted_iota(jnp.int32, (leaves, slots), axis) for axis in range(2)]
    late_ref[...] = jnp.zeros((leaves, slots), jnp.int32)
    for member in range(leaves):

        def slot(q, carry):
            distance = my_col ^ rows_ref[member, q]
            held, place = early_place(n_col, distance)

            @pl.when(held)
            def _():
                add_product(member, q, top, place, high_ref, low_ref, out_ref)

            @pl.when(jnp.logical_not(held))
            def _():
                mark = (here[0] == member) & (here[1] == q)
                late_ref[...] = jnp.where(mark, 1 + late_place(distance), late_ref[...])

            return carry

        live = row_is_live(rows_ref, counts_ref, member, my_block)
        lax.fori_loop(0, jnp.where(live, counts_ref[0, member], 0), slot, 0)
        turn(member, out_ref, sent, turned)


def select_kernel(chips, late_ref, top, high_ref, low_ref, early_ref, *refs):
    early_sent, out_ref, sent, turned = refs[:chips], refs[chips], refs[chips + 1 : -1], refs[-1]
    leaves, slots = late_ref.shape
    out_ref[...] = early_ref[...]
    for step in range(chips):
        sent[step][...] = early_sent[step][...]
    for member in range(leaves):
        marks = late_ref[member : member + 1, :]

        @pl.when(jnp.max(marks) > 0)
        def _():
            def slot(q, carry):
                lane = lax.broadcasted_iota(jnp.int32, marks.shape, 1)
                mark = jnp.max(jnp.where(lane == q, marks, 0))

                @pl.when(mark > 0)
                def _():
                    add_product(member, q, top, mark - 1, high_ref, low_ref, out_ref)

                return carry

            lax.fori_loop(0, slots, slot, 0)
            turn(member, out_ref, sent, turned)


def write_kernel(value_ref, out_ref):
    out_ref[...] = value_ref[...]


def diagonal_kernel(rows_ref, *refs):
    pieces, (high_ref, low_ref, diag_ref, keep_ref, give_ref, whole) = refs[:-6], refs[-6:]
    leaves, slots = rows_ref.shape
    _, _, chip_share, row_dev = pieces[0].shape
    share = keep_ref.shape[1]
    me = lax.axis_index("row")
    core = me % 2

    def pick(member, q):
        block = jnp.broadcast_to(rows_ref[member : member + 1, q : q + 1], (2 * chip_share, row_dev))
        picked = jnp.zeros(block.shape, F32)
        for step, piece in enumerate(reversed(pieces)):
            here = block == (me // 2) ^ step
            picked = jnp.where(here, piece[member].reshape(block.shape), picked)
        return jnp.concatenate(split(picked), axis=0)

    for member in range(leaves):
        cols = slice(member * B, (member + 1) * B)
        left = jnp.concatenate([pick(member, q) for q in range(slots)], axis=1)
        both = left[: 2 * chip_share]

        def panel(ref, part):
            starts = [pl.multiple_of(q * B + core * row_dev, row_dev) for q in range(slots)]
            return jnp.concatenate(
                [ref[part, pl.ds(start, row_dev), cols] for start in starts], axis=0
            )

        with_real = dot(left, panel(high_ref, 0))
        with_imag = dot(left, panel(high_ref, 1))
        with_real = with_real[: 2 * chip_share] + with_real[2 * chip_share :]
        with_imag = with_imag[: 2 * chip_share] + with_imag[2 * chip_share :]
        with_real += dot(both, panel(low_ref, 0))
        with_imag += dot(both, panel(low_ref, 1))
        whole[0, :, cols] = with_real[:chip_share] - with_imag[chip_share:]
        whole[1, :, cols] = with_imag[:chip_share] + with_real[chip_share:]
    mine = pl.ds(pl.multiple_of(core * share, share), share)
    other = pl.ds(pl.multiple_of((1 - core) * share, share), share)
    keep_ref[...] = diag_ref[...] - whole[:, mine, :]
    give_ref[...] = whole[:, other, :]


def subtract_kernel(left_ref, right_ref, out_ref):
    out_ref[...] = left_ref[...] - right_ref[...]


def on_device(n_row, n_col, top_inverse, panel, leaf_rows, leaf_counts, diag_inverse):
    vmem = pl.BlockSpec(memory_space=pltpu.VMEM)
    hbm = pl.BlockSpec(memory_space=pl.ANY)
    _, row_dev, _ = top_inverse.shape
    _, panel_rows, columns = panel.shape
    leaves = columns // B
    chips = n_row // 2
    chip_share = B // chips
    depth = n_row * panel_rows
    params = pltpu.CompilerParams(vmem_limit_bytes=max(16 << 20, 40 * depth * columns))

    def cut(block):
        sizes = 3 * row_dev // 8, row_dev - 3 * row_dev // 8
        return pl.pallas_call(
            cut_kernel,
            out_shape=[jax.ShapeDtypeStruct((2, size, B), F32) for size in sizes],
            in_specs=[vmem],
            out_specs=[vmem] * 2,
            compiler_params=params,
            name="cut_rows",
        )(block)

    blocks, halves = line_gather(top_inverse, "col", n_col, cut)

    swap = [(i, i ^ 1) for i in range(n_row)]
    like = {
        step: lax.ppermute(panel, "row", [(i, i ^ step) for i in range(n_row)])
        for step in range(2, n_row, 2)
    }
    near = [step for step in like if step & -step == step]
    far = [step for step in like if step not in near]
    like, _ = lax.optimization_barrier((like, [blocks[k] for k in blocks if k > 0]))
    packed = (2, len(near) * panel_rows, columns)
    leaf_counts = leaf_counts[None, :]
    mine, near_high, near_low, leaf_rows, leaf_counts = pl.pallas_call(
        pack_kernel,
        out_shape=[jax.ShapeDtypeStruct(packed, dtype) for dtype in (F32, BF16, BF16)]
        + [jax.ShapeDtypeStruct(value.shape, value.dtype) for value in (leaf_rows, leaf_counts)],
        in_specs=[vmem] * (2 + len(near)),
        out_specs=[vmem] * 5,
        compiler_params=params,
        name="pack_panel",
    )(leaf_rows, leaf_counts, *[like[step] for step in near])
    late_panel, _ = lax.optimization_barrier((panel, [like[step] for step in near]))
    mate = lax.ppermute(late_panel, "row", swap)
    near_mates = lax.ppermute(mine, "row", swap)
    far_panels = []
    for step in far:
        far_panels += [like[step], lax.ppermute(like[step], "row", swap)]

    early_blocks = [blocks[k] for k in range(0, n_col, 2)] + [blocks[1]]
    firsts = [halves[k][0] for k in range(3, n_col, 2)]
    early_blocks, firsts = lax.optimization_barrier((early_blocks, firsts))
    late_blocks = [half for k in range(3, n_col, 2) for half in halves[k]]

    def split_blocks(values):
        count = sum(value.shape[1] for value in values) // row_dev
        return pl.pallas_call(
            blocks_kernel,
            out_shape=jax.ShapeDtypeStruct((count, 4 * row_dev, B), BF16),
            in_specs=[vmem] * len(values),
            out_specs=vmem,
            compiler_params=params,
            cost_estimate=pl.CostEstimate(
                flops=10**11, bytes_accessed=10**9, transcendentals=0
            ),
            name="split_blocks",
        )(*values)

    indices = [
        pltpu.SMEM(leaf_rows.shape, leaf_rows.dtype),
        pltpu.SMEM(leaf_counts.shape, leaf_counts.dtype),
        pltpu.SemaphoreType.DMA((2,)),
    ]
    rows_shape = jax.ShapeDtypeStruct((2, row_dev, columns), F32)
    piece = jax.ShapeDtypeStruct((leaves, 2, chip_share, row_dev), F32)
    scratch = [pltpu.VMEM((chips,) + piece.shape[1:], F32)] + indices
    high, low, late, *early = pl.pallas_call(
        functools.partial(early_kernel, n_col, panel_rows, near, far),
        out_shape=[jax.ShapeDtypeStruct((2, depth, columns), BF16)] * 2
        + [jax.ShapeDtypeStruct(leaf_rows.shape, jnp.int32), rows_shape]
        + [piece] * chips,
        in_specs=[hbm, hbm] + [vmem] * (6 + len(far_panels)),
        out_specs=[vmem] * (4 + chips),
        scratch_shapes=scratch,
        compiler_params=params,
        name="early_rows",
    )(
        leaf_rows,
        leaf_counts,
        split_blocks(early_blocks),
        panel,
        mate,
        near_high,
        near_low,
        near_mates,
        *far_panels,
    )
    early, late_blocks = lax.optimization_barrier((early, late_blocks))

    selected, *sent = pl.pallas_call(
        functools.partial(select_kernel, chips),
        out_shape=[rows_shape] + [piece] * chips,
        in_specs=[vmem] * (5 + chips),
        out_specs=[vmem] * (1 + chips),
        scratch_shapes=scratch[:1],
        compiler_params=params,
        name="selected_rows",
    )(late, split_blocks(late_blocks), high, low, *early)

    for step in range(chips - 1, 0, -1):
        perm = [(i, i ^ (2 * step)) for i in range(n_row)]
        sent[step] = lax.ppermute(sent[step], "row", perm)
    selected = pl.pallas_call(
        write_kernel,
        out_shape=jax.ShapeDtypeStruct(selected.shape, F32),
        in_specs=[vmem],
        out_specs=vmem,
        compiler_params=params,
        name="write_rows",
    )(selected)
    selected, sent = lax.optimization_barrier((selected, sent[::-1]))

    keep, give = pl.pallas_call(
        diagonal_kernel,
        out_shape=[jax.ShapeDtypeStruct(diag_inverse.shape, F32)] * 2,
        in_specs=[vmem] * (chips + 4),
        out_specs=[vmem] * 2,
        scratch_shapes=[pltpu.VMEM((2, chip_share, columns), F32)],
        compiler_params=params,
        cost_estimate=pl.CostEstimate(
            flops=12 * chip_share * depth * columns,
            bytes_accessed=8 * (depth + 2 * chip_share) * columns,
            transcendentals=0,
        ),
        name="diagonal_part",
    )(leaf_rows, *sent, high, low, diag_inverse)
    give = lax.ppermute(give, "row", [(i, i ^ 1) for i in range(n_row)])
    diagonal = pl.pallas_call(
        subtract_kernel,
        out_shape=jax.ShapeDtypeStruct(diag_inverse.shape, F32),
        in_specs=[vmem] * 2,
        out_specs=vmem,
        compiler_params=params,
        name="diagonal_rows",
    )(keep, give)
    return selected, diagonal


def solution(mesh):
    return jax.shard_map(
        functools.partial(on_device, mesh.shape["row"], mesh.shape["col"]),
        mesh=mesh,
        in_specs=(
            P(None, "row", "col"),
            P(None, "row", "col"),
            P("col", None),
            P("col"),
            P(None, "row", "col"),
        ),
        out_specs=(P(None, "row", "col"), P(None, "row", "col")),
        check_vma=False,
    )
```

```python
import functools

import jax
import jax.numpy as jnp
from jax import lax
from jax.experimental import pallas as pl
from jax.experimental.pallas import tpu as pltpu
from jax.sharding import PartitionSpec as P

B = 256
F32 = jnp.float32
BF16 = jnp.bfloat16


def split(value):
    high = value.astype(BF16)
    low = (value - high.astype(F32)).astype(BF16)
    return high, low


def dot(left, right):
    return jnp.dot(left, right, preferred_element_type=F32)


def line_gather(own, axis, n, cut):
    blocks = {0: own}
    for step in line_steps(n):
        perm = [(i, i ^ step) for i in range(n)]
        if step > 1:
            blocks |= {k ^ step: lax.ppermute(block, axis, perm) for k, block in blocks.items()}
    halves = {k ^ 1: cut(block) for k, block in blocks.items() if k > 0}
    halves = {k: [lax.ppermute(half, axis, perm) for half in pair] for k, pair in halves.items()}
    blocks[1] = lax.ppermute(own, axis, perm)
    return blocks, halves


def line_steps(n):
    steps = []
    while n > 1:
        n //= 2
        steps.append(n)
    return steps


def cut_kernel(block_ref, first_ref, second_ref):
    size = first_ref.shape[1]
    first_ref[...] = block_ref[:, :size, :]
    second_ref[...] = block_ref[:, size:, :]


def pack_kernel(*refs):
    (rows_ref, counts_ref), pieces = refs[:2], refs[2:-5]
    out_ref, high_ref, low_ref, rows_out, counts_out = refs[-5:]
    rows_out[...] = rows_ref[...]
    counts_out[...] = counts_ref[...]
    share_rows = pieces[0].shape[1]
    for place, piece in enumerate(pieces):
        here = slice(place * share_rows, (place + 1) * share_rows)
        out_ref[:, here, :] = piece[...]
        for part in range(2):
            high_ref[part, here, :], low_ref[part, here, :] = split(piece[part])


def add_slot(total, left, high_ref, low_ref, rows, cols):
    real, imag = total
    size = real.shape[0]
    both = left[0 : 2 * size]
    left = jnp.concatenate([both, left[2 * size : 4 * size], both], axis=1)

    def panel(part):
        high, low = high_ref[part, rows, cols], low_ref[part, rows, cols]
        return jnp.concatenate([high, high, low], axis=0)

    with_real, with_imag = dot(left, panel(0)), dot(left, panel(1))
    real = real - (with_real[:size] - with_imag[size:])
    imag = imag - (with_imag[:size] + with_real[size:])
    return real, imag


def row_is_live(rows_ref, counts_ref, member, block):
    return lax.fori_loop(
        0,
        counts_ref[0, member],
        lambda q, seen: seen | (rows_ref[member, q] == block),
        False,
    )


def blocks_kernel(*refs):
    pieces, out_ref = refs[:-1], refs[-1]
    rows = out_ref.shape[1] // 4
    first = 0
    for piece in pieces:
        size = piece.shape[1]
        for part in range(2):
            for scale, value in enumerate(split(piece[part])):
                start = (2 * scale + part) * rows + first % rows
                out_ref[first // rows, start : start + size, :] = value
        first += size


def add_product(member, q, top, place, high_ref, low_ref, out_ref):
    cols = slice(member * B, (member + 1) * B)
    rows = pl.ds(pl.multiple_of(q * B, B), B)
    total = out_ref[0, :, cols], out_ref[1, :, cols]
    total = add_slot(total, top[place], high_ref, low_ref, rows, cols)
    out_ref[0, :, cols], out_ref[1, :, cols] = total


def early_place(n_col, distance):
    return (distance % 2 == 0) | (distance == 1), jnp.where(distance == 1, n_col // 2, distance // 2)


def late_place(distance):
    return (distance - 3) // 2


def fetch(sems, *pairs):
    copies = [pltpu.make_async_copy(*pair, sems.at[k]) for k, pair in enumerate(pairs)]
    for copy in copies:
        copy.start()
    return copies


def turn(member, out_ref, sent, turned):
    chips, _, share, row_dev = turned.shape
    cols = slice(member * B, (member + 1) * B)
    for part in range(2):
        turned[:, part] = out_ref[part, :, cols].T.reshape(chips, share, row_dev)
    for step in range(chips):
        sent[step][member] = turned[(lax.axis_index("row") // 2) ^ step]


def early_kernel(n_col, share_rows, near, far, *refs):
    rows_hbm, counts_hbm, top, own, mate, near_high, near_low, near_mates = refs[:8]
    far_panels, refs = refs[8 : 8 + 2 * len(far)], refs[8 + 2 * len(far) :]
    high_ref, low_ref, late_ref, out_ref = refs[:4]
    sent, (turned, rows_ref, counts_ref, sems) = refs[4:-4], refs[-4:]
    leaves, slots = rows_ref.shape
    me = lax.axis_index("row")
    my_block = (me * out_ref.shape[1]) // B
    my_col = lax.axis_index("col")
    arrivals = fetch(sems, (rows_hbm, rows_ref), (counts_hbm, counts_ref))

    def put(owner, high, low):
        rows = pl.ds(pl.multiple_of(owner * share_rows, share_rows), share_rows)
        high_ref[:, rows, :], low_ref[:, rows, :] = high, low

    put(me, *split(own[...]))
    put(me ^ 1, *split(mate[...]))
    for place, step in enumerate(near):
        here = slice(place * share_rows, (place + 1) * share_rows)
        put(me ^ step, near_high[:, here, :], near_low[:, here, :])
        put(me ^ step ^ 1, *split(near_mates[:, here, :]))
    for place, step in enumerate(far):
        put(me ^ step, *split(far_panels[2 * place][...]))
        put(me ^ step ^ 1, *split(far_panels[2 * place + 1][...]))
    out_ref[...] = jnp.zeros(out_ref.shape, F32)
    for copy in arrivals:
        copy.wait()
    here = [lax.broadcasted_iota(jnp.int32, (leaves, slots), axis) for axis in range(2)]
    late_ref[...] = jnp.zeros((leaves, slots), jnp.int32)
    for member in range(leaves):

        def slot(q, carry):
            distance = my_col ^ rows_ref[member, q]
            held, place = early_place(n_col, distance)

            @pl.when(held)
            def _():
                add_product(member, q, top, place, high_ref, low_ref, out_ref)

            @pl.when(jnp.logical_not(held))
            def _():
                mark = (here[0] == member) & (here[1] == q)
                late_ref[...] = jnp.where(mark, 1 + late_place(distance), late_ref[...])

            return carry

        live = row_is_live(rows_ref, counts_ref, member, my_block)
        lax.fori_loop(0, jnp.where(live, counts_ref[0, member], 0), slot, 0)
        turn(member, out_ref, sent, turned)


def select_kernel(chips, late_ref, top, high_ref, low_ref, early_ref, *refs):
    early_sent, out_ref, sent, turned = refs[:chips], refs[chips], refs[chips + 1 : -1], refs[-1]
    leaves, slots = late_ref.shape

    def last_marked(member, below):
        marks = late_ref[member : member + 1, :]
        lane = lax.broadcasted_iota(jnp.int32, marks.shape, 1)
        return jnp.max(jnp.where((marks > 0) & (lane < below), lane * 256 + marks, -1))

    found = [last_marked(member, slots) for member in range(leaves)]
    out_ref[...] = early_ref[...]
    for step in range(chips):
        sent[step][...] = early_sent[step][...]
    for member in range(leaves):

        def slot(_, code):
            @pl.when(code >= 0)
            def _():
                add_product(member, code >> 8, top, (code & 255) - 1, high_ref, low_ref, out_ref)

            return last_marked(member, code >> 8)

        @pl.when(found[member] >= 0)
        def _():
            if top.shape[0] == 1:
                add_product(member, found[member] >> 8, top, 0, high_ref, low_ref, out_ref)
            else:
                lax.fori_loop(0, top.shape[0], slot, found[member])
            turn(member, out_ref, sent, turned)


def write_kernel(value_ref, out_ref):
    out_ref[...] = value_ref[...]


def diagonal_kernel(rows_ref, *refs):
    pieces, (high_ref, low_ref, diag_ref, keep_ref, give_ref, whole) = refs[:-6], refs[-6:]
    leaves, slots = rows_ref.shape
    _, _, chip_share, row_dev = pieces[0].shape
    share = keep_ref.shape[1]
    me = lax.axis_index("row")
    core = me % 2

    def pick(member, q):
        block = jnp.broadcast_to(rows_ref[member : member + 1, q : q + 1], (2 * chip_share, row_dev))
        picked = jnp.zeros(block.shape, F32)
        for step, piece in enumerate(reversed(pieces)):
            here = block == (me // 2) ^ step
            picked = jnp.where(here, piece[member].reshape(block.shape), picked)
        return jnp.concatenate(split(picked), axis=0)

    for member in range(leaves):
        cols = slice(member * B, (member + 1) * B)
        left = jnp.concatenate([pick(member, q) for q in range(slots)], axis=1)
        both = left[: 2 * chip_share]

        def panel(ref, part):
            starts = [pl.multiple_of(q * B + core * row_dev, row_dev) for q in range(slots)]
            return jnp.concatenate(
                [ref[part, pl.ds(start, row_dev), cols] for start in starts], axis=0
            )

        with_real = dot(left, panel(high_ref, 0))
        with_imag = dot(left, panel(high_ref, 1))
        with_real = with_real[: 2 * chip_share] + with_real[2 * chip_share :]
        with_imag = with_imag[: 2 * chip_share] + with_imag[2 * chip_share :]
        with_real += dot(both, panel(low_ref, 0))
        with_imag += dot(both, panel(low_ref, 1))
        whole[0, :, cols] = with_real[:chip_share] - with_imag[chip_share:]
        whole[1, :, cols] = with_imag[:chip_share] + with_real[chip_share:]
    mine = pl.ds(pl.multiple_of(core * share, share), share)
    other = pl.ds(pl.multiple_of((1 - core) * share, share), share)
    keep_ref[...] = diag_ref[...] - whole[:, mine, :]
    give_ref[...] = whole[:, other, :]


def subtract_kernel(left_ref, right_ref, out_ref):
    out_ref[...] = left_ref[...] - right_ref[...]


def on_device(n_row, n_col, top_inverse, panel, leaf_rows, leaf_counts, diag_inverse):
    vmem = pl.BlockSpec(memory_space=pltpu.VMEM)
    hbm = pl.BlockSpec(memory_space=pl.ANY)
    _, row_dev, _ = top_inverse.shape
    _, panel_rows, columns = panel.shape
    leaves = columns // B
    chips = n_row // 2
    chip_share = B // chips
    depth = n_row * panel_rows
    params = pltpu.CompilerParams(vmem_limit_bytes=max(16 << 20, 40 * depth * columns))

    def cut(block):
        sizes = 3 * row_dev // 8, row_dev - 3 * row_dev // 8
        return pl.pallas_call(
            cut_kernel,
            out_shape=[jax.ShapeDtypeStruct((2, size, B), F32) for size in sizes],
            in_specs=[vmem],
            out_specs=[vmem] * 2,
            compiler_params=params,
            name="cut_rows",
        )(block)

    blocks, halves = line_gather(top_inverse, "col", n_col, cut)

    swap = [(i, i ^ 1) for i in range(n_row)]
    like = {
        step: lax.ppermute(panel, "row", [(i, i ^ step) for i in range(n_row)])
        for step in range(2, n_row, 2)
    }
    near = [step for step in like if step & -step == step]
    far = [step for step in like if step not in near]
    packed = (2, len(near) * panel_rows, columns)
    leaf_counts = leaf_counts[None, :]
    mine, near_high, near_low, leaf_rows, leaf_counts = pl.pallas_call(
        pack_kernel,
        out_shape=[jax.ShapeDtypeStruct(packed, dtype) for dtype in (F32, BF16, BF16)]
        + [jax.ShapeDtypeStruct(value.shape, value.dtype) for value in (leaf_rows, leaf_counts)],
        in_specs=[vmem] * (2 + len(near)),
        out_specs=[vmem] * 5,
        compiler_params=params,
        name="pack_panel",
    )(leaf_rows, leaf_counts, *[like[step] for step in near])
    late_panel, _ = lax.optimization_barrier((panel, [like[step] for step in near]))
    mate = lax.ppermute(late_panel, "row", swap)
    near_mates = lax.ppermute(mine, "row", swap)
    far_panels = []
    for step in far:
        far_panels += [like[step], lax.ppermute(like[step], "row", swap)]

    early_blocks = [blocks[k] for k in range(0, n_col, 2)] + [blocks[1]]
    firsts = [halves[k][0] for k in range(3, n_col, 2)]
    early_blocks, firsts = lax.optimization_barrier((early_blocks, firsts))
    late_blocks = [half for k in range(3, n_col, 2) for half in halves[k]]

    def split_blocks(values):
        count = sum(value.shape[1] for value in values) // row_dev
        return pl.pallas_call(
            blocks_kernel,
            out_shape=jax.ShapeDtypeStruct((count, 4 * row_dev, B), BF16),
            in_specs=[vmem] * len(values),
            out_specs=vmem,
            compiler_params=params,
            cost_estimate=pl.CostEstimate(
                flops=10**11, bytes_accessed=10**9, transcendentals=0
            ),
            name="split_blocks",
        )(*values)

    indices = [
        pltpu.SMEM(leaf_rows.shape, leaf_rows.dtype),
        pltpu.SMEM(leaf_counts.shape, leaf_counts.dtype),
        pltpu.SemaphoreType.DMA((2,)),
    ]
    rows_shape = jax.ShapeDtypeStruct((2, row_dev, columns), F32)
    piece = jax.ShapeDtypeStruct((leaves, 2, chip_share, row_dev), F32)
    scratch = [pltpu.VMEM((chips,) + piece.shape[1:], F32)] + indices
    high, low, late, *early = pl.pallas_call(
        functools.partial(early_kernel, n_col, panel_rows, near, far),
        out_shape=[jax.ShapeDtypeStruct((2, depth, columns), BF16)] * 2
        + [jax.ShapeDtypeStruct(leaf_rows.shape, jnp.int32), rows_shape]
        + [piece] * chips,
        in_specs=[hbm, hbm] + [vmem] * (6 + len(far_panels)),
        out_specs=[vmem] * (4 + chips),
        scratch_shapes=scratch,
        compiler_params=params,
        name="early_rows",
    )(
        leaf_rows,
        leaf_counts,
        split_blocks(early_blocks),
        panel,
        mate,
        near_high,
        near_low,
        near_mates,
        *far_panels,
    )
    early, late_blocks = lax.optimization_barrier((early, late_blocks))

    selected, *sent = pl.pallas_call(
        functools.partial(select_kernel, chips),
        out_shape=[rows_shape] + [piece] * chips,
        in_specs=[vmem] * (5 + chips),
        out_specs=[vmem] * (1 + chips),
        scratch_shapes=scratch[:1],
        compiler_params=params,
        name="selected_rows",
    )(late, split_blocks(late_blocks), high, low, *early)

    for step in range(chips - 1, 0, -1):
        perm = [(i, i ^ (2 * step)) for i in range(n_row)]
        sent[step] = lax.ppermute(sent[step], "row", perm)
    selected = pl.pallas_call(
        write_kernel,
        out_shape=jax.ShapeDtypeStruct(selected.shape, F32),
        in_specs=[vmem],
        out_specs=vmem,
        compiler_params=params,
        name="write_rows",
    )(selected)
    selected, sent = lax.optimization_barrier((selected, sent[::-1]))

    keep, give = pl.pallas_call(
        diagonal_kernel,
        out_shape=[jax.ShapeDtypeStruct(diag_inverse.shape, F32)] * 2,
        in_specs=[vmem] * (chips + 4),
        out_specs=[vmem] * 2,
        scratch_shapes=[pltpu.VMEM((2, chip_share, columns), F32)],
        compiler_params=params,
        cost_estimate=pl.CostEstimate(
            flops=12 * chip_share * depth * columns,
            bytes_accessed=8 * (depth + 2 * chip_share) * columns,
            transcendentals=0,
        ),
        name="diagonal_part",
    )(leaf_rows, *sent, high, low, diag_inverse)
    give = lax.ppermute(give, "row", [(i, i ^ 1) for i in range(n_row)])
    diagonal = pl.pallas_call(
        subtract_kernel,
        out_shape=jax.ShapeDtypeStruct(diag_inverse.shape, F32),
        in_specs=[vmem] * 2,
        out_specs=vmem,
        compiler_params=params,
        name="diagonal_rows",
    )(keep, give)
    return selected, diagonal


def solution(mesh):
    return jax.shard_map(
        functools.partial(on_device, mesh.shape["row"], mesh.shape["col"]),
        mesh=mesh,
        in_specs=(
            P(None, "row", "col"),
            P(None, "row", "col"),
            P("col", None),
            P("col"),
            P(None, "row", "col"),
        ),
        out_specs=(P(None, "row", "col"), P(None, "row", "col")),
        check_vma=False,
    )
```

```python
import functools

import jax
import jax.numpy as jnp
from jax import lax
from jax.experimental import pallas as pl
from jax.experimental.pallas import tpu as pltpu
from jax.sharding import PartitionSpec as P

B = 256
F32 = jnp.float32
BF16 = jnp.bfloat16


def split(value):
    high = value.astype(BF16)
    low = (value - high.astype(F32)).astype(BF16)
    return high, low


def dot(left, right):
    return jnp.dot(left, right, preferred_element_type=F32)


def line_gather(own, n_row, n_col, later):
    def swap(block, step, cores):
        pairs = [
            (i * n_col + j, i * n_col + (j ^ step))
            for i in range(n_row)
            for j in range(n_col)
            if i % 2 in cores
        ]
        return lax.ppermute(block, ("row", "col"), pairs)

    blocks = {0: own}
    for step in line_steps(n_col)[:-1]:
        blocks |= {k ^ step: swap(block, step, (0, 1)) for k, block in blocks.items()}
    handed = {}
    for k, block in blocks.items():
        if k > 0:
            late, _ = lax.optimization_barrier((block, later))
            handed[k ^ 1] = [swap(block, 1, (1,)), swap(late, 1, (0,))]
    blocks[1] = swap(own, 1, (0, 1))
    return blocks, handed


def line_steps(n):
    steps = []
    while n > 1:
        n //= 2
        steps.append(n)
    return steps


def pack_kernel(*refs):
    (rows_ref, counts_ref), pieces = refs[:2], refs[2:-5]
    out_ref, high_ref, low_ref, rows_out, counts_out = refs[-5:]
    rows_out[...] = rows_ref[...]
    counts_out[...] = counts_ref[...]
    share_rows = pieces[0].shape[1]
    for place, piece in enumerate(pieces):
        here = slice(place * share_rows, (place + 1) * share_rows)
        out_ref[:, here, :] = piece[...]
        for part in range(2):
            high_ref[part, here, :], low_ref[part, here, :] = split(piece[part])


def add_slot(total, left, high_ref, low_ref, rows, cols):
    real, imag = total
    size = real.shape[0]
    both = left[0 : 2 * size]
    left = jnp.concatenate([both, left[2 * size : 4 * size], both], axis=1)

    def panel(part):
        high, low = high_ref[part, rows, cols], low_ref[part, rows, cols]
        return jnp.concatenate([high, high, low], axis=0)

    with_real, with_imag = dot(left, panel(0)), dot(left, panel(1))
    real = real - (with_real[:size] - with_imag[size:])
    imag = imag - (with_imag[:size] + with_real[size:])
    return real, imag


def row_is_live(rows_ref, counts_ref, member, block):
    return lax.fori_loop(
        0,
        counts_ref[0, member],
        lambda q, seen: seen | (rows_ref[member, q] == block),
        False,
    )


def put_block(out_ref, place, value):
    both = 2 * value.shape[1]
    out_ref[place, 0:both, :], out_ref[place, both : 2 * both, :] = split(value.reshape(both, B))


def early_blocks_kernel(*refs):
    blocks, out_ref = refs[:-1], refs[-1]
    for place, block in enumerate(blocks):
        put_block(out_ref, place, block[...])


def late_blocks_kernel(*refs):
    blocks, out_ref = refs[:-1], refs[-1]
    core = lax.axis_index("row") % 2
    for place in range(out_ref.shape[0]):
        first, second = blocks[2 * place], blocks[2 * place + 1]
        put_block(out_ref, place, jnp.where(core == 1, first[...], second[...]))


def add_product(member, q, top, place, high_ref, low_ref, out_ref):
    cols = slice(member * B, (member + 1) * B)
    rows = pl.ds(pl.multiple_of(q * B, B), B)
    total = out_ref[0, :, cols], out_ref[1, :, cols]
    total = add_slot(total, top[place], high_ref, low_ref, rows, cols)
    out_ref[0, :, cols], out_ref[1, :, cols] = total


def early_place(n_col, distance):
    return (distance % 2 == 0) | (distance == 1), jnp.where(distance == 1, n_col // 2, distance // 2)


def late_place(distance):
    return (distance - 3) // 2


def fetch(sems, *pairs):
    copies = [pltpu.make_async_copy(*pair, sems.at[k]) for k, pair in enumerate(pairs)]
    for copy in copies:
        copy.start()
    return copies


def turn(member, out_ref, sent, turned):
    chips, _, share, row_dev = turned.shape
    cols = slice(member * B, (member + 1) * B)
    for part in range(2):
        turned[:, part] = out_ref[part, :, cols].T.reshape(chips, share, row_dev)
    for step in range(chips):
        sent[step][member] = turned[(lax.axis_index("row") // 2) ^ step]


def early_kernel(n_col, share_rows, near, far, *refs):
    rows_hbm, counts_hbm, top, own, mate, near_high, near_low, near_mates = refs[:8]
    far_panels, refs = refs[8 : 8 + 2 * len(far)], refs[8 + 2 * len(far) :]
    high_ref, low_ref, late_ref, out_ref = refs[:4]
    sent, (turned, rows_ref, counts_ref, sems) = refs[4:-4], refs[-4:]
    leaves, slots = rows_ref.shape
    me = lax.axis_index("row")
    my_block = (me * out_ref.shape[1]) // B
    my_col = lax.axis_index("col")
    arrivals = fetch(sems, (rows_hbm, rows_ref), (counts_hbm, counts_ref))

    def put(owner, high, low):
        rows = pl.ds(pl.multiple_of(owner * share_rows, share_rows), share_rows)
        high_ref[:, rows, :], low_ref[:, rows, :] = high, low

    put(me, *split(own[...]))
    put(me ^ 1, *split(mate[...]))
    for place, step in enumerate(near):
        here = slice(place * share_rows, (place + 1) * share_rows)
        put(me ^ step, near_high[:, here, :], near_low[:, here, :])
        put(me ^ step ^ 1, *split(near_mates[:, here, :]))
    for place, step in enumerate(far):
        put(me ^ step, *split(far_panels[2 * place][...]))
        put(me ^ step ^ 1, *split(far_panels[2 * place + 1][...]))
    out_ref[...] = jnp.zeros(out_ref.shape, F32)
    for copy in arrivals:
        copy.wait()
    here = [lax.broadcasted_iota(jnp.int32, (leaves, slots), axis) for axis in range(2)]
    late_ref[...] = jnp.zeros((leaves, slots), jnp.int32)
    for member in range(leaves):

        def slot(q, carry):
            distance = my_col ^ rows_ref[member, q]
            held, place = early_place(n_col, distance)

            @pl.when(held)
            def _():
                add_product(member, q, top, place, high_ref, low_ref, out_ref)

            @pl.when(jnp.logical_not(held))
            def _():
                mark = (here[0] == member) & (here[1] == q)
                late_ref[...] = jnp.where(mark, 1 + late_place(distance), late_ref[...])

            return carry

        live = row_is_live(rows_ref, counts_ref, member, my_block)
        lax.fori_loop(0, jnp.where(live, counts_ref[0, member], 0), slot, 0)
        turn(member, out_ref, sent, turned)


def select_kernel(chips, late_ref, top, high_ref, low_ref, early_ref, *refs):
    early_sent, out_ref, sent, turned = refs[:chips], refs[chips], refs[chips + 1 : -1], refs[-1]
    leaves, slots = late_ref.shape

    def last_marked(member, below):
        marks = late_ref[member : member + 1, :]
        lane = lax.broadcasted_iota(jnp.int32, marks.shape, 1)
        return jnp.max(jnp.where((marks > 0) & (lane < below), lane * 256 + marks, -1))

    found = [last_marked(member, slots) for member in range(leaves)]
    out_ref[...] = early_ref[...]
    for step in range(chips):
        sent[step][...] = early_sent[step][...]
    for member in range(leaves):

        def slot(_, code):
            @pl.when(code >= 0)
            def _():
                add_product(member, code >> 8, top, (code & 255) - 1, high_ref, low_ref, out_ref)

            return last_marked(member, code >> 8)

        @pl.when(found[member] >= 0)
        def _():
            if top.shape[0] == 1:
                add_product(member, found[member] >> 8, top, 0, high_ref, low_ref, out_ref)
            else:
                lax.fori_loop(0, top.shape[0], slot, found[member])
            turn(member, out_ref, sent, turned)


def write_kernel(value_ref, out_ref):
    out_ref[...] = value_ref[...]


def diagonal_kernel(rows_ref, *refs):
    pieces, (high_ref, low_ref, diag_ref, keep_ref, give_ref, whole) = refs[:-6], refs[-6:]
    leaves, slots = rows_ref.shape
    _, _, chip_share, row_dev = pieces[0].shape
    share = keep_ref.shape[1]
    me = lax.axis_index("row")
    core = me % 2

    def pick(member, q):
        block = jnp.broadcast_to(rows_ref[member : member + 1, q : q + 1], (2 * chip_share, row_dev))
        picked = jnp.zeros(block.shape, F32)
        for step, piece in enumerate(reversed(pieces)):
            here = block == (me // 2) ^ step
            picked = jnp.where(here, piece[member].reshape(block.shape), picked)
        return jnp.concatenate(split(picked), axis=0)

    for member in range(leaves):
        cols = slice(member * B, (member + 1) * B)
        left = jnp.concatenate([pick(member, q) for q in range(slots)], axis=1)
        both = left[: 2 * chip_share]

        def panel(ref, part):
            starts = [pl.multiple_of(q * B + core * row_dev, row_dev) for q in range(slots)]
            return jnp.concatenate(
                [ref[part, pl.ds(start, row_dev), cols] for start in starts], axis=0
            )

        with_real = dot(left, panel(high_ref, 0))
        with_imag = dot(left, panel(high_ref, 1))
        with_real = with_real[: 2 * chip_share] + with_real[2 * chip_share :]
        with_imag = with_imag[: 2 * chip_share] + with_imag[2 * chip_share :]
        with_real += dot(both, panel(low_ref, 0))
        with_imag += dot(both, panel(low_ref, 1))
        whole[0, :, cols] = with_real[:chip_share] - with_imag[chip_share:]
        whole[1, :, cols] = with_imag[:chip_share] + with_real[chip_share:]
    mine = pl.ds(pl.multiple_of(core * share, share), share)
    other = pl.ds(pl.multiple_of((1 - core) * share, share), share)
    keep_ref[...] = diag_ref[...] - whole[:, mine, :]
    give_ref[...] = whole[:, other, :]


def subtract_kernel(left_ref, right_ref, out_ref):
    out_ref[...] = left_ref[...] - right_ref[...]


def on_device(n_row, n_col, top_inverse, panel, leaf_rows, leaf_counts, diag_inverse):
    vmem = pl.BlockSpec(memory_space=pltpu.VMEM)
    hbm = pl.BlockSpec(memory_space=pl.ANY)
    _, row_dev, _ = top_inverse.shape
    _, panel_rows, columns = panel.shape
    leaves = columns // B
    chips = n_row // 2
    chip_share = B // chips
    depth = n_row * panel_rows
    params = pltpu.CompilerParams(vmem_limit_bytes=max(16 << 20, 40 * depth * columns))

    swap = [(i, i ^ 1) for i in range(n_row)]
    like = {
        step: lax.ppermute(panel, "row", [(i, i ^ step) for i in range(n_row)])
        for step in range(2, n_row, 2)
    }
    near = [step for step in like if step & -step == step]
    far = [step for step in like if step not in near]
    blocks, handed = line_gather(top_inverse, n_row, n_col, [like[step] for step in far])
    packed = (2, len(near) * panel_rows, columns)
    leaf_counts = leaf_counts[None, :]
    mine, near_high, near_low, leaf_rows, leaf_counts = pl.pallas_call(
        pack_kernel,
        out_shape=[jax.ShapeDtypeStruct(packed, dtype) for dtype in (F32, BF16, BF16)]
        + [jax.ShapeDtypeStruct(value.shape, value.dtype) for value in (leaf_rows, leaf_counts)],
        in_specs=[vmem] * (2 + len(near)),
        out_specs=[vmem] * 5,
        compiler_params=params,
        name="pack_panel",
    )(leaf_rows, leaf_counts, *[like[step] for step in near])
    late_panel, _ = lax.optimization_barrier((panel, [like[step] for step in near]))
    mate = lax.ppermute(late_panel, "row", swap)
    near_mates = lax.ppermute(mine, "row", swap)
    far_panels = []
    for step in far:
        far_panels += [like[step], lax.ppermute(like[step], "row", swap)]

    early_blocks = [blocks[k] for k in range(0, n_col, 2)] + [blocks[1]]
    firsts = [handed[k][0] for k in range(3, n_col, 2)]
    early_blocks, firsts = lax.optimization_barrier((early_blocks, firsts))
    late_blocks = [block for k in range(3, n_col, 2) for block in handed[k]]

    def split_blocks(kernel, values, count):
        return pl.pallas_call(
            kernel,
            out_shape=jax.ShapeDtypeStruct((count, 4 * row_dev, B), BF16),
            in_specs=[vmem] * len(values),
            out_specs=vmem,
            compiler_params=params,
            cost_estimate=pl.CostEstimate(
                flops=10**11, bytes_accessed=10**9, transcendentals=0
            ),
            name="split_blocks",
        )(*values)

    indices = [
        pltpu.SMEM(leaf_rows.shape, leaf_rows.dtype),
        pltpu.SMEM(leaf_counts.shape, leaf_counts.dtype),
        pltpu.SemaphoreType.DMA((2,)),
    ]
    rows_shape = jax.ShapeDtypeStruct((2, row_dev, columns), F32)
    piece = jax.ShapeDtypeStruct((leaves, 2, chip_share, row_dev), F32)
    scratch = [pltpu.VMEM((chips,) + piece.shape[1:], F32)] + indices
    high, low, late, *early = pl.pallas_call(
        functools.partial(early_kernel, n_col, panel_rows, near, far),
        out_shape=[jax.ShapeDtypeStruct((2, depth, columns), BF16)] * 2
        + [jax.ShapeDtypeStruct(leaf_rows.shape, jnp.int32), rows_shape]
        + [piece] * chips,
        in_specs=[hbm, hbm] + [vmem] * (6 + len(far_panels)),
        out_specs=[vmem] * (4 + chips),
        scratch_shapes=scratch,
        compiler_params=params,
        name="early_rows",
    )(
        leaf_rows,
        leaf_counts,
        split_blocks(early_blocks_kernel, early_blocks, len(early_blocks)),
        panel,
        mate,
        near_high,
        near_low,
        near_mates,
        *far_panels,
    )
    early, late_blocks = lax.optimization_barrier((early, late_blocks))

    selected, *sent = pl.pallas_call(
        functools.partial(select_kernel, chips),
        out_shape=[rows_shape] + [piece] * chips,
        in_specs=[vmem] * (5 + chips),
        out_specs=[vmem] * (1 + chips),
        scratch_shapes=scratch[:1],
        compiler_params=params,
        name="selected_rows",
    )(late, split_blocks(late_blocks_kernel, late_blocks, len(late_blocks) // 2), high, low, *early)

    for step in range(chips - 1, 0, -1):
        perm = [(i, i ^ (2 * step)) for i in range(n_row)]
        sent[step] = lax.ppermute(sent[step], "row", perm)
    selected = pl.pallas_call(
        write_kernel,
        out_shape=jax.ShapeDtypeStruct(selected.shape, F32),
        in_specs=[vmem],
        out_specs=vmem,
        compiler_params=params,
        name="write_rows",
    )(selected)
    selected, sent = lax.optimization_barrier((selected, sent[::-1]))

    keep, give = pl.pallas_call(
        diagonal_kernel,
        out_shape=[jax.ShapeDtypeStruct(diag_inverse.shape, F32)] * 2,
        in_specs=[vmem] * (chips + 4),
        out_specs=[vmem] * 2,
        scratch_shapes=[pltpu.VMEM((2, chip_share, columns), F32)],
        compiler_params=params,
        cost_estimate=pl.CostEstimate(
            flops=12 * chip_share * depth * columns,
            bytes_accessed=8 * (depth + 2 * chip_share) * columns,
            transcendentals=0,
        ),
        name="diagonal_part",
    )(leaf_rows, *sent, high, low, diag_inverse)
    give = lax.ppermute(give, "row", [(i, i ^ 1) for i in range(n_row)])
    diagonal = pl.pallas_call(
        subtract_kernel,
        out_shape=jax.ShapeDtypeStruct(diag_inverse.shape, F32),
        in_specs=[vmem] * 2,
        out_specs=vmem,
        compiler_params=params,
        name="diagonal_rows",
    )(keep, give)
    return selected, diagonal


def solution(mesh):
    return jax.shard_map(
        functools.partial(on_device, mesh.shape["row"], mesh.shape["col"]),
        mesh=mesh,
        in_specs=(
            P(None, "row", "col"),
            P(None, "row", "col"),
            P("col", None),
            P("col"),
            P(None, "row", "col"),
        ),
        out_specs=(P(None, "row", "col"), P(None, "row", "col")),
        check_vma=False,
    )
```

```python
import functools

import jax
import jax.numpy as jnp
from jax import lax
from jax.experimental import pallas as pl
from jax.experimental.pallas import tpu as pltpu
from jax.sharding import PartitionSpec as P

B = 256
F32 = jnp.float32
BF16 = jnp.bfloat16


def split(value):
    high = value.astype(BF16)
    low = (value - high.astype(F32)).astype(BF16)
    return high, low


def dot(left, right):
    return jnp.dot(left, right, preferred_element_type=F32)


def line_gather(own, axis, n, cut):
    blocks = {0: own}
    for step in line_steps(n):
        perm = [(i, i ^ step) for i in range(n)]
        if step > 1:
            blocks |= {k ^ step: lax.ppermute(block, axis, perm) for k, block in blocks.items()}
    halves = {k ^ 1: cut(block) for k, block in blocks.items() if k > 0}
    halves = {k: [lax.ppermute(half, axis, perm) for half in pair] for k, pair in halves.items()}
    blocks[1] = lax.ppermute(own, axis, perm)
    return blocks, halves


def line_steps(n):
    steps = []
    while n > 1:
        n //= 2
        steps.append(n)
    return steps


def cut_kernel(block_ref, first_ref, second_ref):
    size = first_ref.shape[1]
    first_ref[...] = block_ref[:, :size, :]
    second_ref[...] = block_ref[:, size:, :]


def pack_kernel(*refs):
    (rows_ref, counts_ref), pieces = refs[:2], refs[2:-5]
    out_ref, high_ref, low_ref, rows_out, counts_out = refs[-5:]
    rows_out[...] = rows_ref[...]
    counts_out[...] = counts_ref[...]
    share_rows = pieces[0].shape[1]
    for place, piece in enumerate(pieces):
        here = slice(place * share_rows, (place + 1) * share_rows)
        out_ref[:, here, :] = piece[...]
        for part in range(2):
            high_ref[part, here, :], low_ref[part, here, :] = split(piece[part])


def add_slot(total, left, high_ref, low_ref, rows, cols):
    real, imag = total
    size = real.shape[0]
    both = left[0 : 2 * size]
    left = jnp.concatenate([both, left[2 * size : 4 * size], both], axis=1)

    def panel(part):
        high, low = high_ref[part, rows, cols], low_ref[part, rows, cols]
        return jnp.concatenate([high, high, low], axis=0)

    with_real, with_imag = dot(left, panel(0)), dot(left, panel(1))
    real = real - (with_real[:size] - with_imag[size:])
    imag = imag - (with_imag[:size] + with_real[size:])
    return real, imag


def row_is_live(rows_ref, counts_ref, member, block):
    return lax.fori_loop(
        0,
        counts_ref[0, member],
        lambda q, seen: seen | (rows_ref[member, q] == block),
        False,
    )


def blocks_kernel(*refs):
    pieces, out_ref = refs[:-1], refs[-1]
    rows = out_ref.shape[1] // 4
    first = 0
    for piece in pieces:
        size = piece.shape[1]
        for part in range(2):
            for scale, value in enumerate(split(piece[part])):
                start = (2 * scale + part) * rows + first % rows
                out_ref[first // rows, start : start + size, :] = value
        first += size


def add_product(member, q, top, place, high_ref, low_ref, out_ref):
    cols = slice(member * B, (member + 1) * B)
    rows = pl.ds(pl.multiple_of(q * B, B), B)
    total = out_ref[0, :, cols], out_ref[1, :, cols]
    total = add_slot(total, top[place], high_ref, low_ref, rows, cols)
    out_ref[0, :, cols], out_ref[1, :, cols] = total


def early_place(n_col, distance):
    return (distance % 2 == 0) | (distance == 1), jnp.where(distance == 1, n_col // 2, distance // 2)


def late_place(distance):
    return (distance - 3) // 2


def fetch(sems, *pairs):
    copies = [pltpu.make_async_copy(*pair, sems.at[k]) for k, pair in enumerate(pairs)]
    for copy in copies:
        copy.start()
    return copies


def turn(member, out_ref, sent, turned):
    chips, _, share, row_dev = turned.shape
    cols = slice(member * B, (member + 1) * B)
    for part in range(2):
        turned[:, part] = out_ref[part, :, cols].T.reshape(chips, share, row_dev)
    for step in range(chips):
        sent[step][member] = turned[(lax.axis_index("row") // 2) ^ step]


def early_kernel(n_col, share_rows, near, far, *refs):
    rows_hbm, counts_hbm, top, own, mate, near_high, near_low, near_mates = refs[:8]
    far_panels, refs = refs[8 : 8 + 2 * len(far)], refs[8 + 2 * len(far) :]
    high_ref, low_ref, late_ref, out_ref = refs[:4]
    sent, (turned, rows_ref, counts_ref, sems) = refs[4:-4], refs[-4:]
    leaves, slots = rows_ref.shape
    me = lax.axis_index("row")
    my_block = (me * out_ref.shape[1]) // B
    my_col = lax.axis_index("col")
    arrivals = fetch(sems, (rows_hbm, rows_ref), (counts_hbm, counts_ref))

    def put(owner, high, low):
        rows = pl.ds(pl.multiple_of(owner * share_rows, share_rows), share_rows)
        high_ref[:, rows, :], low_ref[:, rows, :] = high, low

    put(me, *split(own[...]))
    put(me ^ 1, *split(mate[...]))
    for place, step in enumerate(near):
        here = slice(place * share_rows, (place + 1) * share_rows)
        put(me ^ step, near_high[:, here, :], near_low[:, here, :])
        put(me ^ step ^ 1, *split(near_mates[:, here, :]))
    for place, step in enumerate(far):
        put(me ^ step, *split(far_panels[2 * place][...]))
        put(me ^ step ^ 1, *split(far_panels[2 * place + 1][...]))
    out_ref[...] = jnp.zeros(out_ref.shape, F32)
    for copy in arrivals:
        copy.wait()
    here = [lax.broadcasted_iota(jnp.int32, (leaves, slots), axis) for axis in range(2)]
    late_ref[...] = jnp.zeros((leaves, slots), jnp.int32)
    for member in range(leaves):

        def slot(q, carry):
            distance = my_col ^ rows_ref[member, q]
            held, place = early_place(n_col, distance)

            @pl.when(held)
            def _():
                add_product(member, q, top, place, high_ref, low_ref, out_ref)

            @pl.when(jnp.logical_not(held))
            def _():
                mark = (here[0] == member) & (here[1] == q)
                late_ref[...] = jnp.where(mark, 1 + late_place(distance), late_ref[...])

            return carry

        live = row_is_live(rows_ref, counts_ref, member, my_block)
        lax.fori_loop(0, jnp.where(live, counts_ref[0, member], 0), slot, 0)
        turn(member, out_ref, sent, turned)


def select_kernel(chips, late_ref, top, high_ref, low_ref, early_ref, *refs):
    early_sent, out_ref, sent, turned = refs[:chips], refs[chips], refs[chips + 1 : -1], refs[-1]
    leaves, slots = late_ref.shape

    def last_marked(member, below):
        marks = late_ref[member : member + 1, :]
        lane = lax.broadcasted_iota(jnp.int32, marks.shape, 1)
        return jnp.max(jnp.where((marks > 0) & (lane < below), lane * 256 + marks, -1))

    found = [last_marked(member, slots) for member in range(leaves)]
    out_ref[...] = early_ref[...]
    for step in range(chips):
        sent[step][...] = early_sent[step][...]
    for member in range(leaves):

        def slot(_, code):
            @pl.when(code >= 0)
            def _():
                add_product(member, code >> 8, top, (code & 255) - 1, high_ref, low_ref, out_ref)

            return last_marked(member, code >> 8)

        @pl.when(found[member] >= 0)
        def _():
            if top.shape[0] == 1:
                add_product(member, found[member] >> 8, top, 0, high_ref, low_ref, out_ref)
            else:
                lax.fori_loop(0, top.shape[0], slot, found[member])
            turn(member, out_ref, sent, turned)


def write_kernel(value_ref, out_ref):
    out_ref[...] = value_ref[...]


def diagonal_kernel(rows_ref, *refs):
    pieces, (high_ref, low_ref, diag_ref, keep_ref, give_ref, whole) = refs[:-6], refs[-6:]
    leaves, slots = rows_ref.shape
    _, _, chip_share, row_dev = pieces[0].shape
    share = keep_ref.shape[1]
    me = lax.axis_index("row")
    core = me % 2

    def pick(member, q):
        block = jnp.broadcast_to(rows_ref[member : member + 1, q : q + 1], (2 * chip_share, row_dev))
        picked = jnp.zeros(block.shape, F32)
        for step, piece in enumerate(reversed(pieces)):
            here = block == (me // 2) ^ step
            picked = jnp.where(here, piece[member].reshape(block.shape), picked)
        return jnp.concatenate(split(picked), axis=0)

    for member in range(leaves):
        cols = slice(member * B, (member + 1) * B)
        left = jnp.concatenate([pick(member, q) for q in range(slots)], axis=1)
        both = left[: 2 * chip_share]

        def panel(ref, part):
            starts = [pl.multiple_of(q * B + core * row_dev, row_dev) for q in range(slots)]
            return jnp.concatenate(
                [ref[part, pl.ds(start, row_dev), cols] for start in starts], axis=0
            )

        with_real = dot(left, panel(high_ref, 0))
        with_imag = dot(left, panel(high_ref, 1))
        with_real = with_real[: 2 * chip_share] + with_real[2 * chip_share :]
        with_imag = with_imag[: 2 * chip_share] + with_imag[2 * chip_share :]
        with_real += dot(both, panel(low_ref, 0))
        with_imag += dot(both, panel(low_ref, 1))
        whole[0, :, cols] = with_real[:chip_share] - with_imag[chip_share:]
        whole[1, :, cols] = with_imag[:chip_share] + with_real[chip_share:]
    mine = pl.ds(pl.multiple_of(core * share, share), share)
    other = pl.ds(pl.multiple_of((1 - core) * share, share), share)
    keep_ref[...] = diag_ref[...] - whole[:, mine, :]
    give_ref[...] = whole[:, other, :]


def on_device(n_row, n_col, top_inverse, panel, leaf_rows, leaf_counts, diag_inverse):
    vmem = pl.BlockSpec(memory_space=pltpu.VMEM)
    hbm = pl.BlockSpec(memory_space=pl.ANY)
    _, row_dev, _ = top_inverse.shape
    _, panel_rows, columns = panel.shape
    leaves = columns // B
    chips = n_row // 2
    chip_share = B // chips
    depth = n_row * panel_rows
    params = pltpu.CompilerParams(vmem_limit_bytes=max(16 << 20, 40 * depth * columns))

    def cut(block):
        sizes = 3 * row_dev // 8, row_dev - 3 * row_dev // 8
        return pl.pallas_call(
            cut_kernel,
            out_shape=[jax.ShapeDtypeStruct((2, size, B), F32) for size in sizes],
            in_specs=[vmem],
            out_specs=[vmem] * 2,
            compiler_params=params,
            name="cut_rows",
        )(block)

    blocks, halves = line_gather(top_inverse, "col", n_col, cut)

    swap = [(i, i ^ 1) for i in range(n_row)]
    like = {
        step: lax.ppermute(panel, "row", [(i, i ^ step) for i in range(n_row)])
        for step in range(2, n_row, 2)
    }
    near = [step for step in like if step & -step == step]
    far = [step for step in like if step not in near]
    packed = (2, len(near) * panel_rows, columns)
    leaf_counts = leaf_counts[None, :]
    mine, near_high, near_low, leaf_rows, leaf_counts = pl.pallas_call(
        pack_kernel,
        out_shape=[jax.ShapeDtypeStruct(packed, dtype) for dtype in (F32, BF16, BF16)]
        + [jax.ShapeDtypeStruct(value.shape, value.dtype) for value in (leaf_rows, leaf_counts)],
        in_specs=[vmem] * (2 + len(near)),
        out_specs=[vmem] * 5,
        compiler_params=params,
        name="pack_panel",
    )(leaf_rows, leaf_counts, *[like[step] for step in near])
    late_panel, _ = lax.optimization_barrier((panel, [like[step] for step in near]))
    mate = lax.ppermute(late_panel, "row", swap)
    near_mates = lax.ppermute(mine, "row", swap)
    far_panels = []
    for step in far:
        far_panels += [like[step], lax.ppermute(like[step], "row", swap)]

    early_blocks = [blocks[k] for k in range(0, n_col, 2)] + [blocks[1]]
    firsts = [halves[k][0] for k in range(3, n_col, 2)]
    early_blocks, firsts = lax.optimization_barrier((early_blocks, firsts))
    late_blocks = [half for k in range(3, n_col, 2) for half in halves[k]]

    def split_blocks(values):
        count = sum(value.shape[1] for value in values) // row_dev
        return pl.pallas_call(
            blocks_kernel,
            out_shape=jax.ShapeDtypeStruct((count, 4 * row_dev, B), BF16),
            in_specs=[vmem] * len(values),
            out_specs=vmem,
            compiler_params=params,
            cost_estimate=pl.CostEstimate(
                flops=10**11, bytes_accessed=10**9, transcendentals=0
            ),
            name="split_blocks",
        )(*values)

    indices = [
        pltpu.SMEM(leaf_rows.shape, leaf_rows.dtype),
        pltpu.SMEM(leaf_counts.shape, leaf_counts.dtype),
        pltpu.SemaphoreType.DMA((2,)),
    ]
    rows_shape = jax.ShapeDtypeStruct((2, row_dev, columns), F32)
    piece = jax.ShapeDtypeStruct((leaves, 2, chip_share, row_dev), F32)
    scratch = [pltpu.VMEM((chips,) + piece.shape[1:], F32)] + indices
    high, low, late, *early = pl.pallas_call(
        functools.partial(early_kernel, n_col, panel_rows, near, far),
        out_shape=[jax.ShapeDtypeStruct((2, depth, columns), BF16)] * 2
        + [jax.ShapeDtypeStruct(leaf_rows.shape, jnp.int32), rows_shape]
        + [piece] * chips,
        in_specs=[hbm, hbm] + [vmem] * (6 + len(far_panels)),
        out_specs=[vmem] * (4 + chips),
        scratch_shapes=scratch,
        compiler_params=params,
        name="early_rows",
    )(
        leaf_rows,
        leaf_counts,
        split_blocks(early_blocks),
        panel,
        mate,
        near_high,
        near_low,
        near_mates,
        *far_panels,
    )
    early, late_blocks = lax.optimization_barrier((early, late_blocks))

    selected, *sent = pl.pallas_call(
        functools.partial(select_kernel, chips),
        out_shape=[rows_shape] + [piece] * chips,
        in_specs=[vmem] * (5 + chips),
        out_specs=[vmem] * (1 + chips),
        scratch_shapes=scratch[:1],
        compiler_params=params,
        name="selected_rows",
    )(late, split_blocks(late_blocks), high, low, *early)

    for step in range(chips - 1, 0, -1):
        perm = [(i, i ^ (2 * step)) for i in range(n_row)]
        sent[step] = lax.ppermute(sent[step], "row", perm)
    selected = pl.pallas_call(
        write_kernel,
        out_shape=jax.ShapeDtypeStruct(selected.shape, F32),
        in_specs=[vmem],
        out_specs=vmem,
        compiler_params=params,
        name="write_rows",
    )(selected)
    selected, sent = lax.optimization_barrier((selected, sent[::-1]))

    keep, give = pl.pallas_call(
        diagonal_kernel,
        out_shape=[jax.ShapeDtypeStruct(diag_inverse.shape, F32)] * 2,
        in_specs=[vmem] * (chips + 4),
        out_specs=[vmem] * 2,
        scratch_shapes=[pltpu.VMEM((2, chip_share, columns), F32)],
        compiler_params=params,
        cost_estimate=pl.CostEstimate(
            flops=12 * chip_share * depth * columns,
            bytes_accessed=8 * (depth + 2 * chip_share) * columns,
            transcendentals=0,
        ),
        name="diagonal_part",
    )(leaf_rows, *sent, high, low, diag_inverse)
    give = lax.ppermute(give, "row", [(i, i ^ 1) for i in range(n_row)])
    diagonal = keep - give
    return selected, diagonal


def solution(mesh):
    return jax.shard_map(
        functools.partial(on_device, mesh.shape["row"], mesh.shape["col"]),
        mesh=mesh,
        in_specs=(
            P(None, "row", "col"),
            P(None, "row", "col"),
            P("col", None),
            P("col"),
            P(None, "row", "col"),
        ),
        out_specs=(P(None, "row", "col"), P(None, "row", "col")),
        check_vma=False,
    )
```

```python
import functools

import jax
import jax.numpy as jnp
from jax import lax
from jax.experimental import pallas as pl
from jax.experimental.pallas import tpu as pltpu
from jax.sharding import PartitionSpec as P

B = 256
F32 = jnp.float32
BF16 = jnp.bfloat16


def split(value):
    high = value.astype(BF16)
    low = (value - high.astype(F32)).astype(BF16)
    return high, low


def dot(left, right):
    return jnp.dot(left, right, preferred_element_type=F32)


def line_gather(own, axis, n, cut):
    blocks = {0: own}
    for step in line_steps(n):
        perm = [(i, i ^ step) for i in range(n)]
        if step > 1:
            blocks |= {k ^ step: lax.ppermute(block, axis, perm) for k, block in blocks.items()}
    halves = {k ^ 1: cut(block) for k, block in blocks.items() if k > 0}
    halves = {k: [lax.ppermute(half, axis, perm) for half in pair] for k, pair in halves.items()}
    blocks[1] = lax.ppermute(own, axis, perm)
    return blocks, halves


def line_steps(n):
    steps = []
    while n > 1:
        n //= 2
        steps.append(n)
    return steps


def cut_kernel(block_ref, first_ref, second_ref):
    size = first_ref.shape[1]
    first_ref[...] = block_ref[:, :size, :]
    second_ref[...] = block_ref[:, size:, :]


def pack_kernel(*refs):
    (rows_ref, counts_ref), pieces = refs[:2], refs[2:-5]
    out_ref, high_ref, low_ref, rows_out, counts_out = refs[-5:]
    rows_out[...] = rows_ref[...]
    counts_out[...] = counts_ref[...]
    share_rows = pieces[0].shape[1]
    for place, piece in enumerate(pieces):
        here = slice(place * share_rows, (place + 1) * share_rows)
        out_ref[:, here, :] = piece[...]
        for part in range(2):
            high_ref[part, here, :], low_ref[part, here, :] = split(piece[part])


def add_slot(total, left, high_ref, low_ref, rows, cols):
    real, imag = total
    size = real.shape[0]
    both = left[0 : 2 * size]
    left = jnp.concatenate([both, left[2 * size : 4 * size], both], axis=1)

    def panel(part):
        high, low = high_ref[part, rows, cols], low_ref[part, rows, cols]
        return jnp.concatenate([high, high, low], axis=0)

    with_real, with_imag = dot(left, panel(0)), dot(left, panel(1))
    real = real - (with_real[:size] - with_imag[size:])
    imag = imag - (with_imag[:size] + with_real[size:])
    return real, imag


def row_is_live(rows_ref, counts_ref, member, block):
    return lax.fori_loop(
        0,
        counts_ref[0, member],
        lambda q, seen: seen | (rows_ref[member, q] == block),
        False,
    )


def blocks_kernel(*refs):
    pieces, out_ref = refs[:-1], refs[-1]
    rows = out_ref.shape[1] // 4
    first = 0
    for piece in pieces:
        size = piece.shape[1]
        for part in range(2):
            for scale, value in enumerate(split(piece[part])):
                start = (2 * scale + part) * rows + first % rows
                out_ref[first // rows, start : start + size, :] = value
        first += size


def add_product(member, q, top, place, high_ref, low_ref, out_ref):
    cols = slice(member * B, (member + 1) * B)
    rows = pl.ds(pl.multiple_of(q * B, B), B)
    total = out_ref[0, :, cols], out_ref[1, :, cols]
    total = add_slot(total, top[place], high_ref, low_ref, rows, cols)
    out_ref[0, :, cols], out_ref[1, :, cols] = total


def early_place(n_col, distance):
    return (distance % 2 == 0) | (distance == 1), jnp.where(distance == 1, n_col // 2, distance // 2)


def late_place(distance):
    return (distance - 3) // 2


def fetch(sems, *pairs):
    copies = [pltpu.make_async_copy(*pair, sems.at[k]) for k, pair in enumerate(pairs)]
    for copy in copies:
        copy.start()
    return copies


def chip_step(slot, core):
    return slot ^ (3 * core) if slot in (1, 2) else slot


def turn(member, out_ref, sent, turned):
    me = lax.axis_index("row")
    chips, _, share, row_dev = turned.shape
    cols = slice(member * B, (member + 1) * B)
    for part in range(2):
        turned[:, part] = out_ref[part, :, cols].T.reshape(chips, share, row_dev)
    for slot in range(chips):
        sent[slot][member] = turned[(me // 2) ^ chip_step(slot, me % 2)]


def early_kernel(n_col, share_rows, near, far, *refs):
    rows_hbm, counts_hbm, top, own, mate, near_high, near_low, near_mates = refs[:8]
    far_panels, refs = refs[8 : 8 + 2 * len(far)], refs[8 + 2 * len(far) :]
    high_ref, low_ref, late_ref, out_ref = refs[:4]
    sent, (turned, rows_ref, counts_ref, sems) = refs[4:-4], refs[-4:]
    leaves, slots = rows_ref.shape
    me = lax.axis_index("row")
    my_block = (me * out_ref.shape[1]) // B
    my_col = lax.axis_index("col")
    arrivals = fetch(sems, (rows_hbm, rows_ref), (counts_hbm, counts_ref))

    def put(owner, high, low):
        rows = pl.ds(pl.multiple_of(owner * share_rows, share_rows), share_rows)
        high_ref[:, rows, :], low_ref[:, rows, :] = high, low

    put(me, *split(own[...]))
    put(me ^ 1, *split(mate[...]))
    for place, step in enumerate(near):
        here = slice(place * share_rows, (place + 1) * share_rows)
        put(me ^ step, near_high[:, here, :], near_low[:, here, :])
        put(me ^ step ^ 1, *split(near_mates[:, here, :]))
    for place, step in enumerate(far):
        put(me ^ step, *split(far_panels[2 * place][...]))
        put(me ^ step ^ 1, *split(far_panels[2 * place + 1][...]))
    out_ref[...] = jnp.zeros(out_ref.shape, F32)
    for copy in arrivals:
        copy.wait()
    here = [lax.broadcasted_iota(jnp.int32, (leaves, slots), axis) for axis in range(2)]
    late_ref[...] = jnp.zeros((leaves, slots), jnp.int32)
    for member in range(leaves):

        def slot(q, carry):
            distance = my_col ^ rows_ref[member, q]
            held, place = early_place(n_col, distance)

            @pl.when(held)
            def _():
                add_product(member, q, top, place, high_ref, low_ref, out_ref)

            @pl.when(jnp.logical_not(held))
            def _():
                mark = (here[0] == member) & (here[1] == q)
                late_ref[...] = jnp.where(mark, 1 + late_place(distance), late_ref[...])

            return carry

        live = row_is_live(rows_ref, counts_ref, member, my_block)
        lax.fori_loop(0, jnp.where(live, counts_ref[0, member], 0), slot, 0)
        turn(member, out_ref, sent, turned)


def select_kernel(chips, late_ref, top, high_ref, low_ref, early_ref, *refs):
    early_sent, out_ref, sent, turned = refs[:chips], refs[chips], refs[chips + 1 : -1], refs[-1]
    leaves, slots = late_ref.shape

    def last_marked(member, below):
        marks = late_ref[member : member + 1, :]
        lane = lax.broadcasted_iota(jnp.int32, marks.shape, 1)
        return jnp.max(jnp.where((marks > 0) & (lane < below), lane * 256 + marks, -1))

    found = [last_marked(member, slots) for member in range(leaves)]
    out_ref[...] = early_ref[...]
    for step in range(chips):
        sent[step][...] = early_sent[step][...]
    for member in range(leaves):

        def slot(_, code):
            @pl.when(code >= 0)
            def _():
                add_product(member, code >> 8, top, (code & 255) - 1, high_ref, low_ref, out_ref)

            return last_marked(member, code >> 8)

        @pl.when(found[member] >= 0)
        def _():
            if top.shape[0] == 1:
                add_product(member, found[member] >> 8, top, 0, high_ref, low_ref, out_ref)
            else:
                lax.fori_loop(0, top.shape[0], slot, found[member])
            turn(member, out_ref, sent, turned)


def write_kernel(value_ref, out_ref):
    out_ref[...] = value_ref[...]


def diagonal_kernel(rows_ref, *refs):
    pieces, (high_ref, low_ref, diag_ref, keep_ref, give_ref, whole) = refs[:-6], refs[-6:]
    leaves, slots = rows_ref.shape
    _, _, chip_share, row_dev = pieces[0].shape
    share = keep_ref.shape[1]
    me = lax.axis_index("row")
    core = me % 2

    def pick(member, q):
        block = jnp.broadcast_to(rows_ref[member : member + 1, q : q + 1], (2 * chip_share, row_dev))
        picked = jnp.zeros(block.shape, F32)
        for slot, piece in enumerate(reversed(pieces)):
            here = block == (me // 2) ^ chip_step(slot, core)
            picked = jnp.where(here, piece[member].reshape(block.shape), picked)
        return jnp.concatenate(split(picked), axis=0)

    for member in range(leaves):
        cols = slice(member * B, (member + 1) * B)
        left = jnp.concatenate([pick(member, q) for q in range(slots)], axis=1)
        both = left[: 2 * chip_share]

        def panel(ref, part):
            starts = [pl.multiple_of(q * B + core * row_dev, row_dev) for q in range(slots)]
            return jnp.concatenate(
                [ref[part, pl.ds(start, row_dev), cols] for start in starts], axis=0
            )

        with_real = dot(left, panel(high_ref, 0))
        with_imag = dot(left, panel(high_ref, 1))
        with_real = with_real[: 2 * chip_share] + with_real[2 * chip_share :]
        with_imag = with_imag[: 2 * chip_share] + with_imag[2 * chip_share :]
        with_real += dot(both, panel(low_ref, 0))
        with_imag += dot(both, panel(low_ref, 1))
        whole[0, :, cols] = with_real[:chip_share] - with_imag[chip_share:]
        whole[1, :, cols] = with_imag[:chip_share] + with_real[chip_share:]
    mine = pl.ds(pl.multiple_of(core * share, share), share)
    other = pl.ds(pl.multiple_of((1 - core) * share, share), share)
    keep_ref[...] = diag_ref[...] - whole[:, mine, :]
    give_ref[...] = whole[:, other, :]


def on_device(n_row, n_col, top_inverse, panel, leaf_rows, leaf_counts, diag_inverse):
    vmem = pl.BlockSpec(memory_space=pltpu.VMEM)
    hbm = pl.BlockSpec(memory_space=pl.ANY)
    _, row_dev, _ = top_inverse.shape
    _, panel_rows, columns = panel.shape
    leaves = columns // B
    chips = n_row // 2
    chip_share = B // chips
    depth = n_row * panel_rows
    params = pltpu.CompilerParams(vmem_limit_bytes=max(16 << 20, 40 * depth * columns))

    def cut(block):
        sizes = 3 * row_dev // 8, row_dev - 3 * row_dev // 8
        return pl.pallas_call(
            cut_kernel,
            out_shape=[jax.ShapeDtypeStruct((2, size, B), F32) for size in sizes],
            in_specs=[vmem],
            out_specs=[vmem] * 2,
            compiler_params=params,
            name="cut_rows",
        )(block)

    blocks, halves = line_gather(top_inverse, "col", n_col, cut)

    swap = [(i, i ^ 1) for i in range(n_row)]
    like = {
        step: lax.ppermute(panel, "row", [(i, i ^ step) for i in range(n_row)])
        for step in range(2, n_row, 2)
    }
    near = [step for step in like if step & -step == step]
    far = [step for step in like if step not in near]
    packed = (2, len(near) * panel_rows, columns)
    leaf_counts = leaf_counts[None, :]
    mine, near_high, near_low, leaf_rows, leaf_counts = pl.pallas_call(
        pack_kernel,
        out_shape=[jax.ShapeDtypeStruct(packed, dtype) for dtype in (F32, BF16, BF16)]
        + [jax.ShapeDtypeStruct(value.shape, value.dtype) for value in (leaf_rows, leaf_counts)],
        in_specs=[vmem] * (2 + len(near)),
        out_specs=[vmem] * 5,
        compiler_params=params,
        name="pack_panel",
    )(leaf_rows, leaf_counts, *[like[step] for step in near])
    late_panel, _ = lax.optimization_barrier((panel, [like[step] for step in near]))
    mate = lax.ppermute(late_panel, "row", swap)
    near_mates = lax.ppermute(mine, "row", swap)
    far_panels = []
    for step in far:
        far_panels += [like[step], lax.ppermute(like[step], "row", swap)]

    early_blocks = [blocks[k] for k in range(0, n_col, 2)] + [blocks[1]]
    firsts = [halves[k][0] for k in range(3, n_col, 2)]
    early_blocks, firsts = lax.optimization_barrier((early_blocks, firsts))
    late_blocks = [half for k in range(3, n_col, 2) for half in halves[k]]

    def split_blocks(values):
        count = sum(value.shape[1] for value in values) // row_dev
        return pl.pallas_call(
            blocks_kernel,
            out_shape=jax.ShapeDtypeStruct((count, 4 * row_dev, B), BF16),
            in_specs=[vmem] * len(values),
            out_specs=vmem,
            compiler_params=params,
            cost_estimate=pl.CostEstimate(
                flops=10**11, bytes_accessed=10**9, transcendentals=0
            ),
            name="split_blocks",
        )(*values)

    indices = [
        pltpu.SMEM(leaf_rows.shape, leaf_rows.dtype),
        pltpu.SMEM(leaf_counts.shape, leaf_counts.dtype),
        pltpu.SemaphoreType.DMA((2,)),
    ]
    rows_shape = jax.ShapeDtypeStruct((2, row_dev, columns), F32)
    piece = jax.ShapeDtypeStruct((leaves, 2, chip_share, row_dev), F32)
    scratch = [pltpu.VMEM((chips,) + piece.shape[1:], F32)] + indices
    high, low, late, *early = pl.pallas_call(
        functools.partial(early_kernel, n_col, panel_rows, near, far),
        out_shape=[jax.ShapeDtypeStruct((2, depth, columns), BF16)] * 2
        + [jax.ShapeDtypeStruct(leaf_rows.shape, jnp.int32), rows_shape]
        + [piece] * chips,
        in_specs=[hbm, hbm] + [vmem] * (6 + len(far_panels)),
        out_specs=[vmem] * (4 + chips),
        scratch_shapes=scratch,
        compiler_params=params,
        name="early_rows",
    )(
        leaf_rows,
        leaf_counts,
        split_blocks(early_blocks),
        panel,
        mate,
        near_high,
        near_low,
        near_mates,
        *far_panels,
    )
    early, late_blocks = lax.optimization_barrier((early, late_blocks))

    selected, *sent = pl.pallas_call(
        functools.partial(select_kernel, chips),
        out_shape=[rows_shape] + [piece] * chips,
        in_specs=[vmem] * (5 + chips),
        out_specs=[vmem] * (1 + chips),
        scratch_shapes=scratch[:1],
        compiler_params=params,
        name="selected_rows",
    )(late, split_blocks(late_blocks), high, low, *early)

    for slot in range(chips - 1, 0, -1):
        perm = [(i, i ^ (2 * chip_step(slot, i % 2))) for i in range(n_row)]
        sent[slot] = lax.ppermute(sent[slot], "row", perm)
    selected = pl.pallas_call(
        write_kernel,
        out_shape=jax.ShapeDtypeStruct(selected.shape, F32),
        in_specs=[vmem],
        out_specs=vmem,
        compiler_params=params,
        name="write_rows",
    )(selected)
    selected, sent = lax.optimization_barrier((selected, sent[::-1]))

    keep, give = pl.pallas_call(
        diagonal_kernel,
        out_shape=[jax.ShapeDtypeStruct(diag_inverse.shape, F32)] * 2,
        in_specs=[vmem] * (chips + 4),
        out_specs=[vmem] * 2,
        scratch_shapes=[pltpu.VMEM((2, chip_share, columns), F32)],
        compiler_params=params,
        cost_estimate=pl.CostEstimate(
            flops=12 * chip_share * depth * columns,
            bytes_accessed=8 * (depth + 2 * chip_share) * columns,
            transcendentals=0,
        ),
        name="diagonal_part",
    )(leaf_rows, *sent, high, low, diag_inverse)
    give = lax.ppermute(give, "row", [(i, i ^ 1) for i in range(n_row)])
    diagonal = keep - give
    return selected, diagonal


def solution(mesh):
    return jax.shard_map(
        functools.partial(on_device, mesh.shape["row"], mesh.shape["col"]),
        mesh=mesh,
        in_specs=(
            P(None, "row", "col"),
            P(None, "row", "col"),
            P("col", None),
            P("col"),
            P(None, "row", "col"),
        ),
        out_specs=(P(None, "row", "col"), P(None, "row", "col")),
        check_vma=False,
    )
```

```python
import functools

import jax
import jax.numpy as jnp
from jax import lax
from jax.experimental import pallas as pl
from jax.experimental.pallas import tpu as pltpu
from jax.sharding import PartitionSpec as P

B = 256
F32 = jnp.float32
BF16 = jnp.bfloat16


def split(value):
    high = value.astype(BF16)
    low = (value - high.astype(F32)).astype(BF16)
    return high, low


def dot(left, right):
    return jnp.dot(left, right, preferred_element_type=F32)


def line_gather(own, axis, n, cut):
    blocks = {0: own}
    for step in line_steps(n):
        perm = [(i, i ^ step) for i in range(n)]
        if step > 1:
            blocks |= {k ^ step: lax.ppermute(block, axis, perm) for k, block in blocks.items()}
    halves = {k ^ 1: cut(block) for k, block in blocks.items() if k > 0}
    halves = {k: [lax.ppermute(half, axis, perm) for half in pair] for k, pair in halves.items()}
    blocks[1] = lax.ppermute(own, axis, perm)
    return blocks, halves


def line_steps(n):
    steps = []
    while n > 1:
        n //= 2
        steps.append(n)
    return steps


def cut_kernel(block_ref, first_ref, second_ref):
    size = first_ref.shape[1]
    first_ref[...] = block_ref[:, :size, :]
    second_ref[...] = block_ref[:, size:, :]


def pack_kernel(*refs):
    (rows_ref, counts_ref), pieces = refs[:2], refs[2:-5]
    out_ref, high_ref, low_ref, rows_out, counts_out = refs[-5:]
    rows_out[...] = rows_ref[...]
    counts_out[...] = counts_ref[...]
    share_rows = pieces[0].shape[1]
    for place, piece in enumerate(pieces):
        here = slice(place * share_rows, (place + 1) * share_rows)
        out_ref[:, here, :] = piece[...]
        for part in range(2):
            high_ref[part, here, :], low_ref[part, here, :] = split(piece[part])


def add_slot(total, left, high_ref, low_ref, rows, cols):
    real, imag = total
    size = real.shape[0]
    both = left[0 : 2 * size]
    left = jnp.concatenate([both, left[2 * size : 4 * size], both], axis=1)

    def panel(part):
        high, low = high_ref[part, rows, cols], low_ref[part, rows, cols]
        return jnp.concatenate([high, high, low], axis=0)

    with_real, with_imag = dot(left, panel(0)), dot(left, panel(1))
    real = real - (with_real[:size] - with_imag[size:])
    imag = imag - (with_imag[:size] + with_real[size:])
    return real, imag


def row_is_live(rows_ref, counts_ref, member, block):
    return lax.fori_loop(
        0,
        counts_ref[0, member],
        lambda q, seen: seen | (rows_ref[member, q] == block),
        False,
    )


def blocks_kernel(*refs):
    pieces, out_ref = refs[:-1], refs[-1]
    rows = out_ref.shape[1] // 4
    first = 0
    for piece in pieces:
        size = piece.shape[1]
        for part in range(2):
            for scale, value in enumerate(split(piece[part])):
                start = (2 * scale + part) * rows + first % rows
                out_ref[first // rows, start : start + size, :] = value
        first += size


def add_product(member, q, top, place, high_ref, low_ref, out_ref):
    cols = slice(member * B, (member + 1) * B)
    rows = pl.ds(pl.multiple_of(q * B, B), B)
    total = out_ref[0, :, cols], out_ref[1, :, cols]
    total = add_slot(total, top[place], high_ref, low_ref, rows, cols)
    out_ref[0, :, cols], out_ref[1, :, cols] = total


def early_place(n_col, distance):
    return (distance % 2 == 0) | (distance == 1), jnp.where(distance == 1, n_col // 2, distance // 2)


def late_place(distance):
    return (distance - 3) // 2


def fetch(sems, *pairs):
    copies = [pltpu.make_async_copy(*pair, sems.at[k]) for k, pair in enumerate(pairs)]
    for copy in copies:
        copy.start()
    return copies


def turn(member, out_ref, sent, turned):
    chips, _, share, row_dev = turned.shape
    cols = slice(member * B, (member + 1) * B)
    for part in range(2):
        turned[:, part] = out_ref[part, :, cols].T.reshape(chips, share, row_dev)
    for step in range(chips):
        sent[step][member] = turned[(lax.axis_index("row") // 2) ^ step]


def early_kernel(n_col, share_rows, near, far, *refs):
    rows_hbm, counts_hbm, top, own, mate, near_high, near_low, near_mates = refs[:8]
    far_panels, refs = refs[8 : 8 + 2 * len(far)], refs[8 + 2 * len(far) :]
    high_ref, low_ref, late_ref, out_ref = refs[:4]
    sent, (turned, rows_ref, counts_ref, sems) = refs[4:-4], refs[-4:]
    leaves, slots = rows_ref.shape
    me = lax.axis_index("row")
    my_block = (me * out_ref.shape[1]) // B
    my_col = lax.axis_index("col")
    arrivals = fetch(sems, (rows_hbm, rows_ref), (counts_hbm, counts_ref))

    def put(owner, high, low):
        rows = pl.ds(pl.multiple_of(owner * share_rows, share_rows), share_rows)
        high_ref[:, rows, :], low_ref[:, rows, :] = high, low

    put(me, *split(own[...]))
    put(me ^ 1, *split(mate[...]))
    for place, step in enumerate(near):
        here = slice(place * share_rows, (place + 1) * share_rows)
        put(me ^ step, near_high[:, here, :], near_low[:, here, :])
        put(me ^ step ^ 1, *split(near_mates[:, here, :]))
    for place, step in enumerate(far):
        put(me ^ step, *split(far_panels[2 * place][...]))
        put(me ^ step ^ 1, *split(far_panels[2 * place + 1][...]))
    out_ref[...] = jnp.zeros(out_ref.shape, F32)
    for copy in arrivals:
        copy.wait()
    here = [lax.broadcasted_iota(jnp.int32, (leaves, slots), axis) for axis in range(2)]
    late_ref[...] = jnp.zeros((leaves, slots), jnp.int32)
    for member in range(leaves):

        def slot(q, carry):
            distance = my_col ^ rows_ref[member, q]
            held, place = early_place(n_col, distance)

            @pl.when(held)
            def _():
                add_product(member, q, top, place, high_ref, low_ref, out_ref)

            @pl.when(jnp.logical_not(held))
            def _():
                mark = (here[0] == member) & (here[1] == q)
                late_ref[...] = jnp.where(mark, 1 + late_place(distance), late_ref[...])

            return carry

        live = row_is_live(rows_ref, counts_ref, member, my_block)
        lax.fori_loop(0, jnp.where(live, counts_ref[0, member], 0), slot, 0)
        turn(member, out_ref, sent, turned)


def select_kernel(chips, late_ref, top, high_ref, low_ref, early_ref, *refs):
    early_sent, out_ref, sent, turned = refs[:chips], refs[chips], refs[chips + 1 : -1], refs[-1]
    leaves, slots = late_ref.shape

    def last_marked(member, below):
        marks = late_ref[member : member + 1, :]
        lane = lax.broadcasted_iota(jnp.int32, marks.shape, 1)
        return jnp.max(jnp.where((marks > 0) & (lane < below), lane * 256 + marks, -1))

    found = [last_marked(member, slots) for member in range(leaves)]
    out_ref[...] = early_ref[...]
    for step in range(chips):
        sent[step][...] = early_sent[step][...]
    for member in range(leaves):

        def slot(_, code):
            @pl.when(code >= 0)
            def _():
                add_product(member, code >> 8, top, (code & 255) - 1, high_ref, low_ref, out_ref)

            return last_marked(member, code >> 8)

        @pl.when(found[member] >= 0)
        def _():
            if top.shape[0] == 1:
                add_product(member, found[member] >> 8, top, 0, high_ref, low_ref, out_ref)
            else:
                lax.fori_loop(0, top.shape[0], slot, found[member])
            turn(member, out_ref, sent, turned)


def write_kernel(value_ref, out_ref):
    out_ref[...] = value_ref[...]


def diagonal_kernel(rows_ref, *refs):
    pieces, (high_ref, low_ref, diag_ref, keep_ref, give_ref, whole) = refs[:-6], refs[-6:]
    leaves, slots = rows_ref.shape
    _, _, chip_share, row_dev = pieces[0].shape
    share = keep_ref.shape[1]
    me = lax.axis_index("row")
    core = me % 2

    def pick(member, q):
        block = jnp.broadcast_to(rows_ref[member : member + 1, q : q + 1], (2 * chip_share, row_dev))
        picked = jnp.zeros(block.shape, F32)
        for step, piece in enumerate(reversed(pieces)):
            here = block == (me // 2) ^ step
            picked = jnp.where(here, piece[member].reshape(block.shape), picked)
        return jnp.concatenate(split(picked), axis=0)

    for member in range(leaves):
        cols = slice(member * B, (member + 1) * B)
        left = jnp.concatenate([pick(member, q) for q in range(slots)], axis=1)
        both = left[: 2 * chip_share]

        def panel(ref, part):
            starts = [pl.multiple_of(q * B + core * row_dev, row_dev) for q in range(slots)]
            return jnp.concatenate(
                [ref[part, pl.ds(start, row_dev), cols] for start in starts], axis=0
            )

        with_real = dot(left, panel(high_ref, 0))
        with_imag = dot(left, panel(high_ref, 1))
        with_real = with_real[: 2 * chip_share] + with_real[2 * chip_share :]
        with_imag = with_imag[: 2 * chip_share] + with_imag[2 * chip_share :]
        with_real += dot(both, panel(low_ref, 0))
        with_imag += dot(both, panel(low_ref, 1))
        whole[0, :, cols] = with_real[:chip_share] - with_imag[chip_share:]
        whole[1, :, cols] = with_imag[:chip_share] + with_real[chip_share:]
    mine = pl.ds(pl.multiple_of(core * share, share), share)
    other = pl.ds(pl.multiple_of((1 - core) * share, share), share)
    keep_ref[...] = diag_ref[...] - whole[:, mine, :]
    give_ref[...] = whole[:, other, :]


def on_device(n_row, n_col, top_inverse, panel, leaf_rows, leaf_counts, diag_inverse):
    vmem = pl.BlockSpec(memory_space=pltpu.VMEM)
    hbm = pl.BlockSpec(memory_space=pl.ANY)
    _, row_dev, _ = top_inverse.shape
    _, panel_rows, columns = panel.shape
    leaves = columns // B
    chips = n_row // 2
    chip_share = B // chips
    depth = n_row * panel_rows
    params = pltpu.CompilerParams(vmem_limit_bytes=max(16 << 20, 40 * depth * columns))

    def cut(block):
        sizes = 3 * row_dev // 8, row_dev - 3 * row_dev // 8
        return pl.pallas_call(
            cut_kernel,
            out_shape=[jax.ShapeDtypeStruct((2, size, B), F32) for size in sizes],
            in_specs=[vmem],
            out_specs=[vmem] * 2,
            compiler_params=params,
            name="cut_rows",
        )(block)

    blocks, halves = line_gather(top_inverse, "col", n_col, cut)

    swap = [(i, i ^ 1) for i in range(n_row)]
    like = {
        step: lax.ppermute(panel, "row", [(i, i ^ step) for i in range(n_row)])
        for step in range(2, n_row, 2)
    }
    near = [step for step in like if step & -step == step]
    far = [step for step in like if step not in near]
    packed = (2, len(near) * panel_rows, columns)
    leaf_counts = leaf_counts[None, :]
    mine, near_high, near_low, leaf_rows, leaf_counts = pl.pallas_call(
        pack_kernel,
        out_shape=[jax.ShapeDtypeStruct(packed, dtype) for dtype in (F32, BF16, BF16)]
        + [jax.ShapeDtypeStruct(value.shape, value.dtype) for value in (leaf_rows, leaf_counts)],
        in_specs=[vmem] * (2 + len(near)),
        out_specs=[vmem] * 5,
        compiler_params=params,
        name="pack_panel",
    )(leaf_rows, leaf_counts, *[like[step] for step in near])
    late_panel, _ = lax.optimization_barrier((panel, [like[step] for step in near]))
    mate = lax.ppermute(late_panel, "row", swap)
    near_mates = lax.ppermute(mine, "row", swap)
    far_panels = []
    for step in far:
        far_panels += [like[step], lax.ppermute(like[step], "row", swap)]

    early_blocks = [blocks[k] for k in range(0, n_col, 2)] + [blocks[1]]
    firsts = [halves[k][0] for k in range(3, n_col, 2)]
    early_blocks, firsts = lax.optimization_barrier((early_blocks, firsts))
    late_blocks = [half for k in range(3, n_col, 2) for half in halves[k]]

    def split_blocks(values):
        count = sum(value.shape[1] for value in values) // row_dev
        return pl.pallas_call(
            blocks_kernel,
            out_shape=jax.ShapeDtypeStruct((count, 4 * row_dev, B), BF16),
            in_specs=[vmem] * len(values),
            out_specs=vmem,
            compiler_params=params,
            cost_estimate=pl.CostEstimate(
                flops=10**11, bytes_accessed=10**9, transcendentals=0
            ),
            name="split_blocks",
        )(*values)

    indices = [
        pltpu.SMEM(leaf_rows.shape, leaf_rows.dtype),
        pltpu.SMEM(leaf_counts.shape, leaf_counts.dtype),
        pltpu.SemaphoreType.DMA((2,)),
    ]
    rows_shape = jax.ShapeDtypeStruct((2, row_dev, columns), F32)
    piece = jax.ShapeDtypeStruct((leaves, 2, chip_share, row_dev), F32)
    scratch = [pltpu.VMEM((chips,) + piece.shape[1:], F32)] + indices
    high, low, late, *early = pl.pallas_call(
        functools.partial(early_kernel, n_col, panel_rows, near, far),
        out_shape=[jax.ShapeDtypeStruct((2, depth, columns), BF16)] * 2
        + [jax.ShapeDtypeStruct(leaf_rows.shape, jnp.int32), rows_shape]
        + [piece] * chips,
        in_specs=[hbm, hbm] + [vmem] * (6 + len(far_panels)),
        out_specs=[vmem] * (4 + chips),
        scratch_shapes=scratch,
        compiler_params=params,
        name="early_rows",
    )(
        leaf_rows,
        leaf_counts,
        split_blocks(early_blocks),
        panel,
        mate,
        near_high,
        near_low,
        near_mates,
        *far_panels,
    )
    early, late_blocks = lax.optimization_barrier((early, late_blocks))

    selected, *sent = pl.pallas_call(
        functools.partial(select_kernel, chips),
        out_shape=[rows_shape] + [piece] * chips,
        in_specs=[vmem] * (5 + chips),
        out_specs=[vmem] * (1 + chips),
        scratch_shapes=scratch[:1],
        compiler_params=params,
        name="selected_rows",
    )(late, split_blocks(late_blocks), high, low, *early)

    for step in range(chips - 1, 0, -1):
        perm = [(i, i ^ (2 * step)) for i in range(n_row)]
        sent[step] = lax.ppermute(sent[step], "row", perm)
    selected = pl.pallas_call(
        write_kernel,
        out_shape=jax.ShapeDtypeStruct(selected.shape, F32),
        in_specs=[vmem],
        out_specs=vmem,
        compiler_params=params,
        name="write_rows",
    )(selected)
    selected, sent = lax.optimization_barrier((selected, sent))

    keep, give = pl.pallas_call(
        diagonal_kernel,
        out_shape=[jax.ShapeDtypeStruct(diag_inverse.shape, F32)] * 2,
        in_specs=[vmem] * (chips + 4),
        out_specs=[vmem] * 2,
        scratch_shapes=[pltpu.VMEM((2, chip_share, columns), F32)],
        compiler_params=params,
        cost_estimate=pl.CostEstimate(
            flops=12 * chip_share * depth * columns,
            bytes_accessed=8 * (depth + 2 * chip_share) * columns,
            transcendentals=0,
        ),
        name="diagonal_part",
    )(leaf_rows, *sent[::-1], high, low, diag_inverse)
    give = lax.ppermute(give, "row", [(i, i ^ 1) for i in range(n_row)])
    diagonal = keep - give
    return selected, diagonal


def solution(mesh):
    return jax.shard_map(
        functools.partial(on_device, mesh.shape["row"], mesh.shape["col"]),
        mesh=mesh,
        in_specs=(
            P(None, "row", "col"),
            P(None, "row", "col"),
            P("col", None),
            P("col"),
            P(None, "row", "col"),
        ),
        out_specs=(P(None, "row", "col"), P(None, "row", "col")),
        check_vma=False,
    )
```

```python
import functools

import jax
import jax.numpy as jnp
from jax import lax
from jax.experimental import pallas as pl
from jax.experimental.pallas import tpu as pltpu
from jax.sharding import PartitionSpec as P

B = 256
F32 = jnp.float32
BF16 = jnp.bfloat16


def split(value):
    high = value.astype(BF16)
    low = (value - high.astype(F32)).astype(BF16)
    return high, low


def dot(left, right):
    return jnp.dot(left, right, preferred_element_type=F32)


def line_gather(own, axis, n, cut):
    blocks = {0: own}
    for step in line_steps(n):
        perm = [(i, i ^ step) for i in range(n)]
        if step > 1:
            blocks |= {k ^ step: lax.ppermute(block, axis, perm) for k, block in blocks.items()}
    halves = {k ^ 1: cut(block) for k, block in blocks.items() if k > 0}
    halves = {k: [lax.ppermute(half, axis, perm) for half in pair] for k, pair in halves.items()}
    blocks[1] = lax.ppermute(own, axis, perm)
    return blocks, halves


def line_steps(n):
    steps = []
    while n > 1:
        n //= 2
        steps.append(n)
    return steps


def cut_kernel(block_ref, first_ref, second_ref):
    size = first_ref.shape[1]
    first_ref[...] = block_ref[:, :size, :]
    second_ref[...] = block_ref[:, size:, :]


def pack_kernel(*refs):
    (rows_ref, counts_ref), pieces = refs[:2], refs[2:-5]
    out_ref, high_ref, low_ref, rows_out, counts_out = refs[-5:]
    rows_out[...] = rows_ref[...]
    counts_out[...] = counts_ref[...]
    share_rows = pieces[0].shape[1]
    for place, piece in enumerate(pieces):
        here = slice(place * share_rows, (place + 1) * share_rows)
        out_ref[:, here, :] = piece[...]
        for part in range(2):
            high_ref[part, here, :], low_ref[part, here, :] = split(piece[part])


def add_slot(total, left, high_ref, low_ref, rows, cols):
    real, imag = total
    size = real.shape[0]
    both = left[0 : 2 * size]
    left = jnp.concatenate([both, left[2 * size : 4 * size], both], axis=1)

    def panel(part):
        high, low = high_ref[part, rows, cols], low_ref[part, rows, cols]
        return jnp.concatenate([high, high, low], axis=0)

    with_real, with_imag = dot(left, panel(0)), dot(left, panel(1))
    real = real - (with_real[:size] - with_imag[size:])
    imag = imag - (with_imag[:size] + with_real[size:])
    return real, imag


def row_is_live(rows_ref, counts_ref, member, block):
    return lax.fori_loop(
        0,
        counts_ref[0, member],
        lambda q, seen: seen | (rows_ref[member, q] == block),
        False,
    )


def blocks_kernel(*refs):
    pieces, out_ref = refs[:-1], refs[-1]
    rows = out_ref.shape[1] // 4
    first = 0
    for piece in pieces:
        size = piece.shape[1]
        for part in range(2):
            for scale, value in enumerate(split(piece[part])):
                start = (2 * scale + part) * rows + first % rows
                out_ref[first // rows, start : start + size, :] = value
        first += size


def add_product(member, q, top, place, high_ref, low_ref, out_ref):
    cols = slice(member * B, (member + 1) * B)
    rows = pl.ds(pl.multiple_of(q * B, B), B)
    total = out_ref[0, :, cols], out_ref[1, :, cols]
    total = add_slot(total, top[place], high_ref, low_ref, rows, cols)
    out_ref[0, :, cols], out_ref[1, :, cols] = total


def early_place(n_col, distance):
    return (distance % 2 == 0) | (distance == 1), jnp.where(distance == 1, n_col // 2, distance // 2)


def late_place(distance):
    return (distance - 3) // 2


def fetch(sems, *pairs):
    copies = [pltpu.make_async_copy(*pair, sems.at[k]) for k, pair in enumerate(pairs)]
    for copy in copies:
        copy.start()
    return copies


def turn(member, out_ref, sent, turned):
    chips, _, share, row_dev = turned.shape
    cols = slice(member * B, (member + 1) * B)
    for part in range(2):
        turned[:, part] = out_ref[part, :, cols].T.reshape(chips, share, row_dev)
    for step in range(chips):
        sent[step][member] = turned[(lax.axis_index("row") // 2) ^ step]


def early_kernel(n_col, share_rows, near, far, *refs):
    rows_hbm, counts_hbm, top, own, mate, near_high, near_low, near_mates = refs[:8]
    far_panels, refs = refs[8 : 8 + 2 * len(far)], refs[8 + 2 * len(far) :]
    high_ref, low_ref, late_ref, out_ref = refs[:4]
    sent, (turned, rows_ref, counts_ref, sems) = refs[4:-4], refs[-4:]
    leaves, slots = rows_ref.shape
    me = lax.axis_index("row")
    my_block = (me * out_ref.shape[1]) // B
    my_col = lax.axis_index("col")
    arrivals = fetch(sems, (rows_hbm, rows_ref), (counts_hbm, counts_ref))

    def put(owner, high, low):
        rows = pl.ds(pl.multiple_of(owner * share_rows, share_rows), share_rows)
        high_ref[:, rows, :], low_ref[:, rows, :] = high, low

    put(me, *split(own[...]))
    put(me ^ 1, *split(mate[...]))
    for place, step in enumerate(near):
        here = slice(place * share_rows, (place + 1) * share_rows)
        put(me ^ step, near_high[:, here, :], near_low[:, here, :])
        put(me ^ step ^ 1, *split(near_mates[:, here, :]))
    for place, step in enumerate(far):
        put(me ^ step, *split(far_panels[2 * place][...]))
        put(me ^ step ^ 1, *split(far_panels[2 * place + 1][...]))
    out_ref[...] = jnp.zeros(out_ref.shape, F32)
    for copy in arrivals:
        copy.wait()
    here = [lax.broadcasted_iota(jnp.int32, (leaves, slots), axis) for axis in range(2)]
    late_ref[...] = jnp.zeros((leaves, slots), jnp.int32)
    for member in range(leaves):

        def slot(q, carry):
            distance = my_col ^ rows_ref[member, q]
            held, place = early_place(n_col, distance)

            @pl.when(held)
            def _():
                add_product(member, q, top, place, high_ref, low_ref, out_ref)

            @pl.when(jnp.logical_not(held))
            def _():
                mark = (here[0] == member) & (here[1] == q)
                late_ref[...] = jnp.where(mark, 1 + late_place(distance), late_ref[...])

            return carry

        live = row_is_live(rows_ref, counts_ref, member, my_block)
        lax.fori_loop(0, jnp.where(live, counts_ref[0, member], 0), slot, 0)
        turn(member, out_ref, sent, turned)


def select_kernel(chips, late_ref, top, high_ref, low_ref, early_ref, *refs):
    early_sent, out_ref, sent, turned = refs[:chips], refs[chips], refs[chips + 1 : -1], refs[-1]
    leaves, slots = late_ref.shape

    def last_marked(member, below):
        marks = late_ref[member : member + 1, :]
        lane = lax.broadcasted_iota(jnp.int32, marks.shape, 1)
        return jnp.max(jnp.where((marks > 0) & (lane < below), lane * 256 + marks, -1))

    found = [last_marked(member, slots) for member in range(leaves)]
    out_ref[...] = early_ref[...]
    for step in range(chips):
        sent[step][...] = early_sent[step][...]
    for member in range(leaves):

        def slot(_, code):
            @pl.when(code >= 0)
            def _():
                add_product(member, code >> 8, top, (code & 255) - 1, high_ref, low_ref, out_ref)

            return last_marked(member, code >> 8)

        @pl.when(found[member] >= 0)
        def _():
            if top.shape[0] == 1:
                add_product(member, found[member] >> 8, top, 0, high_ref, low_ref, out_ref)
            else:
                lax.fori_loop(0, top.shape[0], slot, found[member])
            turn(member, out_ref, sent, turned)


def write_kernel(value_ref, out_ref):
    out_ref[...] = value_ref[...]


def diagonal_kernel(for_mate, rows_ref, *refs):
    pieces, (high_ref, low_ref, out_ref) = refs[:-3], refs[-3:]
    leaves, slots = rows_ref.shape
    row_dev = pieces[0].shape[3]
    share = out_ref.shape[1]
    me = lax.axis_index("row")
    core = me % 2
    owner = 1 - core if for_mate else core
    mine = pl.ds(pl.multiple_of(owner * share, share), share)

    def pick(member, q):
        block = jnp.broadcast_to(rows_ref[member : member + 1, q : q + 1], (2 * share, row_dev))
        picked = jnp.zeros(block.shape, F32)
        for step, piece in enumerate(reversed(pieces)):
            here = block == (me // 2) ^ step
            picked = jnp.where(here, piece[member, :, mine, :].reshape(block.shape), picked)
        return jnp.concatenate(split(picked), axis=0)

    for member in range(leaves):
        cols = slice(member * B, (member + 1) * B)
        left = jnp.concatenate([pick(member, q) for q in range(slots)], axis=1)
        both = left[: 2 * share]

        def panel(ref, part):
            starts = [pl.multiple_of(q * B + core * row_dev, row_dev) for q in range(slots)]
            return jnp.concatenate(
                [ref[part, pl.ds(start, row_dev), cols] for start in starts], axis=0
            )

        with_real = dot(left, panel(high_ref, 0))
        with_imag = dot(left, panel(high_ref, 1))
        with_real = with_real[: 2 * share] + with_real[2 * share :]
        with_imag = with_imag[: 2 * share] + with_imag[2 * share :]
        with_real += dot(both, panel(low_ref, 0))
        with_imag += dot(both, panel(low_ref, 1))
        out_ref[0, :, cols] = with_real[:share] - with_imag[share:]
        out_ref[1, :, cols] = with_imag[:share] + with_real[share:]


def on_device(n_row, n_col, top_inverse, panel, leaf_rows, leaf_counts, diag_inverse):
    vmem = pl.BlockSpec(memory_space=pltpu.VMEM)
    hbm = pl.BlockSpec(memory_space=pl.ANY)
    _, row_dev, _ = top_inverse.shape
    _, panel_rows, columns = panel.shape
    leaves = columns // B
    chips = n_row // 2
    chip_share = B // chips
    depth = n_row * panel_rows
    params = pltpu.CompilerParams(vmem_limit_bytes=max(16 << 20, 40 * depth * columns))

    def cut(block):
        sizes = 3 * row_dev // 8, row_dev - 3 * row_dev // 8
        return pl.pallas_call(
            cut_kernel,
            out_shape=[jax.ShapeDtypeStruct((2, size, B), F32) for size in sizes],
            in_specs=[vmem],
            out_specs=[vmem] * 2,
            compiler_params=params,
            name="cut_rows",
        )(block)

    blocks, halves = line_gather(top_inverse, "col", n_col, cut)

    swap = [(i, i ^ 1) for i in range(n_row)]
    like = {
        step: lax.ppermute(panel, "row", [(i, i ^ step) for i in range(n_row)])
        for step in range(2, n_row, 2)
    }
    near = [step for step in like if step & -step == step]
    far = [step for step in like if step not in near]
    packed = (2, len(near) * panel_rows, columns)
    leaf_counts = leaf_counts[None, :]
    mine, near_high, near_low, leaf_rows, leaf_counts = pl.pallas_call(
        pack_kernel,
        out_shape=[jax.ShapeDtypeStruct(packed, dtype) for dtype in (F32, BF16, BF16)]
        + [jax.ShapeDtypeStruct(value.shape, value.dtype) for value in (leaf_rows, leaf_counts)],
        in_specs=[vmem] * (2 + len(near)),
        out_specs=[vmem] * 5,
        compiler_params=params,
        name="pack_panel",
    )(leaf_rows, leaf_counts, *[like[step] for step in near])
    late_panel, _ = lax.optimization_barrier((panel, [like[step] for step in near]))
    mate = lax.ppermute(late_panel, "row", swap)
    near_mates = lax.ppermute(mine, "row", swap)
    far_panels = []
    for step in far:
        far_panels += [like[step], lax.ppermute(like[step], "row", swap)]

    early_blocks = [blocks[k] for k in range(0, n_col, 2)] + [blocks[1]]
    firsts = [halves[k][0] for k in range(3, n_col, 2)]
    early_blocks, firsts = lax.optimization_barrier((early_blocks, firsts))
    late_blocks = [half for k in range(3, n_col, 2) for half in halves[k]]

    def split_blocks(values):
        count = sum(value.shape[1] for value in values) // row_dev
        return pl.pallas_call(
            blocks_kernel,
            out_shape=jax.ShapeDtypeStruct((count, 4 * row_dev, B), BF16),
            in_specs=[vmem] * len(values),
            out_specs=vmem,
            compiler_params=params,
            cost_estimate=pl.CostEstimate(
                flops=10**11, bytes_accessed=10**9, transcendentals=0
            ),
            name="split_blocks",
        )(*values)

    indices = [
        pltpu.SMEM(leaf_rows.shape, leaf_rows.dtype),
        pltpu.SMEM(leaf_counts.shape, leaf_counts.dtype),
        pltpu.SemaphoreType.DMA((2,)),
    ]
    rows_shape = jax.ShapeDtypeStruct((2, row_dev, columns), F32)
    piece = jax.ShapeDtypeStruct((leaves, 2, chip_share, row_dev), F32)
    scratch = [pltpu.VMEM((chips,) + piece.shape[1:], F32)] + indices
    high, low, late, *early = pl.pallas_call(
        functools.partial(early_kernel, n_col, panel_rows, near, far),
        out_shape=[jax.ShapeDtypeStruct((2, depth, columns), BF16)] * 2
        + [jax.ShapeDtypeStruct(leaf_rows.shape, jnp.int32), rows_shape]
        + [piece] * chips,
        in_specs=[hbm, hbm] + [vmem] * (6 + len(far_panels)),
        out_specs=[vmem] * (4 + chips),
        scratch_shapes=scratch,
        compiler_params=params,
        name="early_rows",
    )(
        leaf_rows,
        leaf_counts,
        split_blocks(early_blocks),
        panel,
        mate,
        near_high,
        near_low,
        near_mates,
        *far_panels,
    )
    early, late_blocks = lax.optimization_barrier((early, late_blocks))

    selected, *sent = pl.pallas_call(
        functools.partial(select_kernel, chips),
        out_shape=[rows_shape] + [piece] * chips,
        in_specs=[vmem] * (5 + chips),
        out_specs=[vmem] * (1 + chips),
        scratch_shapes=scratch[:1],
        compiler_params=params,
        name="selected_rows",
    )(late, split_blocks(late_blocks), high, low, *early)

    for step in range(chips - 1, 0, -1):
        perm = [(i, i ^ (2 * step)) for i in range(n_row)]
        sent[step] = lax.ppermute(sent[step], "row", perm)
    selected = pl.pallas_call(
        write_kernel,
        out_shape=jax.ShapeDtypeStruct(selected.shape, F32),
        in_specs=[vmem],
        out_specs=vmem,
        compiler_params=params,
        name="write_rows",
    )(selected)
    selected, sent = lax.optimization_barrier((selected, sent[::-1]))

    def diagonal_part(for_mate):
        return pl.pallas_call(
            functools.partial(diagonal_kernel, for_mate),
            out_shape=jax.ShapeDtypeStruct(diag_inverse.shape, F32),
            in_specs=[vmem] * (chips + 3),
            out_specs=vmem,
            compiler_params=params,
            name="diagonal_part",
        )(leaf_rows, *sent, high, low)

    give = lax.ppermute(diagonal_part(True), "row", [(i, i ^ 1) for i in range(n_row)])
    diagonal = diag_inverse - diagonal_part(False) - give
    return selected, diagonal


def solution(mesh):
    return jax.shard_map(
        functools.partial(on_device, mesh.shape["row"], mesh.shape["col"]),
        mesh=mesh,
        in_specs=(
            P(None, "row", "col"),
            P(None, "row", "col"),
            P("col", None),
            P("col"),
            P(None, "row", "col"),
        ),
        out_specs=(P(None, "row", "col"), P(None, "row", "col")),
        check_vma=False,
    )
```
